32 devices in a mesh: gx: 8 (over y, x, core), gy: 4 (over z).
Axes of the slice: x: 2, y: 2, z: 4, core: 2. Of those that a mesh axis runs over, the one named last changes fastest.
Arguments:
- electric: float32 [3, 16, 64, 512], P(None, None, 'gx', 'gy'), may hold values from -6 to 6
- magnetic: float32 [3, 16, 64, 512], P(None, None, 'gx', 'gy'), may hold values from -6 to 6
- material: int32 [16, 64, 512], P(None, 'gx', 'gy'), may hold values from 0 to 3
- permittivity: float32 [4], replicated, may hold values from 1 to 12
- slab_spectra: float32 [2, 128, 64, 512], P(None, None, 'gx', 'gy'), may hold values from -6 to 6
- monitor_spectra: float32 [16, 2, 4, 64, 512], P(None, None, None, 'gx', 'gy'), may hold values from -6 to 6
- wave_index: int32 [16], replicated, may hold values from 0 to 63
Outputs:
- electric_next: float32 [3, 16, 64, 512], P(None, None, 'gx', 'gy')
- magnetic_next: float32 [3, 16, 64, 512], P(None, None, 'gx', 'gy')
- slab_next: float32 [2, 128, 64, 512], P(None, None, 'gx', 'gy')
- monitor_next: float32 [16, 2, 4, 64, 512], P(None, None, None, 'gx', 'gy')
- orders: float32 [16, 2, 4, 128, 64], P('gy', None, None, 'gx')
The draws below stay inside these ranges and needn't reach their ends.
All inputs are finite; a program needn't handle non-finite values.
Results may differ from the reference program's by a relative error of at most 0.00007.
Values sent between devices are 32-bit elements; how exact they have to be, the bound alone decides.
No kernel may reach another device: no remote copies, remote signals or barrier semaphores. Data moves between devices by JAX's collectives and lax.ppermute only.
A program may use at most 64 MiB of HBM per device.

```python
import math
import jax
import jax.numpy as jnp
from jax import lax

NF = 64
NW = 16
OY = 128
OX = 64
CLASSES = 4
NX = 64
NY = 512
NZ = 16


def with_ends(entries, rng, smallest, top_value):
    longest = entries.shape.index(max(entries.shape))
    spots = []
    for shift in (0, 1):
        where = [jax.random.randint(jax.random.fold_in(rng, axis), (), 0, length) for axis, length in enumerate(entries.shape)]
        where[longest] = (where[longest] + shift) % entries.shape[longest]
        spots.append(tuple(where))
    return entries.at[spots[0]].set(smallest).at[spots[1]].set(top_value)


def raised(result, stream_key, source, target, parts, factor):
    owner, partner = [(jnp.arange(result.shape[axis_at]) // (result.shape[axis_at] // parts)).reshape([-1 if axis == axis_at else 1 for axis in range(result.ndim)]) for axis_at in (source, target)]
    chosen = jax.random.permutation(stream_key, parts)[partner]
    strong = (owner == chosen) | (owner == (partner + parts // 2) % parts)
    return jnp.where(strong, factor * result, result)


def level_of(own_key, extent, shards, least, largest):
    def one(axis_at, parts):
        steps = jax.random.uniform(jax.random.fold_in(jax.random.fold_in(own_key, 6), axis_at), (parts,), jnp.float32, least / len(shards), largest / len(shards))
        return jnp.repeat(jnp.exp(steps), extent[axis_at] // parts).reshape((-1,) + (1,) * (len(extent) - axis_at - 1))

    factor_of = one(*shards[0])
    for cut in shards[1:]:
        factor_of = factor_of * one(*cut)
    return factor_of


def scatter_about(stream_key, extent, width, most, pieces=(), held_as=jnp.bfloat16):
    values = width * jax.random.normal(stream_key, extent, jnp.float32)
    if pieces:
        values = values * level_of(stream_key, extent, pieces, -0.22, 0.18)
    return jnp.clip(values, -most, most).astype(held_as)


def heavy_noise(key, dims, spread, most, shards, heavy, kind=jnp.bfloat16):
    result = spread * jax.random.normal(key, dims, jnp.float32)
    if shards:
        result = result * level_of(key, dims, shards, -0.22, 0.18)
    return jnp.clip(raised(result, jax.random.fold_in(key, 3), *heavy), -most, most).astype(kind)


def setup_inputs(seed: int = 0) -> dict:
    seeds = jax.random.split(jax.random.key(seed), 8)
    electric = scatter_about(seeds[0], (3, NZ, NX, NY), 1.0, 6.0, ((2, 8), (3, 4)), jnp.float32)
    magnetic = scatter_about(seeds[1], (3, NZ, NX, NY), 1.0, 6.0, ((2, 8), (3, 4)), jnp.float32)
    material = with_ends(jax.random.randint(seeds[2], (NZ, NX, NY), 0, CLASSES), jax.random.fold_in(seeds[2], 1), 0, CLASSES - 1).astype(jnp.int32)
    permittivity = jnp.clip(jnp.exp(jax.random.uniform(seeds[3], (CLASSES,), jnp.float32, math.log(1.0), math.log(12.0))), 1.0, 12.0)
    slab_spectra = scatter_about(seeds[4], (2, 2 * NF, NX, NY), 1.0, 6.0, ((2, 8), (3, 4)), jnp.float32)
    monitor_spectra = heavy_noise(seeds[5], (NW, 2, 4, NX, NY), 1.0, 6.0, ((3, 8), (4, 4)), (4, 0, 4, 2.0), jnp.float32)
    wave_index = with_ends(jax.random.randint(seeds[6], (NW,), 0, NF), jax.random.fold_in(seeds[6], 1), 0, NF - 1).astype(jnp.int32)
    return {"electric": electric, "magnetic": magnetic, "material": material, "permittivity": permittivity, "slab_spectra": slab_spectra, "monitor_spectra": monitor_spectra, "wave_index": wave_index}


TIME_STEP = 0.5
OMEGA_LOW = 0.15
OMEGA_HIGH = 0.8

def forward_z(values):
    return jnp.concatenate([values[1:], jnp.zeros_like(values[:1])], axis=0) - values

def backward_z(values):
    return values - jnp.concatenate([jnp.zeros_like(values[:1]), values[:-1]], axis=0)

def inverse_map(material, permittivity):
    inverse = jnp.zeros(material.shape, jnp.float32)
    for category in range(permittivity.shape[0]):
        inverse = inverse + jnp.where(material == category, 1.0 / permittivity[category], 0.0)
    return inverse

def all_omegas(freq_count):
    return OMEGA_LOW + (OMEGA_HIGH - OMEGA_LOW) * jnp.arange(freq_count, dtype=jnp.float32) / (freq_count - 1)

def picked_omegas(wave_index, freq_count):
    matches = wave_index[:, None] == jnp.arange(freq_count, dtype=jnp.int32)[None, :]
    return lax.optimization_barrier(jnp.sum(jnp.where(matches, all_omegas(freq_count)[None, :], 0.0), axis=1))

def order_table(length, kept_count, offset, modulus):
    position = jnp.arange(length, dtype=jnp.int32) + offset
    wanted = (jnp.arange(kept_count, dtype=jnp.int32) - kept_count // 2) % modulus
    phases = position[:, None] * wanted[None, :] % modulus
    angles = 2.0 * math.pi / modulus * phases.astype(jnp.float32)
    cosine = jnp.cos(angles)
    sine_part = jnp.sin(angles)
    return jnp.stack([jnp.stack([cosine, -sine_part]), jnp.stack([sine_part, cosine])])

def advance(electric, magnetic, inverse):
    electric_x, electric_y, electric_z = (electric[0], electric[1], electric[2])
    ey_ahead_x = jnp.roll(electric_y, -1, axis=1)
    ez_ahead_x = jnp.roll(electric_z, -1, axis=1)
    ex_ahead_y = jnp.roll(electric_x, -1, axis=2)
    ez_ahead_y = jnp.roll(electric_z, -1, axis=2)
    magnetic_x = magnetic[0] - TIME_STEP * (ez_ahead_y - electric_z - forward_z(electric_y))
    magnetic_y = magnetic[1] - TIME_STEP * (forward_z(electric_x) - (ez_ahead_x - electric_z))
    magnetic_z = magnetic[2] - TIME_STEP * (ey_ahead_x - electric_y - (ex_ahead_y - electric_x))
    hy_behind_x = jnp.roll(magnetic_y, 1, axis=1)
    hz_behind_x = jnp.roll(magnetic_z, 1, axis=1)
    hx_behind_y = jnp.roll(magnetic_x, 1, axis=2)
    hz_behind_y = jnp.roll(magnetic_z, 1, axis=2)
    new_x = electric_x + TIME_STEP * inverse * (magnetic_z - hz_behind_y - backward_z(magnetic_y))
    new_y = electric_y + TIME_STEP * inverse * (backward_z(magnetic_x) - (magnetic_z - hz_behind_x))
    new_z = electric_z + TIME_STEP * inverse * (magnetic_y - hy_behind_x - (magnetic_x - hx_behind_y))
    return (jnp.stack([new_x, new_y, new_z]), jnp.stack([magnetic_x, magnetic_y, magnetic_z]))

def records_of(electric, magnetic):
    middle = electric.shape[1] // 2
    slab_layer = electric[0:2, middle]
    monitor_plane = jnp.concatenate([electric[0:2, -1], magnetic[0:2, -1]], axis=0)
    return (slab_layer, monitor_plane)

def spectra_update(slab_spectra, monitor_spectra, slab_records, monitor_records, wave_index):
    freq_count = slab_spectra.shape[1] // 2
    times = TIME_STEP * (jnp.arange(2, dtype=jnp.float32) + 1.0)
    slab_angles = times[:, None] * all_omegas(freq_count)[None, :]
    slab_table = jnp.concatenate([TIME_STEP * jnp.cos(slab_angles), -TIME_STEP * jnp.sin(slab_angles)], axis=1)
    slab_next = slab_spectra + jnp.einsum('csxy,sf->cfxy', slab_records, slab_table, precision=lax.Precision.HIGHEST)
    half_lag = jnp.array([0.0, 0.0, 0.5, 0.5], jnp.float32) * TIME_STEP
    monitor_times = times[None, :] - half_lag[:, None]
    monitor_angles = monitor_times[:, :, None] * picked_omegas(wave_index, freq_count)[None, None, :]
    real_part = jnp.einsum('csxy,csw->wcxy', monitor_records, TIME_STEP * jnp.cos(monitor_angles), precision=lax.Precision.HIGHEST)
    imag_part = jnp.einsum('csxy,csw->wcxy', monitor_records, -TIME_STEP * jnp.sin(monitor_angles), precision=lax.Precision.HIGHEST)
    monitor_next = monitor_spectra + jnp.stack([real_part, imag_part], axis=1)
    return (slab_next, monitor_next)

def reference(electric, magnetic, material, permittivity, slab_spectra, monitor_spectra, wave_index):
    inverse = inverse_map(material, permittivity)
    slab_list = []
    plane_list = []
    for repeat in range(2):
        electric, magnetic = advance(electric, magnetic, inverse)
        slab_layer, monitor_plane = records_of(electric, magnetic)
        slab_list.append(slab_layer)
        plane_list.append(monitor_plane)
    slab_records = jnp.stack(slab_list, axis=1)
    monitor_records = jnp.stack(plane_list, axis=1)
    slab_next, monitor_next = spectra_update(slab_spectra, monitor_spectra, slab_records, monitor_records, wave_index)
    y_table = order_table(NY, OY, 0, NY)
    spectrum_y = jnp.einsum('wicxy,ioyk->wockx', monitor_next, y_table, precision=lax.Precision.HIGHEST)
    x_table = order_table(NX, OX, 0, NX)
    scaling = 1.0 / math.sqrt(NX * NY)
    orders = jnp.einsum('wicqx,ioxk->wocqk', spectrum_y, x_table, precision=lax.Precision.HIGHEST) * scaling
    return (electric, magnetic, slab_next, monitor_next, orders)
```

```python
import functools
import math

import jax
import jax.numpy as jnp
import numpy as np
from jax import lax
from jax.experimental import pallas as pl
from jax.experimental.pallas import tpu as pltpu
from jax.sharding import PartitionSpec as P

OY = 128
OX = 64

TIME_STEP = 0.5
OMEGA_LOW = 0.15
OMEGA_HIGH = 0.8

STEPS = 2
EDGE = 2 * STEPS
SEAM = 2 * EDGE
DEEP = 4
KINDS = 7
RECORDS = 4

VMEM = pl.BlockSpec(memory_space=pltpu.VMEM)
SMEM = pl.BlockSpec(memory_space=pltpu.SMEM)
PARAMS = pltpu.CompilerParams(vmem_limit_bytes=48 * 1024 * 1024)


def passed_along(block, axis, distance):
    devices = range(lax.axis_size(axis))
    route = [((i - distance) % len(devices), i) for i in devices]
    return lax.ppermute(block, axis, route)


def rolled(values, shift, axis):
    shift %= values.shape[axis]
    return pltpu.roll(values, shift, axis) if shift else values


def iota(shape, axis):
    return lax.broadcasted_iota(jnp.int32, shape, axis)


def rates_of(permittivity, classes, shape):
    return [TIME_STEP / jnp.full(shape, permittivity[k], jnp.float32) for k in range(classes)]


def rate_at(material, rates):
    rate = rates[-1]
    for k in range(len(rates) - 2, -1, -1):
        rate = jnp.where(material == k, rates[k], rate)
    return rate


class Leapfrog:
    def __init__(self, start, layers=None, above=None, below=None):
        self.start = start
        self.layers = layers
        self.above = above
        self.below = below
        self.known = {}

    def first(self, z):
        if ("0", z) not in self.known:
            self.known["0", z] = self.start(z)
        return self.known["0", z]

    def e(self, s, z):
        if s == 0:
            return self.first(z)[0:3]
        if ("e", s, z) not in self.known:
            ex, ey, ez = self.e(s - 1, z)
            hx, hy, hz = self.h(s, z)
            if self.layers is None:
                down_x, down_y = self.below(hx), self.below(hy)
            else:
                down_x, down_y = self.h(s, z - 1)[:2] if z else (0.0, 0.0)
            rate = self.first(z)[6]
            self.known["e", s, z] = (
                ex + rate * ((hz - rolled(hz, 1, 1)) - (hy - down_y)),
                ey + rate * ((hx - down_x) - (hz - rolled(hz, 1, 0))),
                ez + rate * ((hy - rolled(hy, 1, 0)) - (hx - rolled(hx, 1, 1))),
            )
        return self.known["e", s, z]

    def h(self, s, z):
        if s == 0:
            return self.first(z)[3:6]
        if ("h", s, z) not in self.known:
            ex, ey, ez = self.e(s - 1, z)
            hx, hy, hz = self.h(s - 1, z)
            if self.layers is None:
                up_x, up_y = self.above(ex), self.above(ey)
            else:
                up_x, up_y = self.e(s - 1, z + 1)[:2] if z + 1 < self.layers else (0.0, 0.0)
            self.known["h", s, z] = (
                hx - TIME_STEP * ((rolled(ez, -1, 1) - ez) - (up_y - ey)),
                hy - TIME_STEP * ((up_x - ex) - (rolled(ez, -1, 0) - ez)),
                hz - TIME_STEP * ((rolled(ey, -1, 0) - ey) - (rolled(ex, -1, 1) - ex)),
            )
        return self.known["h", s, z]

    def records(self, s, z):
        return self.e(s, z)[:2] + self.h(s, z)[:2]


def seam_leapfrog(tiles, layers):
    layer = iota(tiles[0].shape, 1) // SEAM % layers
    return Leapfrog(
        lambda z: tiles,
        above=lambda f: jnp.where(layer < layers - 1, rolled(f, -SEAM, 1), 0.0),
        below=lambda f: jnp.where(layer > 0, rolled(f, SEAM, 1), 0.0),
    )


def own_planes(e_ref, h_ref, m_ref, rates):
    def at(z):
        rate = rate_at(m_ref[z], rates)
        return [e_ref[c, z] for c in range(3)] + [h_ref[c, z] for c in range(3)] + [rate]

    return at


def widened_planes(own, before_ref, after_ref, first_group=0):
    def at(z):
        planes = own(z)
        rows = planes[0].shape[0]
        group, place = divmod(z, rows // STEPS)
        row = iota(planes[0].shape, 0)
        wide = []
        for kind in range(KINDS):
            after = rolled(after_ref[kind, group], -STEPS * place, 0)
            before = rolled(before_ref[kind, group], rows - STEPS - STEPS * place, 0)
            halo = jnp.where(row < STEPS, after, before)
            wide.append(jnp.concatenate([planes[kind], halo], axis=0))
        return wide

    return at


def pack_faces(perm_ref, e_ref, h_ref, m_ref, forth_ref, back_ref):
    layers, rows, columns = m_ref.shape
    rates = rates_of(perm_ref, perm_ref.shape[0], (rows, columns))
    own = own_planes(e_ref, h_ref, m_ref, rates)
    row = iota((rows, columns), 0)
    per_group = rows // STEPS
    for group in range(layers // per_group):
        planes = [own(group * per_group + place) for place in range(per_group)]
        for kind in range(KINDS):
            forth = rolled(planes[0][kind], STEPS - rows, 0)
            back = planes[0][kind]
            for place in range(1, per_group):
                spot = STEPS * place
                here = planes[place][kind]
                forth = jnp.where(row >= spot, rolled(here, spot + STEPS - rows, 0), forth)
                back = jnp.where(row >= spot, rolled(here, spot, 0), back)
            forth_ref[kind, group] = forth
            back_ref[kind, group] = back


def packed_edges(planes, layers, spot):
    tile = None
    for z in range(layers):
        here = rolled(planes[z], spot + z * SEAM + EDGE, 1)
        if tile is None:
            tile = here
        else:
            tile = jnp.where(iota(tile.shape, 1) >= spot + z * SEAM, here, tile)
    return tile


def monitor_message(perm_ref, e_ref, h_ref, m_ref, before_ref, after_ref, message_ref):
    layers, rows, columns = m_ref.shape
    rates = rates_of(perm_ref, perm_ref.shape[0], (rows, columns))
    wide = widened_planes(own_planes(e_ref, h_ref, m_ref, rates), before_ref, after_ref)
    walk = Leapfrog(wide, layers=layers)
    span = layers * SEAM
    per_tile = columns // span
    lane = iota((2 * rows, columns), 1)
    for tile in range(-(-KINDS // per_tile)):
        total = None
        for place in range(min(per_tile, KINDS - tile * per_tile)):
            kind = tile * per_tile + place
            edges = packed_edges([walk.first(z)[kind] for z in range(layers)], layers, place * span)
            total = edges if total is None else jnp.where(lane >= place * span, edges, total)
        message_ref[pl.ds(tile * 2 * rows, 2 * rows), :] = total
    base = -(-KINDS // per_tile) * 2 * rows
    for s in range(STEPS):
        for c, record in enumerate(walk.records(s + 1, layers - 1)):
            message_ref[pl.ds(base + (s * RECORDS + c) * rows, rows), :] = record[:rows]


def all_edges(perm_ref, e_ref, h_ref, m_ref, before_ref, after_ref, edges_ref):
    layers, rows, columns = m_ref.shape
    rates = rates_of(perm_ref, perm_ref.shape[0], (rows, columns))
    wide = widened_planes(own_planes(e_ref, h_ref, m_ref, rates), before_ref, after_ref)
    planes = [wide(z) for z in range(layers)]
    for kind in range(KINDS):
        edges_ref[kind] = packed_edges([planes[z][kind] for z in range(layers)], layers, 0)


def waves_of(coef_ref, wave):
    base = wave * (STEPS * 4)
    return lambda s, half, part: coef_ref[base + (s * 2 + half) * 2 + part]


def y_orders(group_waves, blocks, me_ref, wave_ref, coef_ref, table_ref, *refs):
    messages = refs[:blocks]
    spectra = refs[blocks : 2 * blocks]
    out_ref = refs[2 * blocks]
    _, _, _, rows, columns = spectra[0].shape
    me = me_ref[0]
    layers = DEEP
    span = layers * SEAM
    per_tile = columns // span
    lane = iota((2 * rows, columns), 1)
    column = lane % SEAM
    walks = []
    for tile in range(-(-blocks // per_tile)):
        seams = range(tile * per_tile, min(blocks, (tile + 1) * per_tile))
        kinds = []
        for kind in range(KINDS):
            source = pl.ds(kind // per_tile * 2 * rows, 2 * rows)
            total = None
            for seam in seams:
                spot = (seam % per_tile) * span
                shift = spot - kind % per_tile * span
                left = rolled(messages[seam][source, :], shift, 1)
                right = rolled(messages[(seam + 1) % blocks][source, :], shift, 1)
                here = jnp.where(column < EDGE, left, right)
                total = here if total is None else jnp.where(lane >= spot, here, total)
            kinds.append(total)
        walks.append(seam_leapfrog(kinds, layers))
    base = -(-KINDS // per_tile) * 2 * rows
    narrow = iota((rows, columns), 1)
    coefs = [waves_of(coef_ref, wave_ref[me * group_waves + w]) for w in range(group_waves)]
    total = None
    for block in range(blocks):
        record = []
        for s in range(STEPS):
            for c in range(RECORDS):
                value = messages[block][pl.ds(base + (s * RECORDS + c) * rows, rows), :]
                after, before = block, (block - 1) % blocks
                spot_after = (after % per_tile) * span + (layers - 1) * SEAM + EDGE
                spot_before = (before % per_tile) * span + (layers - 1) * SEAM + EDGE
                from_after = walks[after // per_tile].records(s + 1, 0)[c][:rows]
                from_before = walks[before // per_tile].records(s + 1, 0)[c][:rows]
                value = jnp.where(narrow >= columns - STEPS, rolled(from_after, -spot_after, 1), value)
                value = jnp.where(narrow < STEPS, rolled(from_before, -spot_before, 1), value)
                record.append(value)
        parts = []
        for part in range(2):
            for w in range(group_waves):
                for c in range(RECORDS):
                    value = spectra[block][w, part, c]
                    for s in range(STEPS):
                        value = value + coefs[w](s, c // 2, part) * record[s * RECORDS + c]
                    parts.append(value)
        values = jnp.concatenate(parts, axis=0)
        owner = lax.rem(me + block, blocks)
        table = table_ref[pl.ds(pl.multiple_of(owner * columns, columns), columns), :]
        product = jnp.dot(
            values, table, precision=lax.Precision.HIGHEST, preferred_element_type=jnp.float32
        )
        total = product if total is None else total + product
    half = group_waves * RECORDS * rows
    real = total[:half, :OY] + total[half:, OY:]
    imag = total[half:, :OY] - total[:half, OY:]
    sources = group_waves * RECORDS
    targets = out_ref.shape[0]
    kept = OY // targets
    wide = iota((rows, OY), 1)
    per_out = OY // kept
    for target in range(targets):
        for part, values in enumerate((real, imag)):
            for first in range(0, sources, per_out):
                tile = None
                for source in range(first, min(sources, first + per_out)):
                    spot = (source - first) * kept
                    here = values[source * rows : (source + 1) * rows]
                    here = rolled(here, spot - target * kept, 1)
                    tile = here if tile is None else jnp.where(wide >= spot, here, tile)
                place = (first // per_out * 2 + part) * rows
                out_ref[target, pl.ds(place, rows), :] = tile


def x_orders(kept, values_ref, table_ref, out_ref):
    sources, height, lanes = values_ref.shape
    waves, _, records, _, _ = out_ref.shape
    depth = table_ref.shape[0]
    rows = depth // sources
    per_tile = lanes // kept
    for tile in range(height // rows):
        values = jnp.concatenate(
            [values_ref[source, pl.ds(tile * rows, rows), :] for source in range(sources)], axis=0
        )
        result = lax.dot_general(
            values,
            table_ref[...],
            (((0,), (0,)), ((), ())),
            precision=lax.Precision.HIGHEST,
            preferred_element_type=jnp.float32,
        )
        for place in range(per_tile):
            wave, record = divmod(tile * per_tile + place, records)
            if wave < waves:
                here = result[place * kept : (place + 1) * kept]
                out_ref[wave, 0, record] = here[:, :OX]
                out_ref[wave, 1, record] = here[:, OX:]


def local_updates(
    perm_ref,
    wave_ref,
    coef_ref,
    e_ref,
    h_ref,
    m_ref,
    before_ref,
    after_ref,
    edges_ref,
    edges_before_ref,
    edges_after_ref,
    slab_ref,
    monitor_ref,
    e_out,
    h_out,
    slab_out,
    monitor_out,
):
    layers, rows, columns = m_ref.shape
    rates = rates_of(perm_ref, perm_ref.shape[0], (rows, columns))
    wide = widened_planes(own_planes(e_ref, h_ref, m_ref, rates), before_ref, after_ref)
    walk = Leapfrog(wide, layers=layers)
    left = iota((2 * rows, layers * SEAM), 1) % SEAM < EDGE
    mine = [edges_ref[kind] for kind in range(KINDS)]
    after = seam_leapfrog(
        [jnp.where(left, mine[k], edges_after_ref[k]) for k in range(KINDS)], layers
    )
    before = seam_leapfrog(
        [jnp.where(left, edges_before_ref[k], mine[k]) for k in range(KINDS)], layers
    )
    column = iota((rows, columns), 1)
    inner = (column >= STEPS) & (column < columns - STEPS)
    joined = {}

    def mended(s, z, kind):
        if (s, kind) not in joined:
            ends = [(side.e(s, 0) + side.h(s, 0))[kind][:rows] for side in (after, before)]
            joined[s, kind] = jnp.where(left[:rows], ends[0], ends[1])
        value = (walk.e(s, z) + walk.h(s, z))[kind][:rows]
        return jnp.where(inner, value, rolled(joined[s, kind], -(z * SEAM + EDGE), 1))

    middle = layers // 2
    slab_records = [[None] * 2 for _ in range(STEPS)]
    records = [[None] * RECORDS for _ in range(STEPS)]
    for z in range(layers):
        for kind in range(6):
            value = mended(STEPS, z, kind)
            if kind < 3:
                e_out[kind, z] = value
            else:
                h_out[kind - 3, z] = value
        for s in range(STEPS):
            if z == middle:
                slab_records[s] = [mended(s + 1, z, kind) for kind in (0, 1)]
            if z == layers - 1:
                records[s] = [mended(s + 1, z, kind) for kind in (0, 1, 3, 4)]
    frequencies = slab_ref.shape[1] // 2

    def one_frequency(f, carry):
        coef = waves_of(coef_ref, f)
        for c in range(2):
            for part in range(2):
                value = slab_ref[c, part * frequencies + f]
                for s in range(STEPS):
                    value = value + coef(s, 0, part) * slab_records[s][c]
                slab_out[c, part * frequencies + f] = value
        return carry

    lax.fori_loop(0, frequencies, one_frequency, 0, unroll=4)
    for w in range(monitor_ref.shape[0]):
        coef = waves_of(coef_ref, wave_ref[w])
        for part in range(2):
            for c in range(RECORDS):
                value = monitor_ref[w, part, c]
                for s in range(STEPS):
                    value = value + coef(s, c // 2, part) * records[s][c]
                monitor_out[w, part, c] = value


def wave_coefficients(freq_count):
    omegas = OMEGA_LOW + (OMEGA_HIGH - OMEGA_LOW) * np.arange(freq_count) / (freq_count - 1)
    times = TIME_STEP * (np.arange(1, STEPS + 1)[:, None] - np.array([0.0, 0.5])[None, :])
    angles = omegas[:, None, None] * times[None]
    table = np.stack([TIME_STEP * np.cos(angles), -TIME_STEP * np.sin(angles)], axis=-1)
    return table.reshape(-1).astype(np.float32)


def angles_of(length, kept):
    wanted = (np.arange(kept) - kept // 2) % length
    return 2.0 * math.pi / length * (np.arange(length)[:, None] * wanted[None, :] % length)


def y_table(length):
    angles = angles_of(length, OY)
    return np.concatenate([np.cos(angles), np.sin(angles)], axis=1).astype(np.float32)


def x_table(length, blocks, scaling):
    angles = angles_of(length, OX).reshape(blocks, length // blocks, OX)
    real = np.concatenate([np.cos(angles), -np.sin(angles)], axis=2)
    imag = np.concatenate([np.sin(angles), np.cos(angles)], axis=2)
    table = np.stack([real, imag], axis=1) * scaling
    return table.reshape(2 * length, 2 * OX).astype(np.float32)


def call(kernel, in_specs, shapes, *operands, name, flops=0, moved=0, **more):
    out = [jax.ShapeDtypeStruct(shape, jnp.float32) for shape in shapes]
    return pl.pallas_call(
        kernel,
        out_shape=out,
        in_specs=in_specs,
        out_specs=[VMEM] * len(out) if "grid" not in more else more.pop("out_specs"),
        compiler_params=PARAMS,
        cost_estimate=pl.CostEstimate(flops=flops, bytes_accessed=moved, transcendentals=0),
        name=name,
        **more,
    )(*operands)


def per_device(
    electric, magnetic, material, permittivity, slab_spectra, monitor_spectra, wave_index
):
    layers, rows, columns = material.shape
    x_blocks, y_blocks = lax.axis_size("gx"), lax.axis_size("gy")
    waves = monitor_spectra.shape[0]
    group_waves = waves // y_blocks
    me = lax.axis_index("gy")
    fields = (electric, magnetic, material)
    groups = layers * STEPS // rows

    faces = (KINDS, groups, rows, columns)
    forth, back = call(
        pack_faces,
        [SMEM] + [VMEM] * 3,
        [faces, faces],
        permittivity,
        *fields,
        name="pack_faces",
        flops=10**5,
        moved=10**6,
    )
    before = passed_along(forth, "gx", 1)
    after = passed_along(back, "gx", -1)

    spectra = [lax.dynamic_slice_in_dim(monitor_spectra, me * group_waves, group_waves, 0)]
    for distance in range(1, y_blocks):
        target = (me - distance) % y_blocks
        block = lax.dynamic_slice_in_dim(monitor_spectra, target * group_waves, group_waves, 0)
        spectra.append(passed_along(block, "gy", -distance))

    top = (layers - DEEP) // DEEP
    top_group = groups - 1
    tiles = -(-KINDS // (columns // (DEEP * SEAM)))
    height = tiles * 2 * rows + STEPS * RECORDS * rows
    fields_spec = pl.BlockSpec((3, DEEP, rows, columns), lambda i: (0, top, 0, 0))
    faces_spec = pl.BlockSpec((KINDS, 1, rows, columns), lambda i: (0, top_group, 0, 0))
    (message,) = call(
        monitor_message,
        [
            SMEM,
            fields_spec,
            fields_spec,
            pl.BlockSpec((DEEP, rows, columns), lambda i: (top, 0, 0)),
            faces_spec,
            faces_spec,
        ],
        [(height, columns)],
        permittivity,
        *fields,
        before,
        after,
        name="monitor_message",
        flops=10**5,
        moved=10**5,
        grid=(1,),
        out_specs=[pl.BlockSpec((height, columns), lambda i: (0, 0))],
    )
    messages = [message]
    for distance in range(1, y_blocks):
        messages.append(passed_along(message, "gy", -distance))

    (edges,) = call(
        all_edges,
        [SMEM] + [VMEM] * 5,
        [(KINDS, 2 * rows, layers * SEAM)],
        permittivity,
        *fields,
        before,
        after,
        name="all_edges",
        flops=10**5,
        moved=10**6,
    )
    edges_before = passed_along(edges, "gy", 1)
    edges_after = passed_along(edges, "gy", -1)

    coefs = jnp.asarray(wave_coefficients(slab_spectra.shape[1] // 2))
    length_x, length_y = rows * x_blocks, columns * y_blocks
    kept = OY // x_blocks
    out_tiles = -(-group_waves * RECORDS * kept // OY)
    (spectrum_y,) = call(
        functools.partial(y_orders, group_waves, y_blocks),
        [SMEM] * 3 + [VMEM] * (1 + 2 * y_blocks),
        [(x_blocks, out_tiles * 2 * rows, OY)],
        me.reshape(1),
        wave_index,
        coefs,
        jnp.asarray(y_table(length_y)),
        *messages,
        *spectra,
        name="y_orders",
        flops=10**8,
        moved=2 * 10**6,
    )
    swapped = lax.all_to_all(spectrum_y, "gx", split_axis=0, concat_axis=0, tiled=True)

    electric_next, magnetic_next, slab_next, monitor_next = call(
        local_updates,
        [SMEM] * 3 + [VMEM] * 10,
        [electric.shape, magnetic.shape, slab_spectra.shape, monitor_spectra.shape],
        permittivity,
        wave_index,
        coefs,
        *fields,
        before,
        after,
        edges,
        edges_before,
        edges_after,
        slab_spectra,
        monitor_spectra,
        name="local_updates",
        flops=10**7,
        moved=6 * 10**6,
    )

    scaling = 1.0 / math.sqrt(length_x * length_y)
    (orders,) = call(
        functools.partial(x_orders, kept),
        [VMEM] * 2,
        [(group_waves, 2, RECORDS, kept, OX)],
        swapped,
        jnp.asarray(x_table(length_x, x_blocks, scaling)),
        name="x_orders",
        flops=10**7,
        moved=5 * 10**5,
    )
    return (electric_next, magnetic_next, slab_next, monitor_next, orders)


def solution(mesh):
    in_specs = (
        P(None, None, "gx", "gy"),
        P(None, None, "gx", "gy"),
        P(None, "gx", "gy"),
        P(),
        P(None, None, "gx", "gy"),
        P(None, None, None, "gx", "gy"),
        P(),
    )
    out_specs = (
        P(None, None, "gx", "gy"),
        P(None, None, "gx", "gy"),
        P(None, None, "gx", "gy"),
        P(None, None, None, "gx", "gy"),
        P("gy", None, None, "gx", None),
    )
    return jax.shard_map(
        per_device, mesh=mesh, in_specs=in_specs, out_specs=out_specs, check_vma=False
    )
```

```python
import functools
import math

import jax
import jax.numpy as jnp
import numpy as np
from jax import lax
from jax.experimental import pallas as pl
from jax.experimental.pallas import tpu as pltpu
from jax.sharding import PartitionSpec as P

OY = 128
OX = 64

TIME_STEP = 0.5
OMEGA_LOW = 0.15
OMEGA_HIGH = 0.8

STEPS = 2
EDGE = 2 * STEPS
SEAM = 2 * EDGE
DEEP = 4
KINDS = 7
RECORDS = 4

VMEM = pl.BlockSpec(memory_space=pltpu.VMEM)
HBM = pl.BlockSpec(memory_space=pltpu.HBM)
SMEM = pl.BlockSpec(memory_space=pltpu.SMEM)
PARAMS = pltpu.CompilerParams(vmem_limit_bytes=48 * 1024 * 1024)


def passed_along(block, axis, distance):
    devices = range(lax.axis_size(axis))
    route = [((i - distance) % len(devices), i) for i in devices]
    return lax.ppermute(block, axis, route)


def rolled(values, shift, axis):
    shift %= values.shape[axis]
    return pltpu.roll(values, shift, axis) if shift else values


def iota(shape, axis):
    return lax.broadcasted_iota(jnp.int32, shape, axis)


def rates_of(permittivity, classes, shape):
    return [TIME_STEP / jnp.full(shape, permittivity[k], jnp.float32) for k in range(classes)]


def rate_at(material, rates):
    rate = rates[-1]
    for k in range(len(rates) - 2, -1, -1):
        rate = jnp.where(material == k, rates[k], rate)
    return rate


class Leapfrog:
    def __init__(self, start, layers=None, above=None, below=None):
        self.start = start
        self.layers = layers
        self.above = above
        self.below = below
        self.known = {}

    def first(self, z):
        if ("0", z) not in self.known:
            self.known["0", z] = self.start(z)
        return self.known["0", z]

    def e(self, s, z):
        if s == 0:
            return self.first(z)[0:3]
        if ("e", s, z) not in self.known:
            ex, ey, ez = self.e(s - 1, z)
            hx, hy, hz = self.h(s, z)
            if self.layers is None:
                down_x, down_y = self.below(hx), self.below(hy)
            else:
                down_x, down_y = self.h(s, z - 1)[:2] if z else (0.0, 0.0)
            rate = self.first(z)[6]
            self.known["e", s, z] = (
                ex + rate * ((hz - rolled(hz, 1, 1)) - (hy - down_y)),
                ey + rate * ((hx - down_x) - (hz - rolled(hz, 1, 0))),
                ez + rate * ((hy - rolled(hy, 1, 0)) - (hx - rolled(hx, 1, 1))),
            )
        return self.known["e", s, z]

    def h(self, s, z):
        if s == 0:
            return self.first(z)[3:6]
        if ("h", s, z) not in self.known:
            ex, ey, ez = self.e(s - 1, z)
            hx, hy, hz = self.h(s - 1, z)
            if self.layers is None:
                up_x, up_y = self.above(ex), self.above(ey)
            else:
                up_x, up_y = self.e(s - 1, z + 1)[:2] if z + 1 < self.layers else (0.0, 0.0)
            self.known["h", s, z] = (
                hx - TIME_STEP * ((rolled(ez, -1, 1) - ez) - (up_y - ey)),
                hy - TIME_STEP * ((up_x - ex) - (rolled(ez, -1, 0) - ez)),
                hz - TIME_STEP * ((rolled(ey, -1, 0) - ey) - (rolled(ex, -1, 1) - ex)),
            )
        return self.known["h", s, z]

    def records(self, s, z):
        return self.e(s, z)[:2] + self.h(s, z)[:2]


def seam_leapfrog(tiles, layers):
    layer = iota(tiles[0].shape, 1) // SEAM % layers
    return Leapfrog(
        lambda z: tiles,
        above=lambda f: jnp.where(layer < layers - 1, rolled(f, -SEAM, 1), 0.0),
        below=lambda f: jnp.where(layer > 0, rolled(f, SEAM, 1), 0.0),
    )


def own_planes(e_ref, h_ref, m_ref, rates):
    def at(z):
        rate = rate_at(m_ref[z], rates)
        return [e_ref[c, z] for c in range(3)] + [h_ref[c, z] for c in range(3)] + [rate]

    return at


def widened_planes(own, before_ref, after_ref, first_group=0):
    def at(z):
        planes = own(z)
        rows = planes[0].shape[0]
        group, place = divmod(z, rows // STEPS)
        row = iota(planes[0].shape, 0)
        wide = []
        for kind in range(KINDS):
            after = rolled(after_ref[kind, group], -STEPS * place, 0)
            before = rolled(before_ref[kind, group], rows - STEPS - STEPS * place, 0)
            halo = jnp.where(row < STEPS, after, before)
            wide.append(jnp.concatenate([planes[kind], halo], axis=0))
        return wide

    return at


def pack_faces(perm_ref, e_ref, h_ref, m_ref, forth_ref, back_ref):
    layers, rows, columns = m_ref.shape
    rates = rates_of(perm_ref, perm_ref.shape[0], (rows, columns))
    own = own_planes(e_ref, h_ref, m_ref, rates)
    row = iota((rows, columns), 0)
    per_group = rows // STEPS
    for group in range(layers // per_group):
        planes = [own(group * per_group + place) for place in range(per_group)]
        for kind in range(KINDS):
            forth = rolled(planes[0][kind], STEPS - rows, 0)
            back = planes[0][kind]
            for place in range(1, per_group):
                spot = STEPS * place
                here = planes[place][kind]
                forth = jnp.where(row >= spot, rolled(here, spot + STEPS - rows, 0), forth)
                back = jnp.where(row >= spot, rolled(here, spot, 0), back)
            forth_ref[kind, group] = forth
            back_ref[kind, group] = back


def packed_edges(planes, layers, spot):
    tile = None
    for z in range(layers):
        here = rolled(planes[z], spot + z * SEAM + EDGE, 1)
        if tile is None:
            tile = here
        else:
            tile = jnp.where(iota(tile.shape, 1) >= spot + z * SEAM, here, tile)
    return tile


def monitor_message(perm_ref, e_ref, h_ref, m_ref, before_ref, after_ref, near_ref, far_ref):
    layers, rows, columns = m_ref.shape
    rates = rates_of(perm_ref, perm_ref.shape[0], (rows, columns))
    wide = widened_planes(own_planes(e_ref, h_ref, m_ref, rates), before_ref, after_ref)
    low = layers - DEEP
    walk = Leapfrog(lambda z: wide(low + z), layers=DEEP)
    height = 2 * rows
    base = KINDS * height
    far_base = far_tiles(columns) * height
    for s in range(STEPS):
        for c, record in enumerate(walk.records(s + 1, DEEP - 1)):
            place = (s * RECORDS + c) * rows
            near_ref[pl.ds(base + place, rows), :] = record[:rows]
            far_ref[pl.ds(far_base + place, rows), :] = record[:rows]
    planes = [wide(z) for z in range(low)] + [walk.first(z) for z in range(DEEP)]
    span = DEEP * SEAM
    per_tile = columns // span
    total = None
    for kind in range(KINDS):
        edges = packed_edges([planes[z][kind] for z in range(layers)], layers, 0)
        near_ref[pl.ds(kind * height, height), :] = edges
        spot = kind % per_tile * span
        here = rolled(edges, spot - low * SEAM, 1)
        total = jnp.where(iota(here.shape, 1) >= spot, here, total) if spot else here
        far_ref[pl.ds(kind // per_tile * height, height), :] = total


def far_tiles(columns):
    return -(-KINDS // (columns // (DEEP * SEAM)))


def waves_of(coef_ref, wave):
    base = wave * (STEPS * 4)
    return lambda s, half, part: coef_ref[base + (s * 2 + half) * 2 + part]


def exact_dot(left, right, contracted):
    return lax.dot_general(
        left,
        right,
        (contracted, ((), ())),
        precision=lax.Precision.HIGHEST,
        preferred_element_type=jnp.float32,
    )


def packed_orders(values, planes, kept, target):
    rows = values.shape[0] // planes
    lane = iota((rows, OY), 1)
    per_tile = OY // kept
    tiles = []
    for first in range(0, planes, per_tile):
        tile = None
        for plane in range(first, min(planes, first + per_tile)):
            spot = (plane - first) * kept
            here = rolled(values[plane * rows : (plane + 1) * rows], spot - target * kept, 1)
            tile = here if tile is None else jnp.where(lane >= spot, here, tile)
        tiles.append(tile)
    return tiles


def y_monitor(group_waves, table_ref, spectra_ref, out_ref):
    waves, _, records, rows, columns = spectra_ref.shape
    total = None
    for block in range(waves // group_waves):
        table = table_ref[pl.ds(block * columns, columns), :]
        parts = []
        for part in range(2):
            for w in range(group_waves):
                parts += [spectra_ref[block * group_waves + w, part, c] for c in range(records)]
        product = exact_dot(jnp.concatenate(parts, axis=0), table, ((1,), (0,)))
        total = product if total is None else total + product
    waves = group_waves
    half = waves * records * rows
    real = total[:half, :OY] + total[half:, OY:]
    imag = total[half:, :OY] - total[:half, OY:]
    targets = out_ref.shape[0]
    for target in range(targets):
        for part, values in enumerate((real, imag)):
            tiles = packed_orders(values, waves * records, OY // targets, target)
            for i, tile in enumerate(tiles):
                out_ref[target, pl.ds((i * 2 + part) * rows, rows), :] = tile


def y_records(waves, wave_ref, coef_ref, table_ref, monitor_ref, *refs):
    *messages, out_ref = refs
    blocks = len(messages)
    columns = messages[0].shape[1]
    targets, height, _ = out_ref.shape
    kept = OY // targets
    out_tiles = -(-waves * RECORDS * kept // OY)
    rows = height // (2 * out_tiles)
    me = lax.axis_index("gy")
    span = DEEP * SEAM
    per_tile = columns // span
    lane = iota((2 * rows, columns), 1)
    column = lane % SEAM

    near_height = (KINDS * 2 + STEPS * RECORDS) * rows

    def edges_of(block, kind, spot):
        if messages[block].shape[0] == near_height:
            return rolled(messages[block][pl.ds(kind * 2 * rows, 2 * rows), :], spot + span, 1)
        source = pl.ds(kind // per_tile * 2 * rows, 2 * rows)
        return rolled(messages[block][source, :], spot - kind % per_tile * span, 1)

    walks = []
    for tile in range(-(-blocks // per_tile)):
        seams = range(tile * per_tile, min(blocks, (tile + 1) * per_tile))
        kinds = []
        for kind in range(KINDS):
            total = None
            for seam in seams:
                spot = (seam % per_tile) * span
                left = edges_of(seam, kind, spot)
                right = edges_of((seam + 1) % blocks, kind, spot)
                here = jnp.where(column < EDGE, left, right)
                total = here if total is None else jnp.where(lane >= spot, here, total)
            kinds.append(total)
        walks.append(seam_leapfrog(kinds, DEEP))
    narrow = iota((rows, columns), 1)
    total = None
    for block in range(blocks):
        record = []
        base = messages[block].shape[0] - STEPS * RECORDS * rows
        for s in range(STEPS):
            for c in range(RECORDS):
                value = messages[block][pl.ds(base + (s * RECORDS + c) * rows, rows), :]
                after, before = block, (block - 1) % blocks
                spot_after = (after % per_tile) * span + (DEEP - 1) * SEAM + EDGE
                spot_before = (before % per_tile) * span + (DEEP - 1) * SEAM + EDGE
                from_after = walks[after // per_tile].records(s + 1, 0)[c][:rows]
                from_before = walks[before // per_tile].records(s + 1, 0)[c][:rows]
                value = jnp.where(narrow >= columns - STEPS, rolled(from_after, -spot_after, 1), value)
                value = jnp.where(narrow < STEPS, rolled(from_before, -spot_before, 1), value)
                record.append(value)
        owner = lax.rem(me + block, blocks)
        table = table_ref[pl.ds(pl.multiple_of(owner * columns, columns), columns), :]
        product = exact_dot(jnp.concatenate(record, axis=0), table, ((1,), (0,)))
        total = product if total is None else total + product
    lane = iota((rows, OY), 1)
    per_wave = RECORDS * kept
    per_tile = OY // per_wave
    weights = []
    for tile in range(out_tiles):
        some = range(tile * per_tile, min(waves, (tile + 1) * per_tile))
        coefs = [waves_of(coef_ref, wave_ref[me * waves + w]) for w in some]
        for s in range(STEPS):
            for part in range(2):
                weight = None
                for i, coef in enumerate(coefs):
                    for half in range(2):
                        value = jnp.full((rows, OY), coef(s, half, part), jnp.float32)
                        spot = i * per_wave + half * (per_wave // 2)
                        weight = value if weight is None else jnp.where(lane >= spot, value, weight)
                weights.append(weight)
    for target in range(targets):
        sides = []
        for part in range(2):
            values = total[:, part * OY : (part + 1) * OY]
            (packed,) = packed_orders(values, STEPS * RECORDS, kept, target)
            steps = []
            for s in range(STEPS):
                spread = None
                for i in range(min(per_tile, waves)):
                    here = rolled(packed, i * per_wave - s * per_wave, 1)
                    spread = here if i == 0 else jnp.where(lane >= i * per_wave, here, spread)
                steps.append(spread)
            sides.append(steps)
        for tile in range(out_tiles):
            for part in range(2):
                place = pl.ds((tile * 2 + part) * rows, rows)
                value = monitor_ref[target, place, :]
                for s in range(STEPS):
                    real, imag = weights[(tile * STEPS + s) * 2 : (tile * STEPS + s) * 2 + 2]
                    if part == 0:
                        value = value + (real * sides[0][s] + imag * sides[1][s])
                    else:
                        value = value + (imag * sides[0][s] - real * sides[1][s])
                out_ref[target, place, :] = value


def x_orders(kept, values_ref, table_ref, out_ref):
    sources, height, lanes = values_ref.shape
    waves, _, records, _, _ = out_ref.shape
    depth = table_ref.shape[0]
    rows = depth // sources
    per_tile = lanes // kept
    for tile in range(height // rows):
        values = jnp.concatenate(
            [values_ref[source, pl.ds(tile * rows, rows), :] for source in range(sources)], axis=0
        )
        result = exact_dot(values, table_ref[...], ((0,), (0,)))
        for place in range(per_tile):
            wave, record = divmod(tile * per_tile + place, records)
            if wave < waves:
                here = result[place * kept : (place + 1) * kept]
                out_ref[wave, 0, record] = here[:, :OX]
                out_ref[wave, 1, record] = here[:, OX:]


def local_updates(
    perm_ref,
    wave_ref,
    coef_ref,
    e_ref,
    h_ref,
    m_ref,
    before_ref,
    after_ref,
    message_ref,
    message_before_ref,
    message_after_ref,
    slab_ref,
    monitor_ref,
    e_out,
    h_out,
    slab_out,
    monitor_out,
):
    layers, rows, columns = m_ref.shape
    rates = rates_of(perm_ref, perm_ref.shape[0], (rows, columns))
    wide = widened_planes(own_planes(e_ref, h_ref, m_ref, rates), before_ref, after_ref)
    walk = Leapfrog(wide, layers=layers)
    left = iota((2 * rows, layers * SEAM), 1) % SEAM < EDGE
    edges = [
        [ref[pl.ds(kind * 2 * rows, 2 * rows), :] for kind in range(KINDS)]
        for ref in (message_before_ref, message_ref, message_after_ref)
    ]
    before = seam_leapfrog([jnp.where(left, edges[0][k], edges[1][k]) for k in range(KINDS)], layers)
    after = seam_leapfrog([jnp.where(left, edges[1][k], edges[2][k]) for k in range(KINDS)], layers)
    column = iota((rows, columns), 1)
    inner = (column >= STEPS) & (column < columns - STEPS)
    joined = {}

    def mended(s, z, kind):
        if (s, kind) not in joined:
            ends = [(side.e(s, 0) + side.h(s, 0))[kind][:rows] for side in (after, before)]
            joined[s, kind] = jnp.where(left[:rows], ends[0], ends[1])
        value = (walk.e(s, z) + walk.h(s, z))[kind][:rows]
        return jnp.where(inner, value, rolled(joined[s, kind], -(z * SEAM + EDGE), 1))

    middle = layers // 2
    slab_records = [[None] * 2 for _ in range(STEPS)]
    records = [[None] * RECORDS for _ in range(STEPS)]
    for z in range(layers):
        for kind in range(6):
            value = mended(STEPS, z, kind)
            if kind < 3:
                e_out[kind, z] = value
            else:
                h_out[kind - 3, z] = value
        for s in range(STEPS):
            if z == middle:
                slab_records[s] = [mended(s + 1, z, kind) for kind in (0, 1)]
            if z == layers - 1:
                records[s] = [mended(s + 1, z, kind) for kind in (0, 1, 3, 4)]
    frequencies = slab_ref.shape[1] // 2

    def one_frequency(f, carry):
        coef = waves_of(coef_ref, f)
        for c in range(2):
            for part in range(2):
                value = slab_ref[c, part * frequencies + f]
                for s in range(STEPS):
                    value = value + coef(s, 0, part) * slab_records[s][c]
                slab_out[c, part * frequencies + f] = value
        return carry

    lax.fori_loop(0, frequencies, one_frequency, 0, unroll=4)
    for w in range(monitor_ref.shape[0]):
        coef = waves_of(coef_ref, wave_ref[w])
        for part in range(2):
            for c in range(RECORDS):
                value = monitor_ref[w, part, c]
                for s in range(STEPS):
                    value = value + coef(s, c // 2, part) * records[s][c]
                monitor_out[w, part, c] = value


def wave_coefficients(freq_count):
    omegas = OMEGA_LOW + (OMEGA_HIGH - OMEGA_LOW) * np.arange(freq_count) / (freq_count - 1)
    times = TIME_STEP * (np.arange(1, STEPS + 1)[:, None] - np.array([0.0, 0.5])[None, :])
    angles = omegas[:, None, None] * times[None]
    table = np.stack([TIME_STEP * np.cos(angles), -TIME_STEP * np.sin(angles)], axis=-1)
    return table.reshape(-1).astype(np.float32)


def angles_of(length, kept):
    wanted = (np.arange(kept) - kept // 2) % length
    return 2.0 * math.pi / length * (np.arange(length)[:, None] * wanted[None, :] % length)


def y_table(length):
    angles = angles_of(length, OY)
    return np.concatenate([np.cos(angles), np.sin(angles)], axis=1).astype(np.float32)


def x_table(length, blocks, scaling):
    angles = angles_of(length, OX).reshape(blocks, length // blocks, OX)
    real = np.concatenate([np.cos(angles), -np.sin(angles)], axis=2)
    imag = np.concatenate([np.sin(angles), np.cos(angles)], axis=2)
    table = np.stack([real, imag], axis=1) * scaling
    return table.reshape(2 * length, 2 * OX).astype(np.float32)


def call(kernel, in_specs, shapes, *operands, name, flops=0, moved=0, **more):
    out = [jax.ShapeDtypeStruct(shape, jnp.float32) for shape in shapes]
    return pl.pallas_call(
        kernel,
        out_shape=out,
        in_specs=in_specs,
        out_specs=[VMEM] * len(out) if "grid" not in more else more.pop("out_specs"),
        compiler_params=PARAMS,
        cost_estimate=pl.CostEstimate(flops=flops, bytes_accessed=moved, transcendentals=0),
        name=name,
        **more,
    )(*operands)


def per_device(
    electric, magnetic, material, permittivity, slab_spectra, monitor_spectra, wave_index
):
    layers, rows, columns = material.shape
    x_blocks, y_blocks = lax.axis_size("gx"), lax.axis_size("gy")
    waves = monitor_spectra.shape[0]
    group_waves = waves // y_blocks
    fields = (electric, magnetic, material)
    groups = layers * STEPS // rows

    spectra = lax.all_to_all(monitor_spectra, "gy", split_axis=0, concat_axis=0, tiled=True)

    faces = (KINDS, groups, rows, columns)
    forth, back = call(
        pack_faces,
        [SMEM] + [VMEM] * 3,
        [faces, faces],
        permittivity,
        *fields,
        name="pack_faces",
        flops=10**5,
        moved=10**6,
    )
    before = passed_along(forth, "gx", 1)
    after = passed_along(back, "gx", -1)

    near_height = (KINDS * 2 + STEPS * RECORDS) * rows
    far_height = (far_tiles(columns) * 2 + STEPS * RECORDS) * rows
    near, far = call(
        monitor_message,
        [SMEM] + [VMEM] * 5,
        [(near_height, columns), (far_height, columns)],
        permittivity,
        *fields,
        before,
        after,
        name="monitor_message",
        flops=10**5,
        moved=10**6,
    )
    messages = [near]
    for distance in range(1, y_blocks):
        message = near if distance in (1, y_blocks - 1) else far
        messages.append(passed_along(message, "gy", -distance))

    coefs = jnp.asarray(wave_coefficients(slab_spectra.shape[1] // 2))
    length_x, length_y = rows * x_blocks, columns * y_blocks
    kept = OY // x_blocks
    out_tiles = -(-group_waves * RECORDS * kept // OY)
    sums_y = jnp.asarray(y_table(length_y))
    (monitor_y,) = call(
        functools.partial(y_monitor, group_waves),
        [VMEM] * 2,
        [(x_blocks, out_tiles * 2 * rows, OY)],
        sums_y,
        spectra,
        name="y_monitor",
        flops=10**8,
        moved=2 * 10**6,
    )
    (spectrum_y,) = call(
        functools.partial(y_records, group_waves),
        [SMEM] * 2 + [VMEM] * (2 + y_blocks),
        [monitor_y.shape],
        wave_index,
        coefs,
        sums_y,
        monitor_y,
        *messages,
        name="y_records",
        flops=10**8,
        moved=2 * 10**6,
    )
    swapped = lax.all_to_all(spectrum_y, "gx", split_axis=0, concat_axis=0, tiled=True)

    electric_next, magnetic_next, slab_next, monitor_next = call(
        local_updates,
        [SMEM] * 3 + [VMEM] * 10,
        [electric.shape, magnetic.shape, slab_spectra.shape, monitor_spectra.shape],
        permittivity,
        wave_index,
        coefs,
        *fields,
        before,
        after,
        messages[0],
        messages[-1],
        messages[1 % y_blocks],
        slab_spectra,
        monitor_spectra,
        name="local_updates",
        flops=10**7,
        moved=6 * 10**6,
    )

    scaling = 1.0 / math.sqrt(length_x * length_y)
    (orders,) = call(
        functools.partial(x_orders, kept),
        [VMEM] * 2,
        [(group_waves, 2, RECORDS, kept, OX)],
        swapped,
        jnp.asarray(x_table(length_x, x_blocks, scaling)),
        name="x_orders",
        flops=10**7,
        moved=5 * 10**5,
    )
    return (electric_next, magnetic_next, slab_next, monitor_next, orders)


def solution(mesh):
    in_specs = (
        P(None, None, "gx", "gy"),
        P(None, None, "gx", "gy"),
        P(None, "gx", "gy"),
        P(),
        P(None, None, "gx", "gy"),
        P(None, None, None, "gx", "gy"),
        P(),
    )
    out_specs = (
        P(None, None, "gx", "gy"),
        P(None, None, "gx", "gy"),
        P(None, None, "gx", "gy"),
        P(None, None, None, "gx", "gy"),
        P("gy", None, None, "gx", None),
    )
    return jax.shard_map(
        per_device, mesh=mesh, in_specs=in_specs, out_specs=out_specs, check_vma=False
    )
```

```python
import functools
import math

import jax
import jax.numpy as jnp
import ml_dtypes
import numpy as np
from jax import lax
from jax.experimental import pallas as pl
from jax.experimental.pallas import tpu as pltpu
from jax.sharding import PartitionSpec as P

OY = 128
OX = 64

TIME_STEP = 0.5
OMEGA_LOW = 0.15
OMEGA_HIGH = 0.8

STEPS = 2
EDGE = 2 * STEPS
SEAM = 2 * EDGE
DEEP = 4
OUTER = SEAM // STEPS
KINDS = 7
RECORDS = 4

VMEM = pl.BlockSpec(memory_space=pltpu.VMEM)
HBM = pl.BlockSpec(memory_space=pltpu.HBM)
SMEM = pl.BlockSpec(memory_space=pltpu.SMEM)
PARAMS = pltpu.CompilerParams(vmem_limit_bytes=48 * 1024 * 1024)


def in_hbm(array):
    return pltpu.with_memory_space_constraint(array, pltpu.HBM)


def passed_along(block, axis, distance):
    devices = range(lax.axis_size(axis))
    route = [((i - distance) % len(devices), i) for i in devices]
    return lax.ppermute(block, axis, route)


def rolled(values, shift, axis):
    shift %= values.shape[axis]
    return pltpu.roll(values, shift, axis) if shift else values


def iota(shape, axis):
    return lax.broadcasted_iota(jnp.int32, shape, axis)


def rates_of(permittivity, classes, shape):
    return [TIME_STEP / jnp.full(shape, permittivity[k], jnp.float32) for k in range(classes)]


def rate_at(material, rates):
    rate = rates[-1]
    for k in range(len(rates) - 2, -1, -1):
        rate = jnp.where(material == k, rates[k], rate)
    return rate


class Leapfrog:
    def __init__(self, start, layers=None, above=None, below=None):
        self.start = start
        self.layers = layers
        self.above = above
        self.below = below
        self.known = {}

    def first(self, z):
        if ("0", z) not in self.known:
            self.known["0", z] = self.start(z)
        return self.known["0", z]

    def e(self, s, z):
        if s == 0:
            return self.first(z)[0:3]
        if ("e", s, z) not in self.known:
            ex, ey, ez = self.e(s - 1, z)
            hx, hy, hz = self.h(s, z)
            if self.layers is None:
                down_x, down_y = self.below(hx), self.below(hy)
            else:
                down_x, down_y = self.h(s, z - 1)[:2] if z else (0.0, 0.0)
            rate = self.first(z)[6]
            self.known["e", s, z] = (
                ex + rate * ((hz - rolled(hz, 1, 1)) - (hy - down_y)),
                ey + rate * ((hx - down_x) - (hz - rolled(hz, 1, 0))),
                ez + rate * ((hy - rolled(hy, 1, 0)) - (hx - rolled(hx, 1, 1))),
            )
        return self.known["e", s, z]

    def h(self, s, z):
        if s == 0:
            return self.first(z)[3:6]
        if ("h", s, z) not in self.known:
            ex, ey, ez = self.e(s - 1, z)
            hx, hy, hz = self.h(s - 1, z)
            if self.layers is None:
                up_x, up_y = self.above(ex), self.above(ey)
            else:
                up_x, up_y = self.e(s - 1, z + 1)[:2] if z + 1 < self.layers else (0.0, 0.0)
            self.known["h", s, z] = (
                hx - TIME_STEP * ((rolled(ez, -1, 1) - ez) - (up_y - ey)),
                hy - TIME_STEP * ((up_x - ex) - (rolled(ez, -1, 0) - ez)),
                hz - TIME_STEP * ((rolled(ey, -1, 0) - ey) - (rolled(ex, -1, 1) - ex)),
            )
        return self.known["h", s, z]

    def records(self, s, z):
        return self.e(s, z)[:2] + self.h(s, z)[:2]


def seam_leapfrog(tiles, layers):
    layer = iota(tiles[0].shape, 1) // SEAM % layers
    return Leapfrog(
        lambda z: tiles,
        above=lambda f: jnp.where(layer < layers - 1, rolled(f, -SEAM, 1), 0.0),
        below=lambda f: jnp.where(layer > 0, rolled(f, SEAM, 1), 0.0),
    )


def own_planes(e_ref, h_ref, m_ref, rates):
    def at(z):
        rate = rate_at(m_ref[z], rates)
        return [e_ref[c, z] for c in range(3)] + [h_ref[c, z] for c in range(3)] + [rate]

    return at


def widened_planes(own, before_ref, after_ref, first_group=0):
    def at(z):
        planes = own(z)
        rows = planes[0].shape[0]
        group, place = divmod(z, rows // STEPS)
        row = iota(planes[0].shape, 0)
        wide = []
        for kind in range(KINDS):
            after = rolled(after_ref[kind, group], -STEPS * place, 0)
            before = rolled(before_ref[kind, group], rows - STEPS - STEPS * place, 0)
            halo = jnp.where(row < STEPS, after, before)
            wide.append(jnp.concatenate([planes[kind], halo], axis=0))
        return wide

    return at


def block_copy(distance, spectra_any, block_ref, semaphore):
    waves = block_ref.shape[0]
    blocks = spectra_any.shape[0] // waves
    owner = lax.rem(lax.axis_index("gy") + blocks - distance, blocks)
    source = spectra_any.at[pl.ds(owner * waves, waves)]
    return pltpu.make_async_copy(source, block_ref, semaphore)


def pack_faces(
    distances,
    perm_any,
    e_any,
    h_any,
    m_any,
    spectra_any,
    forth_ref,
    back_ref,
    *refs,
):
    *block_refs, perm_ref, e_ref, h_ref, m_ref, ready, sent = refs
    sources, targets = (e_any, h_any, m_any, perm_any), (e_ref, h_ref, m_ref, perm_ref)
    copies = [
        pltpu.make_async_copy(source, target, ready.at[i])
        for i, (source, target) in enumerate(zip(sources, targets))
    ]
    for i, (distance, block_ref) in enumerate(zip(distances, block_refs)):
        copies.append(block_copy(distance, spectra_any, block_ref, sent.at[i]))
    for copy in copies:
        copy.start()
    for copy in copies[:4]:
        copy.wait()
    layers, rows, columns = m_ref.shape
    rates = rates_of(perm_ref, perm_ref.shape[0], (rows, columns))
    own = own_planes(e_ref, h_ref, m_ref, rates)
    row = iota((rows, columns), 0)
    per_group = rows // STEPS
    for group in range(layers // per_group):
        planes = [own(group * per_group + place) for place in range(per_group)]
        for kind in range(KINDS):
            forth = rolled(planes[0][kind], STEPS - rows, 0)
            back = planes[0][kind]
            for place in range(1, per_group):
                spot = STEPS * place
                here = planes[place][kind]
                forth = jnp.where(row >= spot, rolled(here, spot + STEPS - rows, 0), forth)
                back = jnp.where(row >= spot, rolled(here, spot, 0), back)
            forth_ref[kind, group] = forth
            back_ref[kind, group] = back
    for copy in copies[4:]:
        copy.wait()


def blocks_transposed(tiles):
    tiles = list(tiles)
    count = len(tiles)
    width = tiles[0].shape[1] // count
    block = iota(tiles[0].shape, 1) // width
    bit = 1
    while bit < count:
        low = (block & bit) == 0
        for i in range(count):
            if not i & bit:
                first, second = tiles[i], tiles[i + bit]
                tiles[i] = jnp.where(low, first, rolled(second, bit * width, 1))
                tiles[i + bit] = jnp.where(low, rolled(first, -bit * width, 1), second)
        bit *= 2
    return tiles


def packed_edges(planes, layers, spot):
    tile = None
    for z in range(layers):
        here = rolled(planes[z], spot + z * SEAM + EDGE, 1)
        if tile is None:
            tile = here
        else:
            tile = jnp.where(iota(tile.shape, 1) >= spot + z * SEAM, here, tile)
    return tile


def monitor_message(
    distances,
    perm_ref,
    e_ref,
    h_ref,
    m_ref,
    before_ref,
    after_ref,
    spectra_any,
    forth_ref,
    back_ref,
    far_ref,
    edges_ref,
    *refs,
):
    *block_refs, sent = refs
    copies = [
        block_copy(distance, spectra_any, block_ref, sent.at[i])
        for i, (distance, block_ref) in enumerate(zip(distances, block_refs))
    ]
    for copy in copies:
        copy.start()
    layers, rows, columns = m_ref.shape
    rates = rates_of(perm_ref, perm_ref.shape[0], (rows, columns))
    wide = widened_planes(own_planes(e_ref, h_ref, m_ref, rates), before_ref, after_ref)
    low = layers - DEEP
    walk = Leapfrog(lambda z: wide(low + z), layers=DEEP)
    height = 2 * rows
    messages = (forth_ref, back_ref, far_ref)
    for s in range(STEPS):
        for c, record in enumerate(walk.records(s + 1, DEEP - 1)):
            place = pl.ds((s * RECORDS + c) * rows, rows)
            for ref in messages:
                ref[place, :] = record[:rows]
    planes = [wide(z) for z in range(low)] + [walk.first(z) for z in range(DEEP)]
    span = DEEP * SEAM
    per_tile = columns // span
    base = STEPS * RECORDS * rows
    outer = base + message_tiles(columns) * height
    total = forth = back = None
    for kind in range(KINDS):
        edges = packed_edges([planes[z][kind] for z in range(layers)], layers, 0)
        edges_ref[kind] = edges
        lane = iota(edges.shape, 1)
        spot = kind % per_tile * span
        here = rolled(edges, spot - low * SEAM, 1)
        total = jnp.where(lane >= spot, here, total) if spot else here
        place = pl.ds(base + kind // per_tile * height, height)
        for ref in messages:
            ref[place, :] = total
        spot = kind % OUTER * STEPS
        here = rolled(edges, spot - STEPS, 1)
        forth = jnp.where(lane % SEAM >= spot, here, forth) if spot else here
        here = rolled(edges, spot - EDGE, 1)
        back = jnp.where(lane % SEAM >= spot, here, back) if spot else here
        place = pl.ds(outer + kind // OUTER * height, height)
        forth_ref[place, :] = forth
        back_ref[place, :] = back
    for copy in copies:
        copy.wait()


def message_tiles(columns):
    return -(-KINDS // (columns // (DEEP * SEAM)))


def waves_of(coef_ref, wave):
    base = wave * (STEPS * 4)
    return lambda s, half, part: coef_ref[base + (s * 2 + half) * 2 + part]


def exact_dot(left, right, contracted):
    return lax.dot_general(
        left,
        right,
        (contracted, ((), ())),
        precision=lax.Precision.HIGHEST,
        preferred_element_type=jnp.float32,
    )


def split_dot(values, tables, total):
    coarse = values.astype(jnp.bfloat16)
    fine = (values - coarse.astype(jnp.float32)).astype(jnp.bfloat16)
    for left, right in ((coarse, tables[0]), (fine, tables[0]), (coarse, tables[1])):
        product = jnp.dot(left, right, preferred_element_type=jnp.float32)
        total = product if total is None else total + product
    return total


def packed_orders(values, planes, kept):
    rows = values.shape[0] // planes
    parts = [values[plane * rows : (plane + 1) * rows] for plane in range(planes)]
    targets = per_tile = OY // kept
    if planes % per_tile == 0 and not targets & (targets - 1):
        groups = [parts[i : i + per_tile] for i in range(0, planes, per_tile)]
        return list(zip(*[blocks_transposed(group) for group in groups]))
    lane = iota((rows, OY), 1)
    packed = []
    for target in range(targets):
        tiles = []
        for first in range(0, planes, per_tile):
            tile = None
            for plane in range(first, min(planes, first + per_tile)):
                spot = (plane - first) * kept
                here = rolled(parts[plane], spot - target * kept, 1)
                tile = here if tile is None else jnp.where(lane >= spot, here, tile)
            tiles.append(tile)
        packed.append(tiles)
    return packed


def y_monitor(wave_ref, coef_ref, table_ref, slab_any, monitor_any, *refs):
    *spectra, out_ref, weights_ref, slab_ref, monitor_ref, ready = refs
    copies = [
        pltpu.make_async_copy(slab_any, slab_ref, ready.at[0]),
        pltpu.make_async_copy(monitor_any, monitor_ref, ready.at[1]),
    ]
    for copy in copies:
        copy.start()
    blocks = len(spectra)
    waves, _, records, rows, columns = spectra[0].shape
    me = lax.axis_index("gy")
    total = None
    for block in range(blocks):
        owner = lax.rem(me + block, blocks)
        table = table_ref[pl.ds(pl.multiple_of(owner * columns, columns), columns), :]
        parts = []
        for part in range(2):
            for w in range(waves):
                parts += [spectra[block][w, part, c] for c in range(records)]
        product = exact_dot(jnp.concatenate(parts, axis=0), table, ((1,), (0,)))
        total = product if total is None else total + product
    half = waves * records * rows
    real = total[:half, :OY] + total[half:, OY:]
    imag = total[half:, :OY] - total[:half, OY:]
    targets = out_ref.shape[0]
    for part, values in enumerate((real, imag)):
        packed = packed_orders(values, waves * records, OY // targets)
        for target in range(targets):
            for i, tile in enumerate(packed[target]):
                out_ref[target, pl.ds((i * 2 + part) * rows, rows), :] = tile
    kept = OY // targets
    lane = iota((rows, OY), 1)
    per_wave = RECORDS * kept
    per_tile = OY // per_wave
    for tile in range(weights_ref.shape[0] // (2 * STEPS)):
        some = range(tile * per_tile, min(waves, (tile + 1) * per_tile))
        coefs = [waves_of(coef_ref, wave_ref[me * waves + w]) for w in some]
        for s in range(STEPS):
            for part in range(2):
                weight = None
                for i, coef in enumerate(coefs):
                    for half in range(2):
                        value = jnp.full((rows, OY), coef(s, half, part), jnp.float32)
                        spot = i * per_wave + half * (per_wave // 2)
                        weight = value if weight is None else jnp.where(lane >= spot, value, weight)
                weights_ref[(tile * STEPS + s) * 2 + part] = weight
    for copy in copies:
        copy.wait()


def y_records(waves, table_ref, monitor_ref, weights_ref, *refs):
    *messages, out_ref = refs
    blocks = len(messages)
    columns = messages[0].shape[1]
    targets, height, _ = out_ref.shape
    kept = OY // targets
    out_tiles = -(-waves * RECORDS * kept // OY)
    rows = height // (2 * out_tiles)
    me = lax.axis_index("gy")
    span = DEEP * SEAM
    per_tile = columns // span
    base = STEPS * RECORDS * rows
    lane = iota((2 * rows, columns), 1)
    column = lane % SEAM

    def edges_of(block, tile):
        return messages[block][pl.ds(base + tile * 2 * rows, 2 * rows), :]

    total = None
    for tile in range(-(-blocks // per_tile)):
        seams = range(tile * per_tile, min(blocks, (tile + 1) * per_tile))
        kinds = []
        for part in range(message_tiles(columns)):
            mixed = []
            for seam in list(seams) + [seams[0]] * (per_tile - len(seams)):
                here, after = edges_of(seam, part), edges_of((seam + 1) % blocks, part)
                mixed.append(jnp.where(column < EDGE, here, after))
            kinds += blocks_transposed(mixed)
        walk = seam_leapfrog(kinds[:KINDS], DEEP)
        record = []
        for s in range(STEPS):
            record += [value[:rows] for value in walk.records(s + 1, 0)]
        values = jnp.concatenate(record, axis=0)[:, : len(seams) * span]
        owners = [lax.rem(me + seam, blocks) for seam in seams]
        places = [pl.ds(pl.multiple_of(owner * span, span), span) for owner in owners]
        tables = [
            jnp.concatenate([table_ref[part, place, :] for place in places], axis=0)
            for part in range(2)
        ]
        total = split_dot(values, tables, total)
    for block in range(blocks):
        owner = lax.rem(me + block, blocks)
        place = pl.ds(pl.multiple_of(blocks * span + owner * columns, span), columns)
        values = messages[block][pl.ds(0, base), :]
        total = split_dot(values, [table_ref[part, place, :] for part in range(2)], total)
    lane = iota((rows, OY), 1)
    per_wave = RECORDS * kept
    per_tile = OY // per_wave
    packed_parts = [
        packed_orders(total[:, part * OY : (part + 1) * OY], STEPS * RECORDS, kept)
        for part in range(2)
    ]
    for target in range(targets):
        sides = []
        for part in range(2):
            (packed,) = packed_parts[part][target]
            steps = []
            for s in range(STEPS):
                spread = None
                for i in range(min(per_tile, waves)):
                    here = rolled(packed, i * per_wave - s * per_wave, 1)
                    spread = here if i == 0 else jnp.where(lane >= i * per_wave, here, spread)
                steps.append(spread)
            sides.append(steps)
        for tile in range(out_tiles):
            for part in range(2):
                place = pl.ds((tile * 2 + part) * rows, rows)
                value = monitor_ref[target, place, :]
                for s in range(STEPS):
                    first = (tile * STEPS + s) * 2
                    real, imag = weights_ref[first], weights_ref[first + 1]
                    if part == 0:
                        value = value + (real * sides[0][s] - imag * sides[1][s])
                    else:
                        value = value + (imag * sides[0][s] + real * sides[1][s])
                out_ref[order_of(targets).index(target), place, :] = value


def x_orders(kept, values_ref, table_ref, out_ref):
    sources, height, lanes = values_ref.shape
    waves, _, records, _, _ = out_ref.shape
    depth = table_ref.shape[0]
    rows = depth // sources
    per_tile = lanes // kept
    for tile in range(height // rows):
        values = jnp.concatenate(
            [values_ref[source, pl.ds(tile * rows, rows), :] for source in range(sources)], axis=0
        )
        result = exact_dot(values, table_ref[...], ((0,), (0,)))
        for place in range(per_tile):
            wave, record = divmod(tile * per_tile + place, records)
            if wave < waves:
                here = result[place * kept : (place + 1) * kept]
                out_ref[wave, 0, record] = here[:, :OX]
                out_ref[wave, 1, record] = here[:, OX:]


def local_updates(
    perm_ref,
    wave_ref,
    coef_ref,
    e_ref,
    h_ref,
    m_ref,
    before_ref,
    after_ref,
    edges_ref,
    message_before_ref,
    message_after_ref,
    slab_ref,
    monitor_ref,
    e_any,
    h_any,
    slab_out_any,
    monitor_out_any,
    e_out,
    h_out,
    slab_out,
    monitor_out,
    done,
):
    layers, rows, columns = m_ref.shape
    rates = rates_of(perm_ref, perm_ref.shape[0], (rows, columns))
    wide = widened_planes(own_planes(e_ref, h_ref, m_ref, rates), before_ref, after_ref)
    walk = Leapfrog(wide, layers=layers)
    left = iota((2 * rows, layers * SEAM), 1) % SEAM < EDGE
    outer = message_before_ref.shape[0] - -(-KINDS // OUTER) * 2 * rows
    before, after = [], []
    for kind in range(KINDS):
        mine = edges_ref[kind]
        place = pl.ds(outer + kind // OUTER * 2 * rows, 2 * rows)
        spot = kind % OUTER * STEPS
        from_before = rolled(message_before_ref[place, :], STEPS - spot, 1)
        from_after = rolled(message_after_ref[place, :], EDGE - spot, 1)
        before.append(jnp.where(left, from_before, mine))
        after.append(jnp.where(left, mine, from_after))
    before = seam_leapfrog(before, layers)
    after = seam_leapfrog(after, layers)
    column = iota((rows, columns), 1)
    inner = (column >= STEPS) & (column < columns - STEPS)
    joined = {}

    def mended(s, z, kind):
        if (s, kind) not in joined:
            ends = [(side.e(s, 0) + side.h(s, 0))[kind][:rows] for side in (after, before)]
            joined[s, kind] = jnp.where(left[:rows], ends[0], ends[1])
        value = (walk.e(s, z) + walk.h(s, z))[kind][:rows]
        return jnp.where(inner, value, rolled(joined[s, kind], -(z * SEAM + EDGE), 1))

    middle = layers // 2
    slab_records = [[None] * 2 for _ in range(STEPS)]
    records = [[None] * RECORDS for _ in range(STEPS)]
    for z in range(layers):
        for kind in range(6):
            value = mended(STEPS, z, kind)
            if kind < 3:
                e_out[kind, z] = value
            else:
                h_out[kind - 3, z] = value
        for s in range(STEPS):
            if z == middle:
                slab_records[s] = [mended(s + 1, z, kind) for kind in (0, 1)]
            if z == layers - 1:
                records[s] = [mended(s + 1, z, kind) for kind in (0, 1, 3, 4)]
    sent = [
        pltpu.make_async_copy(e_out, e_any, done.at[0]),
        pltpu.make_async_copy(h_out, h_any, done.at[1]),
    ]
    for copy in sent:
        copy.start()
    frequencies = slab_ref.shape[1] // 2

    def one_frequency(f, carry):
        coef = waves_of(coef_ref, f)
        for c in range(2):
            for part in range(2):
                value = slab_ref[c, part * frequencies + f]
                for s in range(STEPS):
                    value = value + coef(s, 0, part) * slab_records[s][c]
                slab_out[c, part * frequencies + f] = value
        return carry

    lax.fori_loop(0, frequencies, one_frequency, 0, unroll=4)
    sent.append(pltpu.make_async_copy(slab_out, slab_out_any, done.at[2]))
    sent[-1].start()
    for w in range(monitor_ref.shape[0]):
        coef = waves_of(coef_ref, wave_ref[w])
        for part in range(2):
            for c in range(RECORDS):
                value = monitor_ref[w, part, c]
                for s in range(STEPS):
                    value = value + coef(s, c // 2, part) * records[s][c]
                monitor_out[w, part, c] = value
    sent.append(pltpu.make_async_copy(monitor_out, monitor_out_any, done.at[3]))
    sent[-1].start()
    for copy in sent:
        copy.wait()


def wave_coefficients(freq_count):
    omegas = OMEGA_LOW + (OMEGA_HIGH - OMEGA_LOW) * np.arange(freq_count) / (freq_count - 1)
    times = TIME_STEP * (np.arange(1, STEPS + 1)[:, None] - np.array([0.0, 0.5])[None, :])
    angles = omegas[:, None, None] * times[None]
    table = np.stack([TIME_STEP * np.cos(angles), -TIME_STEP * np.sin(angles)], axis=-1)
    return table.reshape(-1).astype(np.float32)


def angles_of(length, kept):
    wanted = (np.arange(kept) - kept // 2) % length
    return 2.0 * math.pi / length * (np.arange(length)[:, None] * wanted[None, :] % length)


def y_table(length):
    angles = angles_of(length, OY)
    return np.concatenate([np.cos(angles), np.sin(angles)], axis=1).astype(np.float32)


def split_table(table):
    table = table.astype(np.float32)
    coarse = table.astype(ml_dtypes.bfloat16)
    fine = (table - coarse.astype(np.float32)).astype(ml_dtypes.bfloat16)
    return jnp.asarray(np.stack([coarse, fine]))


def record_table(length, blocks):
    angles = angles_of(length, OY)
    table = np.concatenate([np.cos(angles), -np.sin(angles)], axis=1)
    columns = length // blocks
    seams = np.zeros((blocks, DEEP, SEAM, 2 * OY))
    for block in range(blocks):
        for column in range(-STEPS, STEPS):
            row = ((block + 1) * columns + column) % length
            seams[block, DEEP - 1, EDGE + column] = table[row]
    inner = table.copy()
    place = np.arange(length) % columns
    inner[(place < STEPS) | (place >= columns - STEPS)] = 0.0
    return split_table(np.concatenate([seams.reshape(-1, 2 * OY), inner]))


def order_of(blocks):
    return list(reversed(range(blocks)))


def x_table(length, blocks, scaling):
    angles = angles_of(length, OX).reshape(blocks, length // blocks, OX)[order_of(blocks)]
    real = np.concatenate([np.cos(angles), -np.sin(angles)], axis=2)
    imag = np.concatenate([np.sin(angles), np.cos(angles)], axis=2)
    table = np.stack([real, imag], axis=1) * scaling
    return table.reshape(2 * length, 2 * OX).astype(np.float32)


def call(kernel, in_specs, shapes, *operands, name, flops=0, moved=0, **more):
    kind = jax.ShapeDtypeStruct
    out = [kind(shape, jnp.float32) for shape in shapes]
    return pl.pallas_call(
        kernel,
        out_shape=out,
        in_specs=in_specs,
        out_specs=more.pop("out_specs", [VMEM] * len(out)),
        compiler_params=PARAMS,
        cost_estimate=pl.CostEstimate(flops=flops, bytes_accessed=moved, transcendentals=0),
        name=name,
        **more,
    )(*operands)


def per_device(
    electric, magnetic, material, permittivity, slab_spectra, monitor_spectra, wave_index
):
    layers, rows, columns = material.shape
    x_blocks, y_blocks = lax.axis_size("gx"), lax.axis_size("gy")
    waves = monitor_spectra.shape[0]
    group_waves = waves // y_blocks
    fields = (electric, magnetic, material)
    groups = layers * STEPS // rows

    faces = (KINDS, groups, rows, columns)
    block = (group_waves,) + monitor_spectra.shape[1:]
    late = [1]
    early = [distance for distance in range(y_blocks) if distance not in late]
    forth, back, *blocks = call(
        functools.partial(pack_faces, early),
        [HBM] * 5,
        [faces, faces] + [block] * len(early),
        *[in_hbm(array) for array in (permittivity, *fields, monitor_spectra)],
        name="pack_faces",
        flops=10**5,
        moved=10**6,
        scratch_shapes=[
            pltpu.SMEM(permittivity.shape, jnp.float32),
            pltpu.VMEM(electric.shape, jnp.float32),
            pltpu.VMEM(magnetic.shape, jnp.float32),
            pltpu.VMEM(material.shape, jnp.int32),
            pltpu.SemaphoreType.DMA((4,)),
            pltpu.SemaphoreType.DMA((len(early),)),
        ],
    )
    before = passed_along(forth, "gx", 1)
    after = passed_along(back, "gx", -1)
    spectra = {
        distance: passed_along(block, "gy", -distance) if distance else block
        for distance, block in zip(early, blocks)
    }

    far_height = (STEPS * RECORDS + message_tiles(columns) * 2) * rows
    near_height = far_height + -(-KINDS // OUTER) * 2 * rows
    forth, back, far, edges, *blocks = call(
        functools.partial(monitor_message, late),
        [SMEM] + [VMEM] * 5 + [HBM],
        [
            (near_height, columns),
            (near_height, columns),
            (far_height, columns),
            (KINDS, 2 * rows, layers * SEAM),
        ]
        + [block] * len(late),
        permittivity,
        *fields,
        before,
        after,
        in_hbm(monitor_spectra),
        scratch_shapes=[pltpu.SemaphoreType.DMA((len(late),))],
        name="monitor_message",
        flops=10**5,
        moved=10**6,
    )
    message_after = passed_along(back, "gy", -1)
    message_before = passed_along(forth, "gy", 1)
    for distance, block in zip(late, blocks):
        spectra[distance] = passed_along(block, "gy", -distance)
    messages = [far, message_after]
    for distance in range(2, y_blocks - 1):
        messages.append(passed_along(far, "gy", -distance))
    messages = (messages + [message_before])[:y_blocks]

    coefs = jnp.asarray(wave_coefficients(slab_spectra.shape[1] // 2))
    length_x, length_y = rows * x_blocks, columns * y_blocks
    kept = OY // x_blocks
    out_tiles = -(-group_waves * RECORDS * kept // OY)
    sums_y = jnp.asarray(y_table(length_y))
    monitor_y, weights, slab_here, monitor_here = call(
        y_monitor,
        [SMEM] * 2 + [VMEM] + [HBM] * 2 + [VMEM] * y_blocks,
        [
            (x_blocks, out_tiles * 2 * rows, OY),
            (out_tiles * STEPS * 2, rows, OY),
            slab_spectra.shape,
            monitor_spectra.shape,
        ],
        wave_index,
        coefs,
        sums_y,
        in_hbm(slab_spectra),
        in_hbm(monitor_spectra),
        *[spectra[distance] for distance in range(y_blocks)],
        name="y_monitor",
        scratch_shapes=[pltpu.SemaphoreType.DMA((2,))],
        flops=10**8,
        moved=2 * 10**6,
    )
    (spectrum_y,) = call(
        functools.partial(y_records, group_waves),
        [VMEM] * (3 + y_blocks),
        [monitor_y.shape],
        record_table(length_y, y_blocks),
        monitor_y,
        weights,
        *messages,
        name="y_records",
        flops=10**8,
        moved=2 * 10**6,
    )
    members = [
        [x * y_blocks + y for x in order_of(x_blocks)] for y in range(y_blocks)
    ]
    swapped = lax.all_to_all(
        spectrum_y, ("gx", "gy"), split_axis=0, concat_axis=0, axis_index_groups=members, tiled=True
    )

    electric_next, magnetic_next, slab_next, monitor_next = call(
        local_updates,
        [SMEM] * 3 + [VMEM] * 10,
        [electric.shape, magnetic.shape, slab_spectra.shape, monitor_spectra.shape],
        permittivity,
        wave_index,
        coefs,
        *fields,
        before,
        after,
        edges,
        message_before,
        message_after,
        slab_here,
        monitor_here,
        name="local_updates",
        scratch_shapes=[
            pltpu.VMEM(electric.shape, jnp.float32),
            pltpu.VMEM(magnetic.shape, jnp.float32),
            pltpu.VMEM(slab_spectra.shape, jnp.float32),
            pltpu.VMEM(monitor_spectra.shape, jnp.float32),
            pltpu.SemaphoreType.DMA((4,)),
        ],
        out_specs=[HBM] * 4,
        flops=10**7,
        moved=6 * 10**6,
    )

    scaling = 1.0 / math.sqrt(length_x * length_y)
    (orders,) = call(
        functools.partial(x_orders, kept),
        [VMEM] * 2,
        [(group_waves, 2, RECORDS, kept, OX)],
        swapped,
        jnp.asarray(x_table(length_x, x_blocks, scaling)),
        name="x_orders",
        flops=10**7,
        moved=5 * 10**5,
    )
    return (electric_next, magnetic_next, slab_next, monitor_next, orders)


def solution(mesh):
    in_specs = (
        P(None, None, "gx", "gy"),
        P(None, None, "gx", "gy"),
        P(None, "gx", "gy"),
        P(),
        P(None, None, "gx", "gy"),
        P(None, None, None, "gx", "gy"),
        P(),
    )
    out_specs = (
        P(None, None, "gx", "gy"),
        P(None, None, "gx", "gy"),
        P(None, None, "gx", "gy"),
        P(None, None, None, "gx", "gy"),
        P("gy", None, None, "gx", None),
    )
    return jax.shard_map(
        per_device, mesh=mesh, in_specs=in_specs, out_specs=out_specs, check_vma=False
    )
```

```python
import functools
import math

import jax
import jax.numpy as jnp
import ml_dtypes
import numpy as np
from jax import lax
from jax.experimental import pallas as pl
from jax.experimental.pallas import tpu as pltpu
from jax.sharding import PartitionSpec as P

OY = 128
OX = 64

TIME_STEP = 0.5
OMEGA_LOW = 0.15
OMEGA_HIGH = 0.8

STEPS = 2
EDGE = 2 * STEPS
SEAM = 2 * EDGE
DEEP = 4
OUTER = SEAM // STEPS
KINDS = 7
RECORDS = 4

VMEM = pl.BlockSpec(memory_space=pltpu.VMEM)
HBM = pl.BlockSpec(memory_space=pltpu.HBM)
ANY = pl.BlockSpec(memory_space=pl.ANY)
SMEM = pl.BlockSpec(memory_space=pltpu.SMEM)
PARAMS = pltpu.CompilerParams(vmem_limit_bytes=48 * 1024 * 1024)


def in_hbm(array):
    return pltpu.with_memory_space_constraint(array, pltpu.HBM)


def passed_along(block, axis, distance):
    devices = range(lax.axis_size(axis))
    route = [((i - distance) % len(devices), i) for i in devices]
    return lax.ppermute(block, axis, route)


def rolled(values, shift, axis):
    shift %= values.shape[axis]
    return pltpu.roll(values, shift, axis) if shift else values


def iota(shape, axis):
    return lax.broadcasted_iota(jnp.int32, shape, axis)


def rates_of(permittivity, classes, shape):
    return [TIME_STEP / jnp.full(shape, permittivity[k], jnp.float32) for k in range(classes)]


def rate_at(material, rates):
    rate = rates[-1]
    for k in range(len(rates) - 2, -1, -1):
        rate = jnp.where(material == k, rates[k], rate)
    return rate


class Leapfrog:
    def __init__(self, start, layers=None, above=None, below=None):
        self.start = start
        self.layers = layers
        self.above = above
        self.below = below
        self.known = {}

    def first(self, z):
        if ("0", z) not in self.known:
            self.known["0", z] = self.start(z)
        return self.known["0", z]

    def e(self, s, z):
        if s == 0:
            return self.first(z)[0:3]
        if ("e", s, z) not in self.known:
            ex, ey, ez = self.e(s - 1, z)
            hx, hy, hz = self.h(s, z)
            if self.layers is None:
                down_x, down_y = self.below(hx), self.below(hy)
            else:
                down_x, down_y = self.h(s, z - 1)[:2] if z else (0.0, 0.0)
            rate = self.first(z)[6]
            self.known["e", s, z] = (
                ex + rate * ((hz - rolled(hz, 1, 1)) - (hy - down_y)),
                ey + rate * ((hx - down_x) - (hz - rolled(hz, 1, 0))),
                ez + rate * ((hy - rolled(hy, 1, 0)) - (hx - rolled(hx, 1, 1))),
            )
        return self.known["e", s, z]

    def h(self, s, z):
        if s == 0:
            return self.first(z)[3:6]
        if ("h", s, z) not in self.known:
            ex, ey, ez = self.e(s - 1, z)
            hx, hy, hz = self.h(s - 1, z)
            if self.layers is None:
                up_x, up_y = self.above(ex), self.above(ey)
            else:
                up_x, up_y = self.e(s - 1, z + 1)[:2] if z + 1 < self.layers else (0.0, 0.0)
            self.known["h", s, z] = (
                hx - TIME_STEP * ((rolled(ez, -1, 1) - ez) - (up_y - ey)),
                hy - TIME_STEP * ((up_x - ex) - (rolled(ez, -1, 0) - ez)),
                hz - TIME_STEP * ((rolled(ey, -1, 0) - ey) - (rolled(ex, -1, 1) - ex)),
            )
        return self.known["h", s, z]

    def records(self, s, z):
        return self.e(s, z)[:2] + self.h(s, z)[:2]


def seam_leapfrog(tiles, layers):
    layer = iota(tiles[0].shape, 1) // SEAM % layers
    return Leapfrog(
        lambda z: tiles,
        above=lambda f: jnp.where(layer < layers - 1, rolled(f, -SEAM, 1), 0.0),
        below=lambda f: jnp.where(layer > 0, rolled(f, SEAM, 1), 0.0),
    )


def own_planes(e_ref, h_ref, m_ref, rates):
    def at(z):
        rate = rate_at(m_ref[z], rates)
        return [e_ref[c, z] for c in range(3)] + [h_ref[c, z] for c in range(3)] + [rate]

    return at


def widened_planes(own, same_ref, cross_ref):
    even = lax.rem(lax.axis_index("gx"), 2) == 0

    def at(z):
        planes = own(z)
        rows = planes[0].shape[0]
        group, place = divmod(z, rows // STEPS)
        row = iota(planes[0].shape, 0)
        wide = []
        for kind in range(KINDS):
            same, cross = same_ref[kind, group], cross_ref[kind, group]
            after = rolled(jnp.where(even, same, cross), -STEPS * place, 0)
            before = rolled(jnp.where(even, cross, same), rows - STEPS - STEPS * place, 0)
            halo = jnp.where(row < STEPS, after, before)
            wide.append(jnp.concatenate([planes[kind], halo], axis=0))
        return wide

    return at


def block_copy(distance, spectra_any, block_ref, semaphore):
    waves = block_ref.shape[0]
    blocks = spectra_any.shape[0] // waves
    owner = lax.rem(lax.axis_index("gy") + blocks - distance, blocks)
    source = spectra_any.at[pl.ds(owner * waves, waves)]
    return pltpu.make_async_copy(source, block_ref, semaphore)


def pack_faces(
    distances,
    perm_any,
    e_any,
    h_any,
    m_any,
    spectra_any,
    same_ref,
    cross_ref,
    *refs,
):
    even = lax.rem(lax.axis_index("gx"), 2) == 0
    *block_refs, perm_ref, e_ref, h_ref, m_ref, ready, sent = refs
    sources, targets = (e_any, h_any, m_any, perm_any), (e_ref, h_ref, m_ref, perm_ref)
    copies = [
        pltpu.make_async_copy(source, target, ready.at[i])
        for i, (source, target) in enumerate(zip(sources, targets))
    ]
    for i, (distance, block_ref) in enumerate(zip(distances, block_refs)):
        copies.append(block_copy(distance, spectra_any, block_ref, sent.at[i]))
    for copy in copies:
        copy.start()
    for copy in copies[:4]:
        copy.wait()
    layers, rows, columns = m_ref.shape
    rates = rates_of(perm_ref, perm_ref.shape[0], (rows, columns))
    own = own_planes(e_ref, h_ref, m_ref, rates)
    row = iota((rows, columns), 0)
    per_group = rows // STEPS
    for group in range(layers // per_group):
        planes = [own(group * per_group + place) for place in range(per_group)]
        for kind in range(KINDS):
            forth = rolled(planes[0][kind], STEPS - rows, 0)
            back = planes[0][kind]
            for place in range(1, per_group):
                spot = STEPS * place
                here = planes[place][kind]
                forth = jnp.where(row >= spot, rolled(here, spot + STEPS - rows, 0), forth)
                back = jnp.where(row >= spot, rolled(here, spot, 0), back)
            same_ref[kind, group] = jnp.where(even, forth, back)
            cross_ref[kind, group] = jnp.where(even, back, forth)
    for copy in copies[4:]:
        copy.wait()


def blocks_transposed(tiles):
    tiles = list(tiles)
    count = len(tiles)
    width = tiles[0].shape[1] // count
    block = iota(tiles[0].shape, 1) // width
    bit = 1
    while bit < count:
        low = (block & bit) == 0
        for i in range(count):
            if not i & bit:
                first, second = tiles[i], tiles[i + bit]
                tiles[i] = jnp.where(low, first, rolled(second, bit * width, 1))
                tiles[i + bit] = jnp.where(low, rolled(first, -bit * width, 1), second)
        bit *= 2
    return tiles


def packed_edges(planes, layers, spot):
    tile = None
    for z in range(layers):
        here = rolled(planes[z], spot + z * SEAM + EDGE, 1)
        if tile is None:
            tile = here
        else:
            tile = jnp.where(iota(tile.shape, 1) >= spot + z * SEAM, here, tile)
    return tile


def squeezed(first, second):
    rows = first.shape[0] // 2
    row = iota((rows, first.shape[1]), 0)
    ends = (row < STEPS) | (row >= rows - STEPS)
    second_halo = second[rows:]
    moved = jnp.where(
        row < 2 * STEPS, rolled(second_halo, STEPS, 0), rolled(second_halo, -STEPS, 0)
    )
    return first[:rows], second[:rows], jnp.where(ends, first[rows:], moved)


def stretched(first, second, halo):
    rows = first.shape[0]
    row = iota(halo.shape, 0)
    moved = jnp.where(row < 2 * STEPS, rolled(halo, -STEPS, 0), rolled(halo, STEPS, 0))
    return jnp.concatenate([first, halo], axis=0), jnp.concatenate([second, moved], axis=0)


def pair_of_tiles(ref, pair, rows):
    base = (STEPS * RECORDS + 3 * pair) * rows
    return stretched(*[ref[pl.ds(base + i * rows, rows), :] for i in range(3)])


def monitor_message(
    perm_ref,
    e_ref,
    h_ref,
    m_ref,
    same_ref,
    cross_ref,
    block_any,
    forth_ref,
    back_ref,
    far_ref,
    edges_ref,
    block_out,
):
    layers, rows, columns = m_ref.shape
    rates = rates_of(perm_ref, perm_ref.shape[0], (rows, columns))
    wide = widened_planes(own_planes(e_ref, h_ref, m_ref, rates), same_ref, cross_ref)
    low = layers - DEEP
    walk = Leapfrog(lambda z: wide(low + z), layers=DEEP)
    for s in range(STEPS):
        for c, record in enumerate(walk.records(s + 1, DEEP - 1)):
            place = pl.ds((s * RECORDS + c) * rows, rows)
            for ref in (forth_ref, back_ref, far_ref):
                ref[place, :] = record[:rows]
    planes = [wide(z) for z in range(low)] + [walk.first(z) for z in range(DEEP)]
    span = DEEP * SEAM
    per_tile = columns // span
    tops, lasts, firsts = ([None, None] for _ in range(3))
    for kind in range(KINDS):
        edges = packed_edges([planes[z][kind] for z in range(layers)], layers, 0)
        edges_ref[kind] = edges
        lane = iota(edges.shape, 1)
        tile, spot = divmod(kind, per_tile)
        here = rolled(edges, spot * span - low * SEAM, 1)
        tops[tile] = jnp.where(lane >= spot * span, here, tops[tile]) if spot else here
        tile, spot = divmod(kind, OUTER)
        for tiles, shift in ((lasts, STEPS), (firsts, EDGE)):
            here = rolled(edges, spot * STEPS - shift, 1)
            tiles[tile] = jnp.where(lane % SEAM >= spot * STEPS, here, tiles[tile]) if spot else here
    base = STEPS * RECORDS * rows
    for i, part in enumerate(squeezed(*tops)):
        for ref in (forth_ref, back_ref, far_ref):
            ref[pl.ds(base + i * rows, rows), :] = part
    for ref, tiles in ((forth_ref, lasts), (back_ref, firsts)):
        for i, part in enumerate(squeezed(*tiles)):
            ref[pl.ds(base + (3 + i) * rows, rows), :] = part


def waves_of(coef_ref, wave):
    base = wave * (STEPS * 4)
    return lambda s, half, part: coef_ref[base + (s * 2 + half) * 2 + part]


def exact_dot(left, right, contracted):
    return lax.dot_general(
        left,
        right,
        (contracted, ((), ())),
        precision=lax.Precision.HIGHEST,
        preferred_element_type=jnp.float32,
    )


def split_dot(values, tables, total):
    coarse = values.astype(jnp.bfloat16)
    fine = (values - coarse.astype(jnp.float32)).astype(jnp.bfloat16)
    for left, right in ((coarse, tables[0]), (fine, tables[0]), (coarse, tables[1])):
        product = jnp.dot(left, right, preferred_element_type=jnp.float32)
        total = product if total is None else total + product
    return total


def packed_orders(values, planes, kept):
    rows = values.shape[0] // planes
    parts = [values[plane * rows : (plane + 1) * rows] for plane in range(planes)]
    targets = per_tile = OY // kept
    if planes % per_tile == 0 and not targets & (targets - 1):
        groups = [parts[i : i + per_tile] for i in range(0, planes, per_tile)]
        return list(zip(*[blocks_transposed(group) for group in groups]))
    lane = iota((rows, OY), 1)
    packed = []
    for target in range(targets):
        tiles = []
        for first in range(0, planes, per_tile):
            tile = None
            for plane in range(first, min(planes, first + per_tile)):
                spot = (plane - first) * kept
                here = rolled(parts[plane], spot - target * kept, 1)
                tile = here if tile is None else jnp.where(lane >= spot, here, tile)
            tiles.append(tile)
        packed.append(tiles)
    return packed


def fetch(after_this, slab_any, monitor_any, slab_ref, monitor_ref, ready):
    copies = [
        pltpu.make_async_copy(slab_any, slab_ref, ready.at[0]),
        pltpu.make_async_copy(monitor_any, monitor_ref, ready.at[1]),
    ]
    for copy in copies:
        copy.start()
    for copy in copies:
        copy.wait()


def y_monitor(wave_ref, coef_ref, table_ref, after_this, *refs):
    *spectra, out_ref, weights_ref = refs
    blocks = len(spectra)
    waves, _, records, rows, columns = spectra[0].shape
    me = lax.axis_index("gy")
    total = None
    for block in range(blocks):
        owner = lax.rem(me + block, blocks)
        place = pl.ds(pl.multiple_of(owner * columns, columns), columns)
        parts = []
        for part in range(2):
            for w in range(waves):
                parts += [spectra[block][w, part, c] for c in range(records)]
        tables = [table_ref[i, place, :] for i in range(2)]
        total = split_dot(jnp.concatenate(parts, axis=0), tables, total)
    half = waves * records * rows
    real = total[:half, :OY] + total[half:, OY:]
    imag = total[half:, :OY] - total[:half, OY:]
    targets = out_ref.shape[0]
    for part, values in enumerate((real, imag)):
        packed = packed_orders(values, waves * records, OY // targets)
        for target in range(targets):
            for i, tile in enumerate(packed[target]):
                out_ref[target, pl.ds((i * 2 + part) * rows, rows), :] = tile
    kept = OY // targets
    lane = iota((rows, OY), 1)
    per_wave = RECORDS * kept
    per_tile = OY // per_wave
    for tile in range(weights_ref.shape[0] // (2 * STEPS)):
        some = range(tile * per_tile, min(waves, (tile + 1) * per_tile))
        coefs = [waves_of(coef_ref, wave_ref[me * waves + w]) for w in some]
        for s in range(STEPS):
            for part in range(2):
                weight = None
                for i, coef in enumerate(coefs):
                    for half in range(2):
                        value = jnp.full((rows, OY), coef(s, half, part), jnp.float32)
                        spot = i * per_wave + half * (per_wave // 2)
                        weight = value if weight is None else jnp.where(lane >= spot, value, weight)
                weights_ref[(tile * STEPS + s) * 2 + part] = weight


def y_records(waves, table_ref, monitor_ref, weights_ref, *refs):
    *messages, out_ref = refs
    blocks = len(messages)
    columns = messages[0].shape[1]
    targets, height, _ = out_ref.shape
    kept = OY // targets
    out_tiles = -(-waves * RECORDS * kept // OY)
    rows = height // (2 * out_tiles)
    me = lax.axis_index("gy")
    span = DEEP * SEAM
    per_tile = columns // span
    base = STEPS * RECORDS * rows
    column = iota((2 * rows, columns), 1) % SEAM
    edges = [pair_of_tiles(message, 0, rows) for message in messages]

    total = None
    for tile in range(-(-blocks // per_tile)):
        seams = range(tile * per_tile, min(blocks, (tile + 1) * per_tile))
        kinds = []
        for part in range(2):
            mixed = []
            for seam in list(seams) + [seams[0]] * (per_tile - len(seams)):
                here, after = edges[seam][part], edges[(seam + 1) % blocks][part]
                mixed.append(jnp.where(column < EDGE, here, after))
            kinds += blocks_transposed(mixed)
        walk = seam_leapfrog(kinds[:KINDS], DEEP)
        record = []
        for s in range(STEPS):
            record += [value[:rows] for value in walk.records(s + 1, 0)]
        values = jnp.concatenate(record, axis=0)[:, : len(seams) * span]
        owners = [lax.rem(me + seam, blocks) for seam in seams]
        places = [pl.ds(pl.multiple_of(owner * span, span), span) for owner in owners]
        tables = [
            jnp.concatenate([table_ref[part, place, :] for place in places], axis=0)
            for part in range(2)
        ]
        total = split_dot(values, tables, total)
    for block in range(blocks):
        owner = lax.rem(me + block, blocks)
        place = pl.ds(pl.multiple_of(blocks * span + owner * columns, span), columns)
        values = messages[block][pl.ds(0, base), :]
        total = split_dot(values, [table_ref[part, place, :] for part in range(2)], total)
    lane = iota((rows, OY), 1)
    per_wave = RECORDS * kept
    per_tile = OY // per_wave
    packed_parts = [
        packed_orders(total[:, part * OY : (part + 1) * OY], STEPS * RECORDS, kept)
        for part in range(2)
    ]
    for target in range(targets):
        sides = []
        for part in range(2):
            (packed,) = packed_parts[part][target]
            steps = []
            for s in range(STEPS):
                spread = None
                for i in range(min(per_tile, waves)):
                    here = rolled(packed, i * per_wave - s * per_wave, 1)
                    spread = here if i == 0 else jnp.where(lane >= i * per_wave, here, spread)
                steps.append(spread)
            sides.append(steps)
        for tile in range(out_tiles):
            for part in range(2):
                place = pl.ds((tile * 2 + part) * rows, rows)
                value = monitor_ref[target, place, :]
                for s in range(STEPS):
                    first = (tile * STEPS + s) * 2
                    real, imag = weights_ref[first], weights_ref[first + 1]
                    if part == 0:
                        value = value + (real * sides[0][s] - imag * sides[1][s])
                    else:
                        value = value + (imag * sides[0][s] + real * sides[1][s])
                out_ref[order_of(targets).index(target), place, :] = value


def x_orders(kept, values_ref, table_ref, out_ref):
    sources, height, lanes = values_ref.shape
    waves, _, records, _, _ = out_ref.shape
    depth = table_ref.shape[0]
    rows = depth // sources
    per_tile = lanes // kept
    for tile in range(height // rows):
        values = jnp.concatenate(
            [values_ref[source, pl.ds(tile * rows, rows), :] for source in range(sources)], axis=0
        )
        result = exact_dot(values, table_ref[...], ((0,), (0,)))
        for place in range(per_tile):
            wave, record = divmod(tile * per_tile + place, records)
            if wave < waves:
                here = result[place * kept : (place + 1) * kept]
                out_ref[wave, 0, record] = here[:, :OX]
                out_ref[wave, 1, record] = here[:, OX:]


def local_updates(
    perm_ref,
    wave_ref,
    coef_ref,
    e_ref,
    h_ref,
    m_ref,
    same_ref,
    cross_ref,
    edges_ref,
    message_before_ref,
    message_after_ref,
    slab_ref,
    monitor_ref,
    e_any,
    h_any,
    slab_out_any,
    monitor_out_any,
    e_out,
    h_out,
    slab_out,
    monitor_out,
    done,
):
    layers, rows, columns = m_ref.shape
    rates = rates_of(perm_ref, perm_ref.shape[0], (rows, columns))
    wide = widened_planes(own_planes(e_ref, h_ref, m_ref, rates), same_ref, cross_ref)
    walk = Leapfrog(wide, layers=layers)
    left = iota((2 * rows, layers * SEAM), 1) % SEAM < EDGE
    last = pair_of_tiles(message_before_ref, 1, rows)
    first = pair_of_tiles(message_after_ref, 1, rows)
    before, after = [], []
    for kind in range(KINDS):
        mine = edges_ref[kind]
        tile, spot = divmod(kind, OUTER)
        from_before = rolled(last[tile], STEPS - spot * STEPS, 1)
        from_after = rolled(first[tile], EDGE - spot * STEPS, 1)
        before.append(jnp.where(left, from_before, mine))
        after.append(jnp.where(left, mine, from_after))
    before = seam_leapfrog(before, layers)
    after = seam_leapfrog(after, layers)
    column = iota((rows, columns), 1)
    inner = (column >= STEPS) & (column < columns - STEPS)
    joined = {}

    def mended(s, z, kind):
        if (s, kind) not in joined:
            ends = [(side.e(s, 0) + side.h(s, 0))[kind][:rows] for side in (after, before)]
            joined[s, kind] = jnp.where(left[:rows], ends[0], ends[1])
        value = (walk.e(s, z) + walk.h(s, z))[kind][:rows]
        return jnp.where(inner, value, rolled(joined[s, kind], -(z * SEAM + EDGE), 1))

    middle = layers // 2
    slab_records = [[None] * 2 for _ in range(STEPS)]
    records = [[None] * RECORDS for _ in range(STEPS)]
    for z in range(layers):
        for kind in range(6):
            value = mended(STEPS, z, kind)
            if kind < 3:
                e_out[kind, z] = value
            else:
                h_out[kind - 3, z] = value
        for s in range(STEPS):
            if z == middle:
                slab_records[s] = [mended(s + 1, z, kind) for kind in (0, 1)]
            if z == layers - 1:
                records[s] = [mended(s + 1, z, kind) for kind in (0, 1, 3, 4)]
    sent = [
        pltpu.make_async_copy(e_out, e_any, done.at[0]),
        pltpu.make_async_copy(h_out, h_any, done.at[1]),
    ]
    for copy in sent:
        copy.start()
    frequencies = slab_ref.shape[1] // 2

    def one_frequency(f, carry):
        coef = waves_of(coef_ref, f)
        for c in range(2):
            for part in range(2):
                value = slab_ref[c, part * frequencies + f]
                for s in range(STEPS):
                    value = value + coef(s, 0, part) * slab_records[s][c]
                slab_out[c, part * frequencies + f] = value
        return carry

    lax.fori_loop(0, frequencies, one_frequency, 0, unroll=4)
    sent.append(pltpu.make_async_copy(slab_out, slab_out_any, done.at[2]))
    sent[-1].start()
    for w in range(monitor_ref.shape[0]):
        coef = waves_of(coef_ref, wave_ref[w])
        for part in range(2):
            for c in range(RECORDS):
                value = monitor_ref[w, part, c]
                for s in range(STEPS):
                    value = value + coef(s, c // 2, part) * records[s][c]
                monitor_out[w, part, c] = value
    sent.append(pltpu.make_async_copy(monitor_out, monitor_out_any, done.at[3]))
    sent[-1].start()
    for copy in sent:
        copy.wait()


def wave_coefficients(freq_count):
    omegas = OMEGA_LOW + (OMEGA_HIGH - OMEGA_LOW) * np.arange(freq_count) / (freq_count - 1)
    times = TIME_STEP * (np.arange(1, STEPS + 1)[:, None] - np.array([0.0, 0.5])[None, :])
    angles = omegas[:, None, None] * times[None]
    table = np.stack([TIME_STEP * np.cos(angles), -TIME_STEP * np.sin(angles)], axis=-1)
    return table.reshape(-1).astype(np.float32)


def angles_of(length, kept):
    wanted = (np.arange(kept) - kept // 2) % length
    return 2.0 * math.pi / length * (np.arange(length)[:, None] * wanted[None, :] % length)


def y_table(length):
    angles = angles_of(length, OY)
    return split_table(np.concatenate([np.cos(angles), np.sin(angles)], axis=1))


def split_table(table):
    table = table.astype(np.float32)
    coarse = table.astype(ml_dtypes.bfloat16)
    fine = (table - coarse.astype(np.float32)).astype(ml_dtypes.bfloat16)
    return jnp.asarray(np.stack([coarse, fine]))


def record_table(length, blocks):
    angles = angles_of(length, OY)
    table = np.concatenate([np.cos(angles), -np.sin(angles)], axis=1)
    columns = length // blocks
    seams = np.zeros((blocks, DEEP, SEAM, 2 * OY))
    for block in range(blocks):
        for column in range(-STEPS, STEPS):
            row = ((block + 1) * columns + column) % length
            seams[block, DEEP - 1, EDGE + column] = table[row]
    inner = table.copy()
    place = np.arange(length) % columns
    inner[(place < STEPS) | (place >= columns - STEPS)] = 0.0
    return split_table(np.concatenate([seams.reshape(-1, 2 * OY), inner]))


def order_of(blocks):
    return list(reversed(range(blocks)))


def x_table(length, blocks, scaling):
    angles = angles_of(length, OX).reshape(blocks, length // blocks, OX)[order_of(blocks)]
    real = np.concatenate([np.cos(angles), -np.sin(angles)], axis=2)
    imag = np.concatenate([np.sin(angles), np.cos(angles)], axis=2)
    table = np.stack([real, imag], axis=1) * scaling
    return table.reshape(2 * length, 2 * OX).astype(np.float32)


def call(kernel, in_specs, shapes, *operands, name, flops=0, moved=0, **more):
    kind = jax.ShapeDtypeStruct
    out = [kind(shape, jnp.float32) for shape in shapes]
    return pl.pallas_call(
        kernel,
        out_shape=out,
        in_specs=in_specs,
        out_specs=more.pop("out_specs", [VMEM] * len(out)),
        compiler_params=PARAMS,
        cost_estimate=pl.CostEstimate(flops=flops, bytes_accessed=moved, transcendentals=0),
        name=name,
        **more,
    )(*operands)


def per_device(
    electric, magnetic, material, permittivity, slab_spectra, monitor_spectra, wave_index
):
    layers, rows, columns = material.shape
    x_blocks, y_blocks = lax.axis_size("gx"), lax.axis_size("gy")
    waves = monitor_spectra.shape[0]
    group_waves = waves // y_blocks
    fields = (electric, magnetic, material)
    groups = layers * STEPS // rows

    faces = (KINDS, groups, rows, columns)
    block = (group_waves,) + monitor_spectra.shape[1:]
    late = [1]
    early = [distance for distance in range(y_blocks) if distance not in late]
    same, cross, *blocks = call(
        functools.partial(pack_faces, early + late),
        [HBM] * 5,
        [faces, faces] + [block] * y_blocks,
        *[in_hbm(array) for array in (permittivity, *fields, monitor_spectra)],
        name="pack_faces",
        flops=10**5,
        moved=10**6,
        scratch_shapes=[
            pltpu.SMEM(permittivity.shape, jnp.float32),
            pltpu.VMEM(electric.shape, jnp.float32),
            pltpu.VMEM(magnetic.shape, jnp.float32),
            pltpu.VMEM(material.shape, jnp.int32),
            pltpu.SemaphoreType.DMA((4,)),
            pltpu.SemaphoreType.DMA((y_blocks,)),
        ],
    )
    line = range(x_blocks)
    same = lax.ppermute(same, "gx", [(i, i ^ 1) for i in line])
    cross = lax.ppermute(cross, "gx", [(i, (i + (1 if i % 2 else -1)) % x_blocks) for i in line])
    spectra = {
        distance: passed_along(block, "gy", -distance) if distance else block
        for distance, block in zip(early, blocks)
    }
    held_back = blocks[len(early) :]

    far_height = (STEPS * RECORDS + 3) * rows
    near_height = far_height + 3 * rows
    forth, back, far, edges, *blocks = call(
        monitor_message,
        [SMEM] + [VMEM] * 5 + [ANY],
        [
            (near_height, columns),
            (near_height, columns),
            (far_height, columns),
            (KINDS, 2 * rows, layers * SEAM),
        ]
        + [block] * len(late),
        permittivity,
        *fields,
        same,
        cross,
        *held_back,
        input_output_aliases={6: 4},
        out_specs=[VMEM] * 4 + [ANY],
        name="monitor_message",
        flops=10**5,
        moved=10**6,
    )
    message_after = passed_along(back, "gy", -1)
    message_before = passed_along(forth, "gy", 1)
    for distance, block in zip(late, blocks):
        spectra[distance] = passed_along(block, "gy", -distance)
    messages = [far, message_after]
    for distance in range(2, y_blocks - 1):
        messages.append(passed_along(far, "gy", -distance))
    messages = (messages + [message_before])[:y_blocks]

    coefs = jnp.asarray(wave_coefficients(slab_spectra.shape[1] // 2))
    length_x, length_y = rows * x_blocks, columns * y_blocks
    kept = OY // x_blocks
    out_tiles = -(-group_waves * RECORDS * kept // OY)
    sums_y = y_table(length_y)
    slab_here, monitor_here = call(
        fetch,
        [ANY] + [HBM] * 2,
        [slab_spectra.shape, monitor_spectra.shape],
        far,
        in_hbm(slab_spectra),
        in_hbm(monitor_spectra),
        name="fetch",
        flops=1,
        moved=3 * 10**6,
        scratch_shapes=[pltpu.SemaphoreType.DMA((2,))],
    )
    monitor_y, weights = call(
        y_monitor,
        [SMEM] * 2 + [VMEM, ANY] + [VMEM] * y_blocks,
        [(x_blocks, out_tiles * 2 * rows, OY), (out_tiles * STEPS * 2, rows, OY)],
        wave_index,
        coefs,
        sums_y,
        slab_here,
        *[spectra[distance] for distance in range(y_blocks)],
        name="y_monitor",
        flops=10**8,
        moved=2 * 10**6,
    )
    (spectrum_y,) = call(
        functools.partial(y_records, group_waves),
        [VMEM] * (3 + y_blocks),
        [monitor_y.shape],
        record_table(length_y, y_blocks),
        monitor_y,
        weights,
        *messages,
        name="y_records",
        flops=10**8,
        moved=2 * 10**6,
    )
    members = [
        [x * y_blocks + y for x in order_of(x_blocks)] for y in range(y_blocks)
    ]
    swapped = lax.all_to_all(
        spectrum_y, ("gx", "gy"), split_axis=0, concat_axis=0, axis_index_groups=members, tiled=True
    )

    electric_next, magnetic_next, slab_next, monitor_next = call(
        local_updates,
        [SMEM] * 3 + [VMEM] * 10,
        [electric.shape, magnetic.shape, slab_spectra.shape, monitor_spectra.shape],
        permittivity,
        wave_index,
        coefs,
        *fields,
        same,
        cross,
        edges,
        message_before,
        message_after,
        slab_here,
        monitor_here,
        name="local_updates",
        scratch_shapes=[
            pltpu.VMEM(electric.shape, jnp.float32),
            pltpu.VMEM(magnetic.shape, jnp.float32),
            pltpu.VMEM(slab_spectra.shape, jnp.float32),
            pltpu.VMEM(monitor_spectra.shape, jnp.float32),
            pltpu.SemaphoreType.DMA((4,)),
        ],
        out_specs=[HBM] * 4,
        flops=10**7,
        moved=6 * 10**6,
    )

    scaling = 1.0 / math.sqrt(length_x * length_y)
    (orders,) = call(
        functools.partial(x_orders, kept),
        [VMEM] * 2,
        [(group_waves, 2, RECORDS, kept, OX)],
        swapped,
        jnp.asarray(x_table(length_x, x_blocks, scaling)),
        name="x_orders",
        flops=10**7,
        moved=5 * 10**5,
    )
    return (electric_next, magnetic_next, slab_next, monitor_next, orders)


def solution(mesh):
    in_specs = (
        P(None, None, "gx", "gy"),
        P(None, None, "gx", "gy"),
        P(None, "gx", "gy"),
        P(),
        P(None, None, "gx", "gy"),
        P(None, None, None, "gx", "gy"),
        P(),
    )
    out_specs = (
        P(None, None, "gx", "gy"),
        P(None, None, "gx", "gy"),
        P(None, None, "gx", "gy"),
        P(None, None, None, "gx", "gy"),
        P("gy", None, None, "gx", None),
    )
    return jax.shard_map(
        per_device, mesh=mesh, in_specs=in_specs, out_specs=out_specs, check_vma=False
    )
```

```python
import functools
import math

import jax
import jax.numpy as jnp
import ml_dtypes
import numpy as np
from jax import lax
from jax.experimental import pallas as pl
from jax.experimental.pallas import tpu as pltpu
from jax.sharding import PartitionSpec as P

OY = 128
OX = 64

TIME_STEP = 0.5
OMEGA_LOW = 0.15
OMEGA_HIGH = 0.8

STEPS = 2
EDGE = 2 * STEPS
SEAM = 2 * EDGE
DEEP = 4
OUTER = SEAM // STEPS
KINDS = 7
RECORDS = 4

VMEM = pl.BlockSpec(memory_space=pltpu.VMEM)
HBM = pl.BlockSpec(memory_space=pltpu.HBM)
ANY = pl.BlockSpec(memory_space=pl.ANY)
SMEM = pl.BlockSpec(memory_space=pltpu.SMEM)
PARAMS = pltpu.CompilerParams(vmem_limit_bytes=48 * 1024 * 1024)


def in_hbm(array):
    return pltpu.with_memory_space_constraint(array, pltpu.HBM)


def passed_along(block, axis, distance):
    devices = range(lax.axis_size(axis))
    route = [((i - distance) % len(devices), i) for i in devices]
    return lax.ppermute(block, axis, route)


def rolled(values, shift, axis):
    shift %= values.shape[axis]
    return pltpu.roll(values, shift, axis) if shift else values


def iota(shape, axis):
    return lax.broadcasted_iota(jnp.int32, shape, axis)


def rates_of(permittivity, classes, shape):
    return [TIME_STEP / jnp.full(shape, permittivity[k], jnp.float32) for k in range(classes)]


def rate_at(material, rates):
    rate = rates[-1]
    for k in range(len(rates) - 2, -1, -1):
        rate = jnp.where(material == k, rates[k], rate)
    return rate


class Leapfrog:
    def __init__(self, start, layers=None, above=None, below=None):
        self.start = start
        self.layers = layers
        self.above = above
        self.below = below
        self.known = {}

    def first(self, z):
        if ("0", z) not in self.known:
            self.known["0", z] = self.start(z)
        return self.known["0", z]

    def e(self, s, z):
        if s == 0:
            return self.first(z)[0:3]
        if ("e", s, z) not in self.known:
            ex, ey, ez = self.e(s - 1, z)
            hx, hy, hz = self.h(s, z)
            if self.layers is None:
                down_x, down_y = self.below(hx), self.below(hy)
            else:
                down_x, down_y = self.h(s, z - 1)[:2] if z else (0.0, 0.0)
            rate = self.first(z)[6]
            self.known["e", s, z] = (
                ex + rate * ((hz - rolled(hz, 1, 1)) - (hy - down_y)),
                ey + rate * ((hx - down_x) - (hz - rolled(hz, 1, 0))),
                ez + rate * ((hy - rolled(hy, 1, 0)) - (hx - rolled(hx, 1, 1))),
            )
        return self.known["e", s, z]

    def h(self, s, z):
        if s == 0:
            return self.first(z)[3:6]
        if ("h", s, z) not in self.known:
            ex, ey, ez = self.e(s - 1, z)
            hx, hy, hz = self.h(s - 1, z)
            if self.layers is None:
                up_x, up_y = self.above(ex), self.above(ey)
            else:
                up_x, up_y = self.e(s - 1, z + 1)[:2] if z + 1 < self.layers else (0.0, 0.0)
            self.known["h", s, z] = (
                hx - TIME_STEP * ((rolled(ez, -1, 1) - ez) - (up_y - ey)),
                hy - TIME_STEP * ((up_x - ex) - (rolled(ez, -1, 0) - ez)),
                hz - TIME_STEP * ((rolled(ey, -1, 0) - ey) - (rolled(ex, -1, 1) - ex)),
            )
        return self.known["h", s, z]

    def records(self, s, z):
        return self.e(s, z)[:2] + self.h(s, z)[:2]


def seam_leapfrog(tiles, layers):
    layer = iota(tiles[0].shape, 1) // SEAM % layers
    return Leapfrog(
        lambda z: tiles,
        above=lambda f: jnp.where(layer < layers - 1, rolled(f, -SEAM, 1), 0.0),
        below=lambda f: jnp.where(layer > 0, rolled(f, SEAM, 1), 0.0),
    )


def own_planes(e_ref, h_ref, m_ref, rates):
    def at(z):
        rate = rate_at(m_ref[z], rates)
        return [e_ref[c, z] for c in range(3)] + [h_ref[c, z] for c in range(3)] + [rate]

    return at


def widened_planes(own, same_ref, cross_ref):
    even = lax.rem(lax.axis_index("gx"), 2) == 0

    def at(z):
        planes = own(z)
        rows = planes[0].shape[0]
        group, place = divmod(z, rows // STEPS)
        row = iota(planes[0].shape, 0)
        wide = []
        for kind in range(KINDS):
            same, cross = same_ref[kind, group], cross_ref[kind, group]
            after = rolled(jnp.where(even, same, cross), -STEPS * place, 0)
            before = rolled(jnp.where(even, cross, same), rows - STEPS - STEPS * place, 0)
            halo = jnp.where(row < STEPS, after, before)
            wide.append(jnp.concatenate([planes[kind], halo], axis=0))
        return wide

    return at


def block_copy(distance, spectra_any, block_ref, semaphore):
    waves = block_ref.shape[0]
    blocks = spectra_any.shape[0] // waves
    owner = lax.rem(lax.axis_index("gy") + blocks - distance, blocks)
    source = spectra_any.at[pl.ds(owner * waves, waves)]
    return pltpu.make_async_copy(source, block_ref, semaphore)


def pack_faces(
    distances,
    perm_any,
    e_any,
    h_any,
    m_any,
    spectra_any,
    same_ref,
    cross_ref,
    *refs,
):
    even = lax.rem(lax.axis_index("gx"), 2) == 0
    *block_refs, perm_ref, e_ref, h_ref, m_ref, ready, sent = refs
    sources, targets = (e_any, h_any, m_any, perm_any), (e_ref, h_ref, m_ref, perm_ref)
    copies = [
        pltpu.make_async_copy(source, target, ready.at[i])
        for i, (source, target) in enumerate(zip(sources, targets))
    ]
    for i, (distance, block_ref) in enumerate(zip(distances, block_refs)):
        copies.append(block_copy(distance, spectra_any, block_ref, sent.at[i]))
    for copy in copies:
        copy.start()
    for copy in copies[:4]:
        copy.wait()
    layers, rows, columns = m_ref.shape
    rates = rates_of(perm_ref, perm_ref.shape[0], (rows, columns))
    own = own_planes(e_ref, h_ref, m_ref, rates)
    row = iota((rows, columns), 0)
    per_group = rows // STEPS
    for group in range(layers // per_group):
        planes = [own(group * per_group + place) for place in range(per_group)]
        for kind in range(KINDS):
            forth = rolled(planes[0][kind], STEPS - rows, 0)
            back = planes[0][kind]
            for place in range(1, per_group):
                spot = STEPS * place
                here = planes[place][kind]
                forth = jnp.where(row >= spot, rolled(here, spot + STEPS - rows, 0), forth)
                back = jnp.where(row >= spot, rolled(here, spot, 0), back)
            same_ref[kind, group] = jnp.where(even, forth, back)
            cross_ref[kind, group] = jnp.where(even, back, forth)
    for copy in copies[4:]:
        copy.wait()


def blocks_transposed(tiles):
    tiles = list(tiles)
    count = len(tiles)
    width = tiles[0].shape[1] // count
    block = iota(tiles[0].shape, 1) // width
    bit = 1
    while bit < count:
        low = (block & bit) == 0
        for i in range(count):
            if not i & bit:
                first, second = tiles[i], tiles[i + bit]
                tiles[i] = jnp.where(low, first, rolled(second, bit * width, 1))
                tiles[i + bit] = jnp.where(low, rolled(first, -bit * width, 1), second)
        bit *= 2
    return tiles


def packed_edges(planes, layers, spot):
    tile = None
    for z in range(layers):
        here = rolled(planes[z], spot + z * SEAM + EDGE, 1)
        if tile is None:
            tile = here
        else:
            tile = jnp.where(iota(tile.shape, 1) >= spot + z * SEAM, here, tile)
    return tile


def squeezed(first, second):
    rows = first.shape[0] // 2
    row = iota((rows, first.shape[1]), 0)
    ends = (row < STEPS) | (row >= rows - STEPS)
    second_halo = second[rows:]
    moved = jnp.where(
        row < 2 * STEPS, rolled(second_halo, STEPS, 0), rolled(second_halo, -STEPS, 0)
    )
    return first[:rows], second[:rows], jnp.where(ends, first[rows:], moved)


def stretched(first, second, halo):
    rows = first.shape[0]
    row = iota(halo.shape, 0)
    moved = jnp.where(row < 2 * STEPS, rolled(halo, -STEPS, 0), rolled(halo, STEPS, 0))
    return jnp.concatenate([first, halo], axis=0), jnp.concatenate([second, moved], axis=0)


def pair_of_tiles(ref, pair, rows):
    base = (STEPS * RECORDS + 3 * pair) * rows
    return stretched(*[ref[pl.ds(base + i * rows, rows), :] for i in range(3)])


def monitor_message(
    perm_ref,
    e_ref,
    h_ref,
    m_ref,
    same_ref,
    cross_ref,
    block_any,
    forth_ref,
    back_ref,
    far_ref,
    edges_ref,
    block_out,
):
    layers, rows, columns = m_ref.shape
    rates = rates_of(perm_ref, perm_ref.shape[0], (rows, columns))
    wide = widened_planes(own_planes(e_ref, h_ref, m_ref, rates), same_ref, cross_ref)
    low = layers - DEEP
    walk = Leapfrog(lambda z: wide(low + z), layers=DEEP)
    for s in range(STEPS):
        for c, record in enumerate(walk.records(s + 1, DEEP - 1)):
            place = pl.ds((s * RECORDS + c) * rows, rows)
            for ref in (forth_ref, back_ref, far_ref):
                ref[place, :] = record[:rows]
    planes = [wide(z) for z in range(low)] + [walk.first(z) for z in range(DEEP)]
    span = DEEP * SEAM
    per_tile = columns // span
    tops, lasts, firsts = ([None, None] for _ in range(3))
    for kind in range(KINDS):
        edges = packed_edges([planes[z][kind] for z in range(layers)], layers, 0)
        edges_ref[kind] = edges
        lane = iota(edges.shape, 1)
        tile, spot = divmod(kind, per_tile)
        here = rolled(edges, spot * span - low * SEAM, 1)
        tops[tile] = jnp.where(lane >= spot * span, here, tops[tile]) if spot else here
        tile, spot = divmod(kind, OUTER)
        for tiles, shift in ((lasts, STEPS), (firsts, EDGE)):
            here = rolled(edges, spot * STEPS - shift, 1)
            tiles[tile] = jnp.where(lane % SEAM >= spot * STEPS, here, tiles[tile]) if spot else here
    base = STEPS * RECORDS * rows
    for i, part in enumerate(squeezed(*tops)):
        for ref in (forth_ref, back_ref, far_ref):
            ref[pl.ds(base + i * rows, rows), :] = part
    for ref, tiles in ((forth_ref, lasts), (back_ref, firsts)):
        for i, part in enumerate(squeezed(*tiles)):
            ref[pl.ds(base + (3 + i) * rows, rows), :] = part


def waves_of(coef_ref, wave):
    base = wave * (STEPS * 4)
    return lambda s, half, part: coef_ref[base + (s * 2 + half) * 2 + part]


def exact_dot(left, right, contracted):
    return lax.dot_general(
        left,
        right,
        (contracted, ((), ())),
        precision=lax.Precision.HIGHEST,
        preferred_element_type=jnp.float32,
    )


def split_dot(values, tables, total, contracted=((1,), (0,))):
    coarse = values.astype(jnp.bfloat16)
    fine = (values - coarse.astype(jnp.float32)).astype(jnp.bfloat16)
    for left, right in ((coarse, tables[0]), (fine, tables[0]), (coarse, tables[1])):
        product = lax.dot_general(
            left, right, (contracted, ((), ())), preferred_element_type=jnp.float32
        )
        total = product if total is None else total + product
    return total


def packed_orders(values, planes, kept):
    rows = values.shape[0] // planes
    parts = [values[plane * rows : (plane + 1) * rows] for plane in range(planes)]
    targets = per_tile = OY // kept
    if planes % per_tile == 0 and not targets & (targets - 1):
        groups = [parts[i : i + per_tile] for i in range(0, planes, per_tile)]
        return list(zip(*[blocks_transposed(group) for group in groups]))
    lane = iota((rows, OY), 1)
    packed = []
    for target in range(targets):
        tiles = []
        for first in range(0, planes, per_tile):
            tile = None
            for plane in range(first, min(planes, first + per_tile)):
                spot = (plane - first) * kept
                here = rolled(parts[plane], spot - target * kept, 1)
                tile = here if tile is None else jnp.where(lane >= spot, here, tile)
            tiles.append(tile)
        packed.append(tiles)
    return packed


def fetch(after_this, slab_any, monitor_any, slab_ref, monitor_ref, ready):
    copies = [
        pltpu.make_async_copy(slab_any, slab_ref, ready.at[0]),
        pltpu.make_async_copy(monitor_any, monitor_ref, ready.at[1]),
    ]
    for copy in copies:
        copy.start()
    for copy in copies:
        copy.wait()


def y_monitor(wave_ref, coef_ref, table_ref, own_ref, *refs):
    *spectra, out_ref, weights_ref = refs
    blocks = len(spectra) + 1
    waves, _, records, rows, columns = spectra[0].shape
    me = lax.axis_index("gy")
    spectra = [own_ref.at[pl.ds(me * waves, waves)]] + spectra
    total = None
    for block in range(blocks):
        owner = lax.rem(me + block, blocks)
        place = pl.ds(pl.multiple_of(owner * columns, columns), columns)
        parts = []
        for part in range(2):
            for w in range(waves):
                parts += [spectra[block][w, part, c] for c in range(records)]
        tables = [table_ref[i, place, :] for i in range(2)]
        total = split_dot(jnp.concatenate(parts, axis=0), tables, total)
    half = waves * records * rows
    real = total[:half, :OY] + total[half:, OY:]
    imag = total[half:, :OY] - total[:half, OY:]
    targets = out_ref.shape[0]
    for part, values in enumerate((real, imag)):
        packed = packed_orders(values, waves * records, OY // targets)
        for target in range(targets):
            for i, tile in enumerate(packed[target]):
                out_ref[target, pl.ds((i * 2 + part) * rows, rows), :] = tile
    kept = OY // targets
    lane = iota((rows, OY), 1)
    per_wave = RECORDS * kept
    per_tile = OY // per_wave
    for tile in range(weights_ref.shape[0] // (2 * STEPS)):
        some = range(tile * per_tile, min(waves, (tile + 1) * per_tile))
        coefs = [waves_of(coef_ref, wave_ref[me * waves + w]) for w in some]
        for s in range(STEPS):
            for part in range(2):
                weight = None
                for i, coef in enumerate(coefs):
                    for half in range(2):
                        value = jnp.full((rows, OY), coef(s, half, part), jnp.float32)
                        spot = i * per_wave + half * (per_wave // 2)
                        weight = value if weight is None else jnp.where(lane >= spot, value, weight)
                weights_ref[(tile * STEPS + s) * 2 + part] = weight


def y_records(waves, table_ref, monitor_ref, weights_ref, *refs):
    *messages, out_any, out_ref, done = refs
    messages = messages[::-1]
    blocks = len(messages)
    columns = messages[0].shape[1]
    targets, height, _ = out_ref.shape
    kept = OY // targets
    out_tiles = -(-waves * RECORDS * kept // OY)
    rows = height // (2 * out_tiles)
    me = lax.axis_index("gy")
    span = DEEP * SEAM
    per_tile = columns // span
    base = STEPS * RECORDS * rows
    column = iota((2 * rows, columns), 1) % SEAM
    edges = [pair_of_tiles(message, 0, rows) for message in messages]

    total = None
    for tile in range(-(-blocks // per_tile)):
        seams = range(tile * per_tile, min(blocks, (tile + 1) * per_tile))
        kinds = []
        for part in range(2):
            mixed = []
            for seam in list(seams) + [seams[0]] * (per_tile - len(seams)):
                here, after = edges[seam][part], edges[(seam + 1) % blocks][part]
                mixed.append(jnp.where(column < EDGE, here, after))
            kinds += blocks_transposed(mixed)
        walk = seam_leapfrog(kinds[:KINDS], DEEP)
        record = []
        for s in range(STEPS):
            record += [value[:rows] for value in walk.records(s + 1, 0)]
        values = jnp.concatenate(record, axis=0)[:, : len(seams) * span]
        owners = [lax.rem(me + seam, blocks) for seam in seams]
        places = [pl.ds(pl.multiple_of(owner * span, span), span) for owner in owners]
        tables = [
            jnp.concatenate([table_ref[part, place, :] for place in places], axis=0)
            for part in range(2)
        ]
        total = split_dot(values, tables, total)
    for block in range(blocks):
        owner = lax.rem(me + block, blocks)
        place = pl.ds(pl.multiple_of(blocks * span + owner * columns, span), columns)
        values = messages[block][pl.ds(0, base), :]
        total = split_dot(values, [table_ref[part, place, :] for part in range(2)], total)
    lane = iota((rows, OY), 1)
    per_wave = RECORDS * kept
    per_tile = OY // per_wave
    packed_parts = [
        packed_orders(total[:, part * OY : (part + 1) * OY], STEPS * RECORDS, kept)
        for part in range(2)
    ]
    copies = []
    for target in range(targets):
        spot = order_of(targets).index(target)
        sides = []
        for part in range(2):
            (packed,) = packed_parts[part][target]
            steps = []
            for s in range(STEPS):
                spread = None
                for i in range(min(per_tile, waves)):
                    here = rolled(packed, i * per_wave - s * per_wave, 1)
                    spread = here if i == 0 else jnp.where(lane >= i * per_wave, here, spread)
                steps.append(spread)
            sides.append(steps)
        for tile in range(out_tiles):
            for part in range(2):
                place = pl.ds((tile * 2 + part) * rows, rows)
                value = monitor_ref[target, place, :]
                for s in range(STEPS):
                    first = (tile * STEPS + s) * 2
                    real, imag = weights_ref[first], weights_ref[first + 1]
                    if part == 0:
                        value = value + (real * sides[0][s] - imag * sides[1][s])
                    else:
                        value = value + (imag * sides[0][s] + real * sides[1][s])
                out_ref[spot, place, :] = value
        copies.append(
            pltpu.make_async_copy(out_ref.at[spot], out_any.at[spot], done.at[spot])
        )
        copies[-1].start()
    for copy in copies:
        copy.wait()


def x_orders(kept, values_ref, table_ref, out_ref):
    sources, height, lanes = values_ref.shape
    waves, _, records, _, _ = out_ref.shape
    depth = table_ref.shape[1]
    rows = depth // sources
    per_tile = lanes // kept
    for tile in range(height // rows):
        values = jnp.concatenate(
            [values_ref[source, pl.ds(tile * rows, rows), :] for source in range(sources)], axis=0
        )
        result = split_dot(values, [table_ref[0], table_ref[1]], None, ((0,), (0,)))
        for place in range(per_tile):
            wave, record = divmod(tile * per_tile + place, records)
            if wave < waves:
                here = result[place * kept : (place + 1) * kept]
                out_ref[wave, 0, record] = here[:, :OX]
                out_ref[wave, 1, record] = here[:, OX:]


def local_updates(
    perm_ref,
    wave_ref,
    coef_ref,
    e_ref,
    h_ref,
    m_ref,
    same_ref,
    cross_ref,
    edges_ref,
    message_after_ref,
    message_before_ref,
    slab_ref,
    monitor_ref,
    e_any,
    h_any,
    slab_out_any,
    monitor_out_any,
    e_out,
    h_out,
    slab_out,
    monitor_out,
    done,
):
    layers, rows, columns = m_ref.shape
    rates = rates_of(perm_ref, perm_ref.shape[0], (rows, columns))
    wide = widened_planes(own_planes(e_ref, h_ref, m_ref, rates), same_ref, cross_ref)
    walk = Leapfrog(wide, layers=layers)
    left = iota((2 * rows, layers * SEAM), 1) % SEAM < EDGE
    last = pair_of_tiles(message_before_ref, 1, rows)
    first = pair_of_tiles(message_after_ref, 1, rows)
    before, after = [], []
    for kind in range(KINDS):
        mine = edges_ref[kind]
        tile, spot = divmod(kind, OUTER)
        from_before = rolled(last[tile], STEPS - spot * STEPS, 1)
        from_after = rolled(first[tile], EDGE - spot * STEPS, 1)
        before.append(jnp.where(left, from_before, mine))
        after.append(jnp.where(left, mine, from_after))
    before = seam_leapfrog(before, layers)
    after = seam_leapfrog(after, layers)
    column = iota((rows, columns), 1)
    inner = (column >= STEPS) & (column < columns - STEPS)
    joined = {}

    def mended(s, z, kind):
        if (s, kind) not in joined:
            ends = [(side.e(s, 0) + side.h(s, 0))[kind][:rows] for side in (after, before)]
            joined[s, kind] = jnp.where(left[:rows], ends[0], ends[1])
        value = (walk.e(s, z) + walk.h(s, z))[kind][:rows]
        return jnp.where(inner, value, rolled(joined[s, kind], -(z * SEAM + EDGE), 1))

    middle = layers // 2
    slab_records = [[None] * 2 for _ in range(STEPS)]
    records = [[None] * RECORDS for _ in range(STEPS)]
    for z in range(layers):
        for kind in range(6):
            value = mended(STEPS, z, kind)
            if kind < 3:
                e_out[kind, z] = value
            else:
                h_out[kind - 3, z] = value
        for s in range(STEPS):
            if z == middle:
                slab_records[s] = [mended(s + 1, z, kind) for kind in (0, 1)]
            if z == layers - 1:
                records[s] = [mended(s + 1, z, kind) for kind in (0, 1, 3, 4)]
    sent = [
        pltpu.make_async_copy(e_out, e_any, done.at[0]),
        pltpu.make_async_copy(h_out, h_any, done.at[1]),
    ]
    for copy in sent:
        copy.start()
    frequencies = slab_ref.shape[1] // 2

    def one_frequency(f, carry):
        coef = waves_of(coef_ref, f)
        for c in range(2):
            for part in range(2):
                value = slab_ref[c, part * frequencies + f]
                for s in range(STEPS):
                    value = value + coef(s, 0, part) * slab_records[s][c]
                slab_out[c, part * frequencies + f] = value
        return carry

    lax.fori_loop(0, frequencies, one_frequency, 0, unroll=4)
    sent.append(pltpu.make_async_copy(slab_out, slab_out_any, done.at[2]))
    sent[-1].start()
    for w in range(monitor_ref.shape[0]):
        coef = waves_of(coef_ref, wave_ref[w])
        for part in range(2):
            for c in range(RECORDS):
                value = monitor_ref[w, part, c]
                for s in range(STEPS):
                    value = value + coef(s, c // 2, part) * records[s][c]
                monitor_out[w, part, c] = value
    sent.append(pltpu.make_async_copy(monitor_out, monitor_out_any, done.at[3]))
    sent[-1].start()
    for copy in sent:
        copy.wait()


def wave_coefficients(freq_count):
    omegas = OMEGA_LOW + (OMEGA_HIGH - OMEGA_LOW) * np.arange(freq_count) / (freq_count - 1)
    times = TIME_STEP * (np.arange(1, STEPS + 1)[:, None] - np.array([0.0, 0.5])[None, :])
    angles = omegas[:, None, None] * times[None]
    table = np.stack([TIME_STEP * np.cos(angles), -TIME_STEP * np.sin(angles)], axis=-1)
    return table.reshape(-1).astype(np.float32)


def angles_of(length, kept):
    wanted = (np.arange(kept) - kept // 2) % length
    return 2.0 * math.pi / length * (np.arange(length)[:, None] * wanted[None, :] % length)


def y_table(length):
    angles = angles_of(length, OY)
    return split_table(np.concatenate([np.cos(angles), np.sin(angles)], axis=1))


def split_table(table):
    table = table.astype(np.float32)
    coarse = table.astype(ml_dtypes.bfloat16)
    fine = (table - coarse.astype(np.float32)).astype(ml_dtypes.bfloat16)
    return jnp.asarray(np.stack([coarse, fine]))


def record_table(length, blocks):
    angles = angles_of(length, OY)
    table = np.concatenate([np.cos(angles), -np.sin(angles)], axis=1)
    columns = length // blocks
    seams = np.zeros((blocks, DEEP, SEAM, 2 * OY))
    for block in range(blocks):
        for column in range(-STEPS, STEPS):
            row = ((block + 1) * columns + column) % length
            seams[block, DEEP - 1, EDGE + column] = table[row]
    inner = table.copy()
    place = np.arange(length) % columns
    inner[(place < STEPS) | (place >= columns - STEPS)] = 0.0
    return split_table(np.concatenate([seams.reshape(-1, 2 * OY), inner]))


def order_of(blocks):
    return list(reversed(range(blocks)))


def x_table(length, blocks, scaling):
    angles = angles_of(length, OX).reshape(blocks, length // blocks, OX)[order_of(blocks)]
    real = np.concatenate([np.cos(angles), -np.sin(angles)], axis=2)
    imag = np.concatenate([np.sin(angles), np.cos(angles)], axis=2)
    table = np.stack([real, imag], axis=1) * scaling
    return split_table(table.reshape(2 * length, 2 * OX))


def call(kernel, in_specs, shapes, *operands, name, flops=0, moved=0, **more):
    kind = jax.ShapeDtypeStruct
    out = [kind(shape, jnp.float32) for shape in shapes]
    return pl.pallas_call(
        kernel,
        out_shape=out,
        in_specs=in_specs,
        out_specs=more.pop("out_specs", [VMEM] * len(out)),
        compiler_params=PARAMS,
        cost_estimate=pl.CostEstimate(flops=flops, bytes_accessed=moved, transcendentals=0),
        name=name,
        **more,
    )(*operands)


def per_device(
    electric, magnetic, material, permittivity, slab_spectra, monitor_spectra, wave_index
):
    layers, rows, columns = material.shape
    x_blocks, y_blocks = lax.axis_size("gx"), lax.axis_size("gy")
    waves = monitor_spectra.shape[0]
    group_waves = waves // y_blocks
    fields = (electric, magnetic, material)
    groups = layers * STEPS // rows

    faces = (KINDS, groups, rows, columns)
    block = (group_waves,) + monitor_spectra.shape[1:]
    late = [1]
    early = [distance for distance in range(1, y_blocks) if distance not in late]
    same, cross, *blocks = call(
        functools.partial(pack_faces, early + late),
        [HBM] * 5,
        [faces, faces] + [block] * (y_blocks - 1),
        *[in_hbm(array) for array in (permittivity, *fields, monitor_spectra)],
        name="pack_faces",
        flops=10**5,
        moved=10**6,
        scratch_shapes=[
            pltpu.SMEM(permittivity.shape, jnp.float32),
            pltpu.VMEM(electric.shape, jnp.float32),
            pltpu.VMEM(magnetic.shape, jnp.float32),
            pltpu.VMEM(material.shape, jnp.int32),
            pltpu.SemaphoreType.DMA((4,)),
            pltpu.SemaphoreType.DMA((y_blocks - 1,)),
        ],
    )
    line = range(x_blocks)
    same = lax.ppermute(same, "gx", [(i, i ^ 1) for i in line])
    cross = lax.ppermute(cross, "gx", [(i, (i + (1 if i % 2 else -1)) % x_blocks) for i in line])
    spectra = {
        distance: passed_along(block, "gy", -distance) for distance, block in zip(early, blocks)
    }
    held_back = blocks[len(early) :]

    far_height = (STEPS * RECORDS + 3) * rows
    near_height = far_height + 3 * rows
    forth, back, far, edges, *blocks = call(
        monitor_message,
        [SMEM] + [VMEM] * 5 + [ANY],
        [
            (near_height, columns),
            (near_height, columns),
            (far_height, columns),
            (KINDS, 2 * rows, layers * SEAM),
        ]
        + [block] * len(late),
        permittivity,
        *fields,
        same,
        cross,
        *held_back,
        input_output_aliases={6: 4},
        out_specs=[VMEM] * 4 + [ANY],
        name="monitor_message",
        flops=10**5,
        moved=10**6,
    )
    message_before = passed_along(forth, "gy", 1)
    message_after = passed_along(back, "gy", -1)
    for distance, block in zip(late, blocks):
        spectra[distance] = passed_along(block, "gy", -distance)
    messages = [far, message_after]
    for distance in range(2, y_blocks - 1):
        messages.append(passed_along(far, "gy", -distance))
    messages = (messages + [message_before])[:y_blocks]

    coefs = jnp.asarray(wave_coefficients(slab_spectra.shape[1] // 2))
    length_x, length_y = rows * x_blocks, columns * y_blocks
    kept = OY // x_blocks
    out_tiles = -(-group_waves * RECORDS * kept // OY)
    sums_y = y_table(length_y)
    slab_here, monitor_here = call(
        fetch,
        [ANY] + [HBM] * 2,
        [slab_spectra.shape, monitor_spectra.shape],
        far,
        in_hbm(slab_spectra),
        in_hbm(monitor_spectra),
        name="fetch",
        flops=1,
        moved=3 * 10**6,
        scratch_shapes=[pltpu.SemaphoreType.DMA((2,))],
    )
    monitor_y, weights = call(
        y_monitor,
        [SMEM] * 2 + [VMEM] * (1 + y_blocks),
        [(x_blocks, out_tiles * 2 * rows, OY), (out_tiles * STEPS * 2, rows, OY)],
        wave_index,
        coefs,
        sums_y,
        monitor_here,
        *[spectra[distance] for distance in range(1, y_blocks)],
        name="y_monitor",
        flops=10**8,
        moved=2 * 10**6,
    )
    (spectrum_y,) = call(
        functools.partial(y_records, group_waves),
        [VMEM] * (3 + y_blocks),
        [monitor_y.shape],
        record_table(length_y, y_blocks),
        monitor_y,
        weights,
        *messages[::-1],
        out_specs=[HBM],
        scratch_shapes=[
            pltpu.VMEM(monitor_y.shape, jnp.float32),
            pltpu.SemaphoreType.DMA((x_blocks,)),
        ],
        name="y_records",
        flops=10**8,
        moved=2 * 10**6,
    )
    members = [
        [x * y_blocks + y for x in order_of(x_blocks)] for y in range(y_blocks)
    ]
    swapped = lax.all_to_all(
        spectrum_y, ("gx", "gy"), split_axis=0, concat_axis=0, axis_index_groups=members, tiled=True
    )

    electric_next, magnetic_next, slab_next, monitor_next = call(
        local_updates,
        [SMEM] * 3 + [VMEM] * 10,
        [electric.shape, magnetic.shape, slab_spectra.shape, monitor_spectra.shape],
        permittivity,
        wave_index,
        coefs,
        *fields,
        same,
        cross,
        edges,
        message_after,
        message_before,
        slab_here,
        monitor_here,
        name="local_updates",
        scratch_shapes=[
            pltpu.VMEM(electric.shape, jnp.float32),
            pltpu.VMEM(magnetic.shape, jnp.float32),
            pltpu.VMEM(slab_spectra.shape, jnp.float32),
            pltpu.VMEM(monitor_spectra.shape, jnp.float32),
            pltpu.SemaphoreType.DMA((4,)),
        ],
        out_specs=[HBM] * 4,
        flops=10**7,
        moved=6 * 10**6,
    )

    scaling = 1.0 / math.sqrt(length_x * length_y)
    (orders,) = call(
        functools.partial(x_orders, kept),
        [VMEM] * 2,
        [(group_waves, 2, RECORDS, kept, OX)],
        swapped,
        x_table(length_x, x_blocks, scaling),
        name="x_orders",
        flops=10**7,
        moved=5 * 10**5,
    )
    return (electric_next, magnetic_next, slab_next, monitor_next, orders)


def solution(mesh):
    in_specs = (
        P(None, None, "gx", "gy"),
        P(None, None, "gx", "gy"),
        P(None, "gx", "gy"),
        P(),
        P(None, None, "gx", "gy"),
        P(None, None, None, "gx", "gy"),
        P(),
    )
    out_specs = (
        P(None, None, "gx", "gy"),
        P(None, None, "gx", "gy"),
        P(None, None, "gx", "gy"),
        P(None, None, None, "gx", "gy"),
        P("gy", None, None, "gx", None),
    )
    return jax.shard_map(
        per_device, mesh=mesh, in_specs=in_specs, out_specs=out_specs, check_vma=False
    )
```

```python
import functools
import math

import jax
import jax.numpy as jnp
import ml_dtypes
import numpy as np
from jax import lax
from jax.experimental import pallas as pl
from jax.experimental.pallas import tpu as pltpu
from jax.sharding import PartitionSpec as P

OY = 128
OX = 64

TIME_STEP = 0.5
OMEGA_LOW = 0.15
OMEGA_HIGH = 0.8

STEPS = 2
EDGE = 2 * STEPS
SEAM = 2 * EDGE
DEEP = 4
OUTER = SEAM // STEPS
KINDS = 7
RECORDS = 4

VMEM = pl.BlockSpec(memory_space=pltpu.VMEM)
HBM = pl.BlockSpec(memory_space=pltpu.HBM)
ANY = pl.BlockSpec(memory_space=pl.ANY)
SMEM = pl.BlockSpec(memory_space=pltpu.SMEM)
PARAMS = pltpu.CompilerParams(vmem_limit_bytes=48 * 1024 * 1024)


def in_hbm(array):
    return pltpu.with_memory_space_constraint(array, pltpu.HBM)


def passed_along(block, axis, distance):
    devices = range(lax.axis_size(axis))
    route = [((i - distance) % len(devices), i) for i in devices]
    return lax.ppermute(block, axis, route)


def rolled(values, shift, axis):
    shift %= values.shape[axis]
    return pltpu.roll(values, shift, axis) if shift else values


def iota(shape, axis):
    return lax.broadcasted_iota(jnp.int32, shape, axis)


def rates_of(permittivity, classes, shape):
    return [TIME_STEP / jnp.full(shape, permittivity[k], jnp.float32) for k in range(classes)]


def rate_at(material, rates):
    rate = rates[-1]
    for k in range(len(rates) - 2, -1, -1):
        rate = jnp.where(material == k, rates[k], rate)
    return rate


class Leapfrog:
    def __init__(self, start, layers=None, above=None, below=None):
        self.start = start
        self.layers = layers
        self.above = above
        self.below = below
        self.known = {}

    def first(self, z):
        if ("0", z) not in self.known:
            self.known["0", z] = self.start(z)
        return self.known["0", z]

    def e(self, s, z):
        if s == 0:
            return self.first(z)[0:3]
        if ("e", s, z) not in self.known:
            ex, ey, ez = self.e(s - 1, z)
            hx, hy, hz = self.h(s, z)
            if self.layers is None:
                down_x, down_y = self.below(hx), self.below(hy)
            else:
                down_x, down_y = self.h(s, z - 1)[:2] if z else (0.0, 0.0)
            rate = self.first(z)[6]
            self.known["e", s, z] = (
                ex + rate * ((hz - rolled(hz, 1, 1)) - (hy - down_y)),
                ey + rate * ((hx - down_x) - (hz - rolled(hz, 1, 0))),
                ez + rate * ((hy - rolled(hy, 1, 0)) - (hx - rolled(hx, 1, 1))),
            )
        return self.known["e", s, z]

    def h(self, s, z):
        if s == 0:
            return self.first(z)[3:6]
        if ("h", s, z) not in self.known:
            ex, ey, ez = self.e(s - 1, z)
            hx, hy, hz = self.h(s - 1, z)
            if self.layers is None:
                up_x, up_y = self.above(ex), self.above(ey)
            else:
                up_x, up_y = self.e(s - 1, z + 1)[:2] if z + 1 < self.layers else (0.0, 0.0)
            self.known["h", s, z] = (
                hx - TIME_STEP * ((rolled(ez, -1, 1) - ez) - (up_y - ey)),
                hy - TIME_STEP * ((up_x - ex) - (rolled(ez, -1, 0) - ez)),
                hz - TIME_STEP * ((rolled(ey, -1, 0) - ey) - (rolled(ex, -1, 1) - ex)),
            )
        return self.known["h", s, z]

    def records(self, s, z):
        return self.e(s, z)[:2] + self.h(s, z)[:2]


def seam_leapfrog(tiles, layers):
    layer = iota(tiles[0].shape, 1) // SEAM % layers
    return Leapfrog(
        lambda z: tiles,
        above=lambda f: jnp.where(layer < layers - 1, rolled(f, -SEAM, 1), 0.0),
        below=lambda f: jnp.where(layer > 0, rolled(f, SEAM, 1), 0.0),
    )


def own_planes(e_ref, h_ref, m_ref, rates):
    def at(z):
        rate = rate_at(m_ref[z], rates)
        return [e_ref[c, z] for c in range(3)] + [h_ref[c, z] for c in range(3)] + [rate]

    return at


def widened_planes(own, same_ref, cross_ref):
    even = lax.rem(lax.axis_index("gx"), 2) == 0

    def at(z):
        planes = own(z)
        rows = planes[0].shape[0]
        group, place = divmod(z, rows // STEPS)
        row = iota(planes[0].shape, 0)
        wide = []
        for kind in range(KINDS):
            same, cross = same_ref[kind, group], cross_ref[kind, group]
            after = rolled(jnp.where(even, same, cross), -STEPS * place, 0)
            before = rolled(jnp.where(even, cross, same), rows - STEPS - STEPS * place, 0)
            halo = jnp.where(row < STEPS, after, before)
            wide.append(jnp.concatenate([planes[kind], halo], axis=0))
        return wide

    return at


def block_copy(distance, spectra_any, block_ref, semaphore):
    waves = block_ref.shape[0]
    blocks = spectra_any.shape[0] // waves
    owner = lax.rem(lax.axis_index("gy") + blocks - distance, blocks)
    source = spectra_any.at[pl.ds(owner * waves, waves)]
    return pltpu.make_async_copy(source, block_ref, semaphore)


def pack_faces(
    distances,
    perm_any,
    e_any,
    h_any,
    m_any,
    spectra_any,
    same_ref,
    cross_ref,
    *refs,
):
    even = lax.rem(lax.axis_index("gx"), 2) == 0
    *block_refs, perm_ref, e_ref, h_ref, m_ref, ready, sent = refs
    sources, targets = (e_any, h_any, m_any, perm_any), (e_ref, h_ref, m_ref, perm_ref)
    copies = [
        pltpu.make_async_copy(source, target, ready.at[i])
        for i, (source, target) in enumerate(zip(sources, targets))
    ]
    for i, (distance, block_ref) in enumerate(zip(distances, block_refs)):
        copies.append(block_copy(distance, spectra_any, block_ref, sent.at[i]))
    for copy in copies:
        copy.start()
    for copy in copies[:4]:
        copy.wait()
    layers, rows, columns = m_ref.shape
    rates = rates_of(perm_ref, perm_ref.shape[0], (rows, columns))
    own = own_planes(e_ref, h_ref, m_ref, rates)
    row = iota((rows, columns), 0)
    per_group = rows // STEPS
    for group in range(layers // per_group):
        planes = [own(group * per_group + place) for place in range(per_group)]
        for kind in range(KINDS):
            forth = rolled(planes[0][kind], STEPS - rows, 0)
            back = planes[0][kind]
            for place in range(1, per_group):
                spot = STEPS * place
                here = planes[place][kind]
                forth = jnp.where(row >= spot, rolled(here, spot + STEPS - rows, 0), forth)
                back = jnp.where(row >= spot, rolled(here, spot, 0), back)
            same_ref[kind, group] = jnp.where(even, forth, back)
            cross_ref[kind, group] = jnp.where(even, back, forth)
    for copy in copies[4:]:
        copy.wait()


def blocks_transposed(tiles):
    tiles = list(tiles)
    count = len(tiles)
    width = tiles[0].shape[1] // count
    block = iota(tiles[0].shape, 1) // width
    bit = 1
    while bit < count:
        low = (block & bit) == 0
        for i in range(count):
            if not i & bit:
                first, second = tiles[i], tiles[i + bit]
                tiles[i] = jnp.where(low, first, rolled(second, bit * width, 1))
                tiles[i + bit] = jnp.where(low, rolled(first, -bit * width, 1), second)
        bit *= 2
    return tiles


def packed_edges(planes, layers, spot):
    tile = None
    for z in range(layers):
        here = rolled(planes[z], spot + z * SEAM + EDGE, 1)
        if tile is None:
            tile = here
        else:
            tile = jnp.where(iota(tile.shape, 1) >= spot + z * SEAM, here, tile)
    return tile


def squeezed(first, second):
    rows = first.shape[0] // 2
    row = iota((rows, first.shape[1]), 0)
    ends = (row < STEPS) | (row >= rows - STEPS)
    second_halo = second[rows:]
    moved = jnp.where(
        row < 2 * STEPS, rolled(second_halo, STEPS, 0), rolled(second_halo, -STEPS, 0)
    )
    return first[:rows], second[:rows], jnp.where(ends, first[rows:], moved)


def stretched(first, second, halo):
    rows = first.shape[0]
    row = iota(halo.shape, 0)
    moved = jnp.where(row < 2 * STEPS, rolled(halo, -STEPS, 0), rolled(halo, STEPS, 0))
    return jnp.concatenate([first, halo], axis=0), jnp.concatenate([second, moved], axis=0)


def pair_of_tiles(ref, pair, rows):
    base = (STEPS * RECORDS + 3 * pair) * rows
    return stretched(*[ref[pl.ds(base + i * rows, rows), :] for i in range(3)])


def monitor_message(
    perm_ref,
    e_ref,
    h_ref,
    m_ref,
    same_ref,
    cross_ref,
    forth_ref,
    back_ref,
    far_ref,
    edges_ref,
):
    layers, rows, columns = m_ref.shape
    rates = rates_of(perm_ref, perm_ref.shape[0], (rows, columns))
    wide = widened_planes(own_planes(e_ref, h_ref, m_ref, rates), same_ref, cross_ref)
    low = layers - DEEP
    walk = Leapfrog(lambda z: wide(low + z), layers=DEEP)
    for s in range(STEPS):
        for c, record in enumerate(walk.records(s + 1, DEEP - 1)):
            place = pl.ds((s * RECORDS + c) * rows, rows)
            for ref in (forth_ref, back_ref, far_ref):
                ref[place, :] = record[:rows]
    planes = [wide(z) for z in range(low)] + [walk.first(z) for z in range(DEEP)]
    span = DEEP * SEAM
    per_tile = columns // span
    tops, lasts, firsts = ([None, None] for _ in range(3))
    for kind in range(KINDS):
        edges = packed_edges([planes[z][kind] for z in range(layers)], layers, 0)
        edges_ref[kind] = edges
        lane = iota(edges.shape, 1)
        tile, spot = divmod(kind, per_tile)
        here = rolled(edges, spot * span - low * SEAM, 1)
        tops[tile] = jnp.where(lane >= spot * span, here, tops[tile]) if spot else here
        tile, spot = divmod(kind, OUTER)
        for tiles, shift in ((lasts, STEPS), (firsts, EDGE)):
            here = rolled(edges, spot * STEPS - shift, 1)
            tiles[tile] = jnp.where(lane % SEAM >= spot * STEPS, here, tiles[tile]) if spot else here
    base = STEPS * RECORDS * rows
    for i, part in enumerate(squeezed(*tops)):
        for ref in (forth_ref, back_ref, far_ref):
            ref[pl.ds(base + i * rows, rows), :] = part
    for ref, tiles in ((forth_ref, lasts), (back_ref, firsts)):
        for i, part in enumerate(squeezed(*tiles)):
            ref[pl.ds(base + (3 + i) * rows, rows), :] = part


def waves_of(coef_ref, wave):
    base = wave * (STEPS * 4)
    return lambda s, half, part: coef_ref[base + (s * 2 + half) * 2 + part]


def exact_dot(left, right, contracted):
    return lax.dot_general(
        left,
        right,
        (contracted, ((), ())),
        precision=lax.Precision.HIGHEST,
        preferred_element_type=jnp.float32,
    )


def split_dot(values, tables, total, contracted=((1,), (0,))):
    coarse = values.astype(jnp.bfloat16)
    fine = (values - coarse.astype(jnp.float32)).astype(jnp.bfloat16)
    for left, right in ((coarse, tables[0]), (fine, tables[0]), (coarse, tables[1])):
        product = lax.dot_general(
            left, right, (contracted, ((), ())), preferred_element_type=jnp.float32
        )
        total = product if total is None else total + product
    return total


def packed_orders(values, planes, kept):
    rows = values.shape[0] // planes
    parts = [values[plane * rows : (plane + 1) * rows] for plane in range(planes)]
    targets = per_tile = OY // kept
    if planes % per_tile == 0 and not targets & (targets - 1):
        groups = [parts[i : i + per_tile] for i in range(0, planes, per_tile)]
        return list(zip(*[blocks_transposed(group) for group in groups]))
    lane = iota((rows, OY), 1)
    packed = []
    for target in range(targets):
        tiles = []
        for first in range(0, planes, per_tile):
            tile = None
            for plane in range(first, min(planes, first + per_tile)):
                spot = (plane - first) * kept
                here = rolled(parts[plane], spot - target * kept, 1)
                tile = here if tile is None else jnp.where(lane >= spot, here, tile)
            tiles.append(tile)
        packed.append(tiles)
    return packed


def fetch(after_this, slab_any, monitor_any, slab_ref, monitor_ref, ready):
    copies = [
        pltpu.make_async_copy(slab_any, slab_ref, ready.at[0]),
        pltpu.make_async_copy(monitor_any, monitor_ref, ready.at[1]),
    ]
    for copy in copies:
        copy.start()
    for copy in copies:
        copy.wait()


def y_monitor(wave_ref, coef_ref, table_ref, own_ref, *refs):
    *spectra, out_ref, weights_ref = refs
    half = len(spectra) // 2
    spectra = spectra[half + 1 :] + spectra[:1] + spectra[1 : half + 1]
    blocks = len(spectra) + 1
    waves, _, records, rows, columns = spectra[0].shape
    me = lax.axis_index("gy")
    spectra = [own_ref.at[pl.ds(me * waves, waves)]] + spectra
    total = None
    for block in range(blocks):
        owner = lax.rem(me + block, blocks)
        place = pl.ds(pl.multiple_of(owner * columns, columns), columns)
        parts = []
        for part in range(2):
            for w in range(waves):
                parts += [spectra[block][w, part, c] for c in range(records)]
        tables = [table_ref[i, place, :] for i in range(2)]
        total = split_dot(jnp.concatenate(parts, axis=0), tables, total)
    half = waves * records * rows
    real = total[:half, :OY] + total[half:, OY:]
    imag = total[half:, :OY] - total[:half, OY:]
    targets = out_ref.shape[0]
    for part, values in enumerate((real, imag)):
        packed = packed_orders(values, waves * records, OY // targets)
        for target in range(targets):
            for i, tile in enumerate(packed[target]):
                out_ref[target, pl.ds((i * 2 + part) * rows, rows), :] = tile
    kept = OY // targets
    lane = iota((rows, OY), 1)
    per_wave = RECORDS * kept
    per_tile = OY // per_wave
    for tile in range(weights_ref.shape[0] // (2 * STEPS)):
        some = range(tile * per_tile, min(waves, (tile + 1) * per_tile))
        coefs = [waves_of(coef_ref, wave_ref[me * waves + w]) for w in some]
        for s in range(STEPS):
            for part in range(2):
                weight = None
                for i, coef in enumerate(coefs):
                    for half in range(2):
                        value = jnp.full((rows, OY), coef(s, half, part), jnp.float32)
                        spot = i * per_wave + half * (per_wave // 2)
                        weight = value if weight is None else jnp.where(lane >= spot, value, weight)
                weights_ref[(tile * STEPS + s) * 2 + part] = weight


def y_records(waves, table_ref, monitor_ref, weights_ref, *refs):
    *messages, out_any, out_ref, done = refs
    messages = messages[::-1]
    blocks = len(messages)
    columns = messages[0].shape[1]
    targets, height, _ = out_ref.shape
    kept = OY // targets
    out_tiles = -(-waves * RECORDS * kept // OY)
    rows = height // (2 * out_tiles)
    me = lax.axis_index("gy")
    span = DEEP * SEAM
    per_tile = columns // span
    base = STEPS * RECORDS * rows
    column = iota((2 * rows, columns), 1) % SEAM
    edges = [pair_of_tiles(message, 0, rows) for message in messages]

    total = None
    for block in range(blocks):
        owner = lax.rem(me + block, blocks)
        place = pl.ds(pl.multiple_of(blocks * span + owner * columns, span), columns)
        values = messages[block][pl.ds(0, base), :]
        total = split_dot(values, [table_ref[part, place, :] for part in range(2)], total)
    for tile in range(-(-blocks // per_tile)):
        seams = range(tile * per_tile, min(blocks, (tile + 1) * per_tile))
        kinds = []
        for part in range(2):
            mixed = []
            for seam in list(seams) + [seams[0]] * (per_tile - len(seams)):
                here, after = edges[seam][part], edges[(seam + 1) % blocks][part]
                mixed.append(jnp.where(column < EDGE, here, after))
            kinds += blocks_transposed(mixed)
        walk = seam_leapfrog(kinds[:KINDS], DEEP)
        record = []
        for s in range(STEPS):
            record += [value[:rows] for value in walk.records(s + 1, 0)]
        values = jnp.concatenate(record, axis=0)[:, : len(seams) * span]
        owners = [lax.rem(me + seam, blocks) for seam in seams]
        places = [pl.ds(pl.multiple_of(owner * span, span), span) for owner in owners]
        tables = [
            jnp.concatenate([table_ref[part, place, :] for place in places], axis=0)
            for part in range(2)
        ]
        total = split_dot(values, tables, total)
    lane = iota((rows, OY), 1)
    per_wave = RECORDS * kept
    per_tile = OY // per_wave
    packed_parts = [
        packed_orders(total[:, part * OY : (part + 1) * OY], STEPS * RECORDS, kept)
        for part in range(2)
    ]
    copies = []
    for target in range(targets):
        spot = order_of(targets).index(target)
        sides = []
        for part in range(2):
            (packed,) = packed_parts[part][target]
            steps = []
            for s in range(STEPS):
                spread = None
                for i in range(min(per_tile, waves)):
                    here = rolled(packed, i * per_wave - s * per_wave, 1)
                    spread = here if i == 0 else jnp.where(lane >= i * per_wave, here, spread)
                steps.append(spread)
            sides.append(steps)
        for tile in range(out_tiles):
            for part in range(2):
                place = pl.ds((tile * 2 + part) * rows, rows)
                value = monitor_ref[target, place, :]
                for s in range(STEPS):
                    first = (tile * STEPS + s) * 2
                    real, imag = weights_ref[first], weights_ref[first + 1]
                    if part == 0:
                        value = value + (real * sides[0][s] - imag * sides[1][s])
                    else:
                        value = value + (imag * sides[0][s] + real * sides[1][s])
                out_ref[spot, place, :] = value
        copies.append(
            pltpu.make_async_copy(out_ref.at[spot], out_any.at[spot], done.at[spot])
        )
        copies[-1].start()
    for copy in copies:
        copy.wait()


def x_orders(kept, values_ref, table_ref, out_ref):
    sources, height, lanes = values_ref.shape
    waves, _, records, _, _ = out_ref.shape
    depth = table_ref.shape[1]
    rows = depth // sources
    per_tile = lanes // kept
    for tile in range(height // rows):
        values = jnp.concatenate(
            [values_ref[source, pl.ds(tile * rows, rows), :] for source in range(sources)], axis=0
        )
        result = split_dot(values, [table_ref[0], table_ref[1]], None, ((0,), (0,)))
        for place in range(per_tile):
            wave, record = divmod(tile * per_tile + place, records)
            if wave < waves:
                here = result[place * kept : (place + 1) * kept]
                out_ref[wave, 0, record] = here[:, :OX]
                out_ref[wave, 1, record] = here[:, OX:]


def local_updates(
    perm_ref,
    wave_ref,
    coef_ref,
    e_ref,
    h_ref,
    m_ref,
    same_ref,
    cross_ref,
    edges_ref,
    message_after_ref,
    message_before_ref,
    slab_ref,
    monitor_ref,
    e_any,
    h_any,
    slab_out_any,
    monitor_out_any,
    e_out,
    h_out,
    slab_out,
    monitor_out,
    done,
):
    layers, rows, columns = m_ref.shape
    rates = rates_of(perm_ref, perm_ref.shape[0], (rows, columns))
    wide = widened_planes(own_planes(e_ref, h_ref, m_ref, rates), same_ref, cross_ref)
    walk = Leapfrog(wide, layers=layers)
    left = iota((2 * rows, layers * SEAM), 1) % SEAM < EDGE
    last = pair_of_tiles(message_before_ref, 1, rows)
    first = pair_of_tiles(message_after_ref, 1, rows)
    before, after = [], []
    for kind in range(KINDS):
        mine = edges_ref[kind]
        tile, spot = divmod(kind, OUTER)
        from_before = rolled(last[tile], STEPS - spot * STEPS, 1)
        from_after = rolled(first[tile], EDGE - spot * STEPS, 1)
        before.append(jnp.where(left, from_before, mine))
        after.append(jnp.where(left, mine, from_after))
    before = seam_leapfrog(before, layers)
    after = seam_leapfrog(after, layers)
    column = iota((rows, columns), 1)
    inner = (column >= STEPS) & (column < columns - STEPS)
    joined = {}

    def mended(s, z, kind):
        if (s, kind) not in joined:
            ends = [(side.e(s, 0) + side.h(s, 0))[kind][:rows] for side in (after, before)]
            joined[s, kind] = jnp.where(left[:rows], ends[0], ends[1])
        value = (walk.e(s, z) + walk.h(s, z))[kind][:rows]
        return jnp.where(inner, value, rolled(joined[s, kind], -(z * SEAM + EDGE), 1))

    middle = layers // 2
    slab_records = [[None] * 2 for _ in range(STEPS)]
    records = [[None] * RECORDS for _ in range(STEPS)]
    for z in range(layers):
        for kind in range(6):
            value = mended(STEPS, z, kind)
            if kind < 3:
                e_out[kind, z] = value
            else:
                h_out[kind - 3, z] = value
        for s in range(STEPS):
            if z == middle:
                slab_records[s] = [mended(s + 1, z, kind) for kind in (0, 1)]
            if z == layers - 1:
                records[s] = [mended(s + 1, z, kind) for kind in (0, 1, 3, 4)]
    sent = [
        pltpu.make_async_copy(e_out, e_any, done.at[0]),
        pltpu.make_async_copy(h_out, h_any, done.at[1]),
    ]
    for copy in sent:
        copy.start()
    frequencies = slab_ref.shape[1] // 2

    def one_frequency(f, carry):
        coef = waves_of(coef_ref, f)
        for c in range(2):
            for part in range(2):
                value = slab_ref[c, part * frequencies + f]
                for s in range(STEPS):
                    value = value + coef(s, 0, part) * slab_records[s][c]
                slab_out[c, part * frequencies + f] = value
        return carry

    lax.fori_loop(0, frequencies, one_frequency, 0, unroll=4)
    sent.append(pltpu.make_async_copy(slab_out, slab_out_any, done.at[2]))
    sent[-1].start()
    for w in range(monitor_ref.shape[0]):
        coef = waves_of(coef_ref, wave_ref[w])
        for part in range(2):
            for c in range(RECORDS):
                value = monitor_ref[w, part, c]
                for s in range(STEPS):
                    value = value + coef(s, c // 2, part) * records[s][c]
                monitor_out[w, part, c] = value
    sent.append(pltpu.make_async_copy(monitor_out, monitor_out_any, done.at[3]))
    sent[-1].start()
    for copy in sent:
        copy.wait()


def wave_coefficients(freq_count):
    omegas = OMEGA_LOW + (OMEGA_HIGH - OMEGA_LOW) * np.arange(freq_count) / (freq_count - 1)
    times = TIME_STEP * (np.arange(1, STEPS + 1)[:, None] - np.array([0.0, 0.5])[None, :])
    angles = omegas[:, None, None] * times[None]
    table = np.stack([TIME_STEP * np.cos(angles), -TIME_STEP * np.sin(angles)], axis=-1)
    return table.reshape(-1).astype(np.float32)


def angles_of(length, kept):
    wanted = (np.arange(kept) - kept // 2) % length
    return 2.0 * math.pi / length * (np.arange(length)[:, None] * wanted[None, :] % length)


def y_table(length):
    angles = angles_of(length, OY)
    return split_table(np.concatenate([np.cos(angles), np.sin(angles)], axis=1))


def split_table(table):
    table = table.astype(np.float32)
    coarse = table.astype(ml_dtypes.bfloat16)
    fine = (table - coarse.astype(np.float32)).astype(ml_dtypes.bfloat16)
    return jnp.asarray(np.stack([coarse, fine]))


def record_table(length, blocks):
    angles = angles_of(length, OY)
    table = np.concatenate([np.cos(angles), -np.sin(angles)], axis=1)
    columns = length // blocks
    seams = np.zeros((blocks, DEEP, SEAM, 2 * OY))
    for block in range(blocks):
        for column in range(-STEPS, STEPS):
            row = ((block + 1) * columns + column) % length
            seams[block, DEEP - 1, EDGE + column] = table[row]
    inner = table.copy()
    place = np.arange(length) % columns
    inner[(place < STEPS) | (place >= columns - STEPS)] = 0.0
    return split_table(np.concatenate([seams.reshape(-1, 2 * OY), inner]))


def order_of(blocks):
    return list(reversed(range(blocks)))


def x_table(length, blocks, scaling):
    angles = angles_of(length, OX).reshape(blocks, length // blocks, OX)[order_of(blocks)]
    real = np.concatenate([np.cos(angles), -np.sin(angles)], axis=2)
    imag = np.concatenate([np.sin(angles), np.cos(angles)], axis=2)
    table = np.stack([real, imag], axis=1) * scaling
    return split_table(table.reshape(2 * length, 2 * OX))


def call(kernel, in_specs, shapes, *operands, name, flops=0, moved=0, **more):
    kind = jax.ShapeDtypeStruct
    out = [kind(shape, jnp.float32) for shape in shapes]
    return pl.pallas_call(
        kernel,
        out_shape=out,
        in_specs=in_specs,
        out_specs=more.pop("out_specs", [VMEM] * len(out)),
        compiler_params=PARAMS,
        cost_estimate=pl.CostEstimate(flops=flops, bytes_accessed=moved, transcendentals=0),
        name=name,
        **more,
    )(*operands)


def per_device(
    electric, magnetic, material, permittivity, slab_spectra, monitor_spectra, wave_index
):
    layers, rows, columns = material.shape
    x_blocks, y_blocks = lax.axis_size("gx"), lax.axis_size("gy")
    waves = monitor_spectra.shape[0]
    group_waves = waves // y_blocks
    fields = (electric, magnetic, material)
    groups = layers * STEPS // rows

    faces = (KINDS, groups, rows, columns)
    block = (group_waves,) + monitor_spectra.shape[1:]
    late = []
    early = [distance for distance in range(1, y_blocks) if distance not in late]
    same, cross, *blocks = call(
        functools.partial(pack_faces, early + late),
        [HBM] * 5,
        [faces, faces] + [block] * (y_blocks - 1),
        *[in_hbm(array) for array in (permittivity, *fields, monitor_spectra)],
        name="pack_faces",
        flops=10**5,
        moved=10**6,
        scratch_shapes=[
            pltpu.SMEM(permittivity.shape, jnp.float32),
            pltpu.VMEM(electric.shape, jnp.float32),
            pltpu.VMEM(magnetic.shape, jnp.float32),
            pltpu.VMEM(material.shape, jnp.int32),
            pltpu.SemaphoreType.DMA((4,)),
            pltpu.SemaphoreType.DMA((y_blocks - 1,)),
        ],
    )
    line = range(x_blocks)
    same = lax.ppermute(same, "gx", [(i, i ^ 1) for i in line])
    cross = lax.ppermute(cross, "gx", [(i, (i + (1 if i % 2 else -1)) % x_blocks) for i in line])
    spectra = {
        distance: passed_along(block, "gy", -distance) for distance, block in zip(early, blocks)
    }
    held_back = blocks[len(early) :]

    far_height = (STEPS * RECORDS + 3) * rows
    near_height = far_height + 3 * rows
    forth, back, far, edges, *blocks = call(
        monitor_message,
        [SMEM] + [VMEM] * 5,
        [
            (near_height, columns),
            (near_height, columns),
            (far_height, columns),
            (KINDS, 2 * rows, layers * SEAM),
        ]
        + [block] * len(late),
        permittivity,
        *fields,
        same,
        cross,
        *held_back,
        name="monitor_message",
        flops=1,
        moved=1,
    )
    message_before = passed_along(forth, "gy", 1)
    message_after = passed_along(back, "gy", -1)
    for distance, block in zip(late, blocks):
        spectra[distance] = passed_along(block, "gy", -distance)
    messages = [far, message_after]
    for distance in range(2, y_blocks - 1):
        messages.append(passed_along(far, "gy", -distance))
    messages = (messages + [message_before])[:y_blocks]

    coefs = jnp.asarray(wave_coefficients(slab_spectra.shape[1] // 2))
    length_x, length_y = rows * x_blocks, columns * y_blocks
    kept = OY // x_blocks
    out_tiles = -(-group_waves * RECORDS * kept // OY)
    sums_y = y_table(length_y)
    slab_here, monitor_here = call(
        fetch,
        [ANY] + [HBM] * 2,
        [slab_spectra.shape, monitor_spectra.shape],
        far,
        in_hbm(slab_spectra),
        in_hbm(monitor_spectra),
        name="fetch",
        flops=1,
        moved=3 * 10**6,
        scratch_shapes=[pltpu.SemaphoreType.DMA((2,))],
    )
    monitor_y, weights = call(
        y_monitor,
        [SMEM] * 2 + [VMEM] * (1 + y_blocks),
        [(x_blocks, out_tiles * 2 * rows, OY), (out_tiles * STEPS * 2, rows, OY)],
        wave_index,
        coefs,
        sums_y,
        monitor_here,
        *[spectra[distance] for distance in [y_blocks // 2] + list(range(y_blocks // 2 + 1, y_blocks)) + list(range(1, y_blocks // 2))],
        name="y_monitor",
        flops=10**8,
        moved=2 * 10**6,
    )
    (spectrum_y,) = call(
        functools.partial(y_records, group_waves),
        [VMEM] * (3 + y_blocks),
        [monitor_y.shape],
        record_table(length_y, y_blocks),
        monitor_y,
        weights,
        *messages[::-1],
        out_specs=[HBM],
        scratch_shapes=[
            pltpu.VMEM(monitor_y.shape, jnp.float32),
            pltpu.SemaphoreType.DMA((x_blocks,)),
        ],
        name="y_records",
        flops=10**8,
        moved=2 * 10**6,
    )
    members = [
        [x * y_blocks + y for x in order_of(x_blocks)] for y in range(y_blocks)
    ]
    swapped = lax.all_to_all(
        spectrum_y, ("gx", "gy"), split_axis=0, concat_axis=0, axis_index_groups=members, tiled=True
    )

    electric_next, magnetic_next, slab_next, monitor_next = call(
        local_updates,
        [SMEM] * 3 + [VMEM] * 10,
        [electric.shape, magnetic.shape, slab_spectra.shape, monitor_spectra.shape],
        permittivity,
        wave_index,
        coefs,
        *fields,
        same,
        cross,
        edges,
        message_after,
        message_before,
        slab_here,
        monitor_here,
        name="local_updates",
        scratch_shapes=[
            pltpu.VMEM(electric.shape, jnp.float32),
            pltpu.VMEM(magnetic.shape, jnp.float32),
            pltpu.VMEM(slab_spectra.shape, jnp.float32),
            pltpu.VMEM(monitor_spectra.shape, jnp.float32),
            pltpu.SemaphoreType.DMA((4,)),
        ],
        out_specs=[HBM] * 4,
        flops=10**7,
        moved=6 * 10**6,
    )

    scaling = 1.0 / math.sqrt(length_x * length_y)
    (orders,) = call(
        functools.partial(x_orders, kept),
        [VMEM] * 2,
        [(group_waves, 2, RECORDS, kept, OX)],
        swapped,
        x_table(length_x, x_blocks, scaling),
        name="x_orders",
        flops=10**7,
        moved=5 * 10**5,
    )
    return (electric_next, magnetic_next, slab_next, monitor_next, orders)


def solution(mesh):
    in_specs = (
        P(None, None, "gx", "gy"),
        P(None, None, "gx", "gy"),
        P(None, "gx", "gy"),
        P(),
        P(None, None, "gx", "gy"),
        P(None, None, None, "gx", "gy"),
        P(),
    )
    out_specs = (
        P(None, None, "gx", "gy"),
        P(None, None, "gx", "gy"),
        P(None, None, "gx", "gy"),
        P(None, None, None, "gx", "gy"),
        P("gy", None, None, "gx", None),
    )
    return jax.shard_map(
        per_device, mesh=mesh, in_specs=in_specs, out_specs=out_specs, check_vma=False
    )
```

```python
import functools
import math

import jax
import jax.numpy as jnp
import ml_dtypes
import numpy as np
from jax import lax
from jax.experimental import pallas as pl
from jax.experimental.pallas import tpu as pltpu
from jax.sharding import PartitionSpec as P

OY = 128
OX = 64

TIME_STEP = 0.5
OMEGA_LOW = 0.15
OMEGA_HIGH = 0.8

STEPS = 2
EDGE = 2 * STEPS
SEAM = 2 * EDGE
DEEP = 4
OUTER = SEAM // STEPS
KINDS = 7
RECORDS = 4

VMEM = pl.BlockSpec(memory_space=pltpu.VMEM)
HBM = pl.BlockSpec(memory_space=pltpu.HBM)
ANY = pl.BlockSpec(memory_space=pl.ANY)
SMEM = pl.BlockSpec(memory_space=pltpu.SMEM)
PARAMS = pltpu.CompilerParams(vmem_limit_bytes=48 * 1024 * 1024)


def in_hbm(array):
    return pltpu.with_memory_space_constraint(array, pltpu.HBM)


def passed_along(block, axis, distance):
    devices = range(lax.axis_size(axis))
    route = [((i - distance) % len(devices), i) for i in devices]
    return lax.ppermute(block, axis, route)


def rolled(values, shift, axis):
    shift %= values.shape[axis]
    return pltpu.roll(values, shift, axis) if shift else values


def iota(shape, axis):
    return lax.broadcasted_iota(jnp.int32, shape, axis)


def rates_of(permittivity, classes, shape):
    return [TIME_STEP / jnp.full(shape, permittivity[k], jnp.float32) for k in range(classes)]


def rate_at(material, rates):
    rate = rates[-1]
    for k in range(len(rates) - 2, -1, -1):
        rate = jnp.where(material == k, rates[k], rate)
    return rate


class Leapfrog:
    def __init__(self, start, layers=None, above=None, below=None):
        self.start = start
        self.layers = layers
        self.above = above
        self.below = below
        self.known = {}

    def first(self, z):
        if ("0", z) not in self.known:
            self.known["0", z] = self.start(z)
        return self.known["0", z]

    def e(self, s, z):
        if s == 0:
            return self.first(z)[0:3]
        if ("e", s, z) not in self.known:
            ex, ey, ez = self.e(s - 1, z)
            hx, hy, hz = self.h(s, z)
            if self.layers is None:
                down_x, down_y = self.below(hx), self.below(hy)
            else:
                down_x, down_y = self.h(s, z - 1)[:2] if z else (0.0, 0.0)
            rate = self.first(z)[6]
            self.known["e", s, z] = (
                ex + rate * ((hz - rolled(hz, 1, 1)) - (hy - down_y)),
                ey + rate * ((hx - down_x) - (hz - rolled(hz, 1, 0))),
                ez + rate * ((hy - rolled(hy, 1, 0)) - (hx - rolled(hx, 1, 1))),
            )
        return self.known["e", s, z]

    def h(self, s, z):
        if s == 0:
            return self.first(z)[3:6]
        if ("h", s, z) not in self.known:
            ex, ey, ez = self.e(s - 1, z)
            hx, hy, hz = self.h(s - 1, z)
            if self.layers is None:
                up_x, up_y = self.above(ex), self.above(ey)
            else:
                up_x, up_y = self.e(s - 1, z + 1)[:2] if z + 1 < self.layers else (0.0, 0.0)
            self.known["h", s, z] = (
                hx - TIME_STEP * ((rolled(ez, -1, 1) - ez) - (up_y - ey)),
                hy - TIME_STEP * ((up_x - ex) - (rolled(ez, -1, 0) - ez)),
                hz - TIME_STEP * ((rolled(ey, -1, 0) - ey) - (rolled(ex, -1, 1) - ex)),
            )
        return self.known["h", s, z]

    def records(self, s, z):
        return self.e(s, z)[:2] + self.h(s, z)[:2]


def seam_leapfrog(tiles, layers):
    layer = iota(tiles[0].shape, 1) // SEAM % layers
    return Leapfrog(
        lambda z: tiles,
        above=lambda f: jnp.where(layer < layers - 1, rolled(f, -SEAM, 1), 0.0),
        below=lambda f: jnp.where(layer > 0, rolled(f, SEAM, 1), 0.0),
    )


def own_planes(e_ref, h_ref, m_ref, rates):
    def at(z):
        rate = rate_at(m_ref[z], rates)
        return [e_ref[c, z] for c in range(3)] + [h_ref[c, z] for c in range(3)] + [rate]

    return at


def widened_planes(own, same_ref, cross_ref):
    even = lax.rem(lax.axis_index("gx"), 2) == 0

    def at(z):
        planes = own(z)
        rows = planes[0].shape[0]
        group, place = divmod(z, rows // STEPS)
        row = iota(planes[0].shape, 0)
        wide = []
        for kind in range(KINDS):
            same, cross = same_ref[kind, group], cross_ref[kind, group]
            after = rolled(jnp.where(even, same, cross), -STEPS * place, 0)
            before = rolled(jnp.where(even, cross, same), rows - STEPS - STEPS * place, 0)
            halo = jnp.where(row < STEPS, after, before)
            wide.append(jnp.concatenate([planes[kind], halo], axis=0))
        return wide

    return at


def block_copy(distance, spectra_any, block_ref, semaphore):
    waves = block_ref.shape[0]
    blocks = spectra_any.shape[0] // waves
    owner = lax.rem(lax.axis_index("gy") + blocks - distance, blocks)
    source = spectra_any.at[pl.ds(owner * waves, waves)]
    return pltpu.make_async_copy(source, block_ref, semaphore)


def other_blocks(distances, after_this, spectra_any, *refs):
    *block_refs, sent = refs
    copies = [
        block_copy(distance, spectra_any, block_ref, sent.at[i])
        for i, (distance, block_ref) in enumerate(zip(distances, block_refs))
    ]
    for copy in copies:
        copy.start()
    for copy in copies:
        copy.wait()


def pack_faces(
    distances,
    perm_any,
    e_any,
    h_any,
    m_any,
    spectra_any,
    same_ref,
    cross_ref,
    *refs,
):
    even = lax.rem(lax.axis_index("gx"), 2) == 0
    *block_refs, perm_ref, e_ref, h_ref, m_ref, ready, sent = refs
    sources, targets = (e_any, h_any, m_any, perm_any), (e_ref, h_ref, m_ref, perm_ref)
    copies = [
        pltpu.make_async_copy(source, target, ready.at[i])
        for i, (source, target) in enumerate(zip(sources, targets))
    ]
    for i, (distance, block_ref) in enumerate(zip(distances, block_refs)):
        copies.append(block_copy(distance, spectra_any, block_ref, sent.at[i]))
    for copy in copies:
        copy.start()
    for copy in copies[:4]:
        copy.wait()
    layers, rows, columns = m_ref.shape
    rates = rates_of(perm_ref, perm_ref.shape[0], (rows, columns))
    own = own_planes(e_ref, h_ref, m_ref, rates)
    row = iota((rows, columns), 0)
    per_group = rows // STEPS
    for group in range(layers // per_group):
        planes = [own(group * per_group + place) for place in range(per_group)]
        for kind in range(KINDS):
            forth = rolled(planes[0][kind], STEPS - rows, 0)
            back = planes[0][kind]
            for place in range(1, per_group):
                spot = STEPS * place
                here = planes[place][kind]
                forth = jnp.where(row >= spot, rolled(here, spot + STEPS - rows, 0), forth)
                back = jnp.where(row >= spot, rolled(here, spot, 0), back)
            same_ref[kind, group] = jnp.where(even, forth, back)
            cross_ref[kind, group] = jnp.where(even, back, forth)
    for copy in copies[4:]:
        copy.wait()


def blocks_transposed(tiles):
    tiles = list(tiles)
    count = len(tiles)
    width = tiles[0].shape[1] // count
    block = iota(tiles[0].shape, 1) // width
    bit = 1
    while bit < count:
        low = (block & bit) == 0
        for i in range(count):
            if not i & bit:
                first, second = tiles[i], tiles[i + bit]
                tiles[i] = jnp.where(low, first, rolled(second, bit * width, 1))
                tiles[i + bit] = jnp.where(low, rolled(first, -bit * width, 1), second)
        bit *= 2
    return tiles


def packed_edges(planes, layers, spot):
    tile = None
    for z in range(layers):
        here = rolled(planes[z], spot + z * SEAM + EDGE, 1)
        if tile is None:
            tile = here
        else:
            tile = jnp.where(iota(tile.shape, 1) >= spot + z * SEAM, here, tile)
    return tile


def squeezed(first, second):
    rows = first.shape[0] // 2
    row = iota((rows, first.shape[1]), 0)
    ends = (row < STEPS) | (row >= rows - STEPS)
    second_halo = second[rows:]
    moved = jnp.where(
        row < 2 * STEPS, rolled(second_halo, STEPS, 0), rolled(second_halo, -STEPS, 0)
    )
    return first[:rows], second[:rows], jnp.where(ends, first[rows:], moved)


def stretched(first, second, halo):
    rows = first.shape[0]
    row = iota(halo.shape, 0)
    moved = jnp.where(row < 2 * STEPS, rolled(halo, -STEPS, 0), rolled(halo, STEPS, 0))
    return jnp.concatenate([first, halo], axis=0), jnp.concatenate([second, moved], axis=0)


def pair_of_tiles(ref, pair, rows):
    base = (STEPS * RECORDS + 3 * pair) * rows
    return stretched(*[ref[pl.ds(base + i * rows, rows), :] for i in range(3)])


def monitor_message(
    perm_ref,
    e_ref,
    h_ref,
    m_ref,
    same_ref,
    cross_ref,
    forth_ref,
    back_ref,
    far_ref,
    edges_ref,
):
    layers, rows, columns = m_ref.shape
    rates = rates_of(perm_ref, perm_ref.shape[0], (rows, columns))
    wide = widened_planes(own_planes(e_ref, h_ref, m_ref, rates), same_ref, cross_ref)
    low = layers - DEEP
    walk = Leapfrog(lambda z: wide(low + z), layers=DEEP)
    for s in range(STEPS):
        for c, record in enumerate(walk.records(s + 1, DEEP - 1)):
            place = pl.ds((s * RECORDS + c) * rows, rows)
            for ref in (forth_ref, back_ref, far_ref):
                ref[place, :] = record[:rows]
    planes = [wide(z) for z in range(low)] + [walk.first(z) for z in range(DEEP)]
    span = DEEP * SEAM
    per_tile = columns // span
    tops, lasts, firsts = ([None, None] for _ in range(3))
    for kind in range(KINDS):
        edges = packed_edges([planes[z][kind] for z in range(layers)], layers, 0)
        edges_ref[kind] = edges
        lane = iota(edges.shape, 1)
        tile, spot = divmod(kind, per_tile)
        here = rolled(edges, spot * span - low * SEAM, 1)
        tops[tile] = jnp.where(lane >= spot * span, here, tops[tile]) if spot else here
        tile, spot = divmod(kind, OUTER)
        for tiles, shift in ((lasts, STEPS), (firsts, EDGE)):
            here = rolled(edges, spot * STEPS - shift, 1)
            tiles[tile] = jnp.where(lane % SEAM >= spot * STEPS, here, tiles[tile]) if spot else here
    base = STEPS * RECORDS * rows
    for i, part in enumerate(squeezed(*tops)):
        for ref in (forth_ref, back_ref, far_ref):
            ref[pl.ds(base + i * rows, rows), :] = part
    for ref, tiles in ((forth_ref, lasts), (back_ref, firsts)):
        for i, part in enumerate(squeezed(*tiles)):
            ref[pl.ds(base + (3 + i) * rows, rows), :] = part


def waves_of(coef_ref, wave):
    base = wave * (STEPS * 4)
    return lambda s, half, part: coef_ref[base + (s * 2 + half) * 2 + part]


def exact_dot(left, right, contracted):
    return lax.dot_general(
        left,
        right,
        (contracted, ((), ())),
        precision=lax.Precision.HIGHEST,
        preferred_element_type=jnp.float32,
    )


def split_dot(values, tables, total, contracted=((1,), (0,))):
    coarse = values.astype(jnp.bfloat16)
    fine = (values - coarse.astype(jnp.float32)).astype(jnp.bfloat16)
    for left, right in ((coarse, tables[0]), (fine, tables[0]), (coarse, tables[1])):
        product = lax.dot_general(
            left, right, (contracted, ((), ())), preferred_element_type=jnp.float32
        )
        total = product if total is None else total + product
    return total


def packed_orders(values, planes, kept):
    rows = values.shape[0] // planes
    parts = [values[plane * rows : (plane + 1) * rows] for plane in range(planes)]
    targets = per_tile = OY // kept
    if planes % per_tile == 0 and not targets & (targets - 1):
        groups = [parts[i : i + per_tile] for i in range(0, planes, per_tile)]
        return list(zip(*[blocks_transposed(group) for group in groups]))
    lane = iota((rows, OY), 1)
    packed = []
    for target in range(targets):
        tiles = []
        for first in range(0, planes, per_tile):
            tile = None
            for plane in range(first, min(planes, first + per_tile)):
                spot = (plane - first) * kept
                here = rolled(parts[plane], spot - target * kept, 1)
                tile = here if tile is None else jnp.where(lane >= spot, here, tile)
            tiles.append(tile)
        packed.append(tiles)
    return packed


def fetch(after_this, slab_any, monitor_any, slab_ref, monitor_ref, ready):
    copies = [
        pltpu.make_async_copy(slab_any, slab_ref, ready.at[0]),
        pltpu.make_async_copy(monitor_any, monitor_ref, ready.at[1]),
    ]
    for copy in copies:
        copy.start()
    for copy in copies:
        copy.wait()


def y_monitor(wave_ref, coef_ref, table_ref, own_ref, *refs):
    *spectra, out_ref, weights_ref = refs
    half = len(spectra) // 2
    spectra = spectra[half + 1 :] + spectra[:1] + spectra[1 : half + 1]
    blocks = len(spectra) + 1
    waves, _, records, rows, columns = spectra[0].shape
    me = lax.axis_index("gy")
    spectra = [own_ref.at[pl.ds(me * waves, waves)]] + spectra
    total = None
    for block in range(blocks):
        owner = lax.rem(me + block, blocks)
        place = pl.ds(pl.multiple_of(owner * columns, columns), columns)
        parts = []
        for part in range(2):
            for w in range(waves):
                parts += [spectra[block][w, part, c] for c in range(records)]
        tables = [table_ref[i, place, :] for i in range(2)]
        total = split_dot(jnp.concatenate(parts, axis=0), tables, total)
    half = waves * records * rows
    real = total[:half, :OY] + total[half:, OY:]
    imag = total[half:, :OY] - total[:half, OY:]
    targets = out_ref.shape[0]
    for part, values in enumerate((real, imag)):
        packed = packed_orders(values, waves * records, OY // targets)
        for target in range(targets):
            for i, tile in enumerate(packed[target]):
                out_ref[target, pl.ds((i * 2 + part) * rows, rows), :] = tile
    kept = OY // targets
    lane = iota((rows, OY), 1)
    per_wave = RECORDS * kept
    per_tile = OY // per_wave
    for tile in range(weights_ref.shape[0] // (2 * STEPS)):
        some = range(tile * per_tile, min(waves, (tile + 1) * per_tile))
        coefs = [waves_of(coef_ref, wave_ref[me * waves + w]) for w in some]
        for s in range(STEPS):
            for part in range(2):
                weight = None
                for i, coef in enumerate(coefs):
                    for half in range(2):
                        value = jnp.full((rows, OY), coef(s, half, part), jnp.float32)
                        spot = i * per_wave + half * (per_wave // 2)
                        weight = value if weight is None else jnp.where(lane >= spot, value, weight)
                weights_ref[(tile * STEPS + s) * 2 + part] = weight


def y_records(waves, table_ref, monitor_ref, weights_ref, *refs):
    *messages, out_any, out_ref, done = refs
    messages = messages[::-1]
    blocks = len(messages)
    columns = messages[0].shape[1]
    targets, height, _ = out_ref.shape
    kept = OY // targets
    out_tiles = -(-waves * RECORDS * kept // OY)
    rows = height // (2 * out_tiles)
    me = lax.axis_index("gy")
    span = DEEP * SEAM
    per_tile = columns // span
    base = STEPS * RECORDS * rows
    column = iota((2 * rows, columns), 1) % SEAM
    edges = [pair_of_tiles(message, 0, rows) for message in messages]

    total = None
    for block in range(blocks):
        owner = lax.rem(me + block, blocks)
        place = pl.ds(pl.multiple_of(blocks * span + owner * columns, span), columns)
        values = messages[block][pl.ds(0, base), :]
        total = split_dot(values, [table_ref[part, place, :] for part in range(2)], total)
    for tile in range(-(-blocks // per_tile)):
        seams = range(tile * per_tile, min(blocks, (tile + 1) * per_tile))
        kinds = []
        for part in range(2):
            mixed = []
            for seam in list(seams) + [seams[0]] * (per_tile - len(seams)):
                here, after = edges[seam][part], edges[(seam + 1) % blocks][part]
                mixed.append(jnp.where(column < EDGE, here, after))
            kinds += blocks_transposed(mixed)
        walk = seam_leapfrog(kinds[:KINDS], DEEP)
        record = []
        for s in range(STEPS):
            record += [value[:rows] for value in walk.records(s + 1, 0)]
        values = jnp.concatenate(record, axis=0)[:, : len(seams) * span]
        owners = [lax.rem(me + seam, blocks) for seam in seams]
        places = [pl.ds(pl.multiple_of(owner * span, span), span) for owner in owners]
        tables = [
            jnp.concatenate([table_ref[part, place, :] for place in places], axis=0)
            for part in range(2)
        ]
        total = split_dot(values, tables, total)
    lane = iota((rows, OY), 1)
    per_wave = RECORDS * kept
    per_tile = OY // per_wave
    packed_parts = [
        packed_orders(total[:, part * OY : (part + 1) * OY], STEPS * RECORDS, kept)
        for part in range(2)
    ]
    copies = []
    for target in range(targets):
        spot = order_of(targets).index(target)
        sides = []
        for part in range(2):
            (packed,) = packed_parts[part][target]
            steps = []
            for s in range(STEPS):
                spread = None
                for i in range(min(per_tile, waves)):
                    here = rolled(packed, i * per_wave - s * per_wave, 1)
                    spread = here if i == 0 else jnp.where(lane >= i * per_wave, here, spread)
                steps.append(spread)
            sides.append(steps)
        for tile in range(out_tiles):
            for part in range(2):
                place = pl.ds((tile * 2 + part) * rows, rows)
                value = monitor_ref[target, place, :]
                for s in range(STEPS):
                    first = (tile * STEPS + s) * 2
                    real, imag = weights_ref[first], weights_ref[first + 1]
                    if part == 0:
                        value = value + (real * sides[0][s] - imag * sides[1][s])
                    else:
                        value = value + (imag * sides[0][s] + real * sides[1][s])
                out_ref[spot, place, :] = value
        copies.append(
            pltpu.make_async_copy(out_ref.at[spot], out_any.at[spot], done.at[spot])
        )
        copies[-1].start()
    for copy in copies:
        copy.wait()


def x_orders(kept, values_ref, table_ref, out_ref):
    sources, height, lanes = values_ref.shape
    waves, _, records, _, _ = out_ref.shape
    depth = table_ref.shape[1]
    rows = depth // sources
    per_tile = lanes // kept
    for tile in range(height // rows):
        values = jnp.concatenate(
            [values_ref[source, pl.ds(tile * rows, rows), :] for source in range(sources)], axis=0
        )
        result = split_dot(values, [table_ref[0], table_ref[1]], None, ((0,), (0,)))
        for place in range(per_tile):
            wave, record = divmod(tile * per_tile + place, records)
            if wave < waves:
                here = result[place * kept : (place + 1) * kept]
                out_ref[wave, 0, record] = here[:, :OX]
                out_ref[wave, 1, record] = here[:, OX:]


def local_updates(
    perm_ref,
    wave_ref,
    coef_ref,
    e_ref,
    h_ref,
    m_ref,
    same_ref,
    cross_ref,
    edges_ref,
    message_after_ref,
    message_before_ref,
    slab_ref,
    monitor_ref,
    e_any,
    h_any,
    slab_out_any,
    monitor_out_any,
    e_out,
    h_out,
    slab_out,
    monitor_out,
    done,
):
    layers, rows, columns = m_ref.shape
    rates = rates_of(perm_ref, perm_ref.shape[0], (rows, columns))
    wide = widened_planes(own_planes(e_ref, h_ref, m_ref, rates), same_ref, cross_ref)
    walk = Leapfrog(wide, layers=layers)
    left = iota((2 * rows, layers * SEAM), 1) % SEAM < EDGE
    last = pair_of_tiles(message_before_ref, 1, rows)
    first = pair_of_tiles(message_after_ref, 1, rows)
    before, after = [], []
    for kind in range(KINDS):
        mine = edges_ref[kind]
        tile, spot = divmod(kind, OUTER)
        from_before = rolled(last[tile], STEPS - spot * STEPS, 1)
        from_after = rolled(first[tile], EDGE - spot * STEPS, 1)
        before.append(jnp.where(left, from_before, mine))
        after.append(jnp.where(left, mine, from_after))
    before = seam_leapfrog(before, layers)
    after = seam_leapfrog(after, layers)
    column = iota((rows, columns), 1)
    inner = (column >= STEPS) & (column < columns - STEPS)
    joined = {}

    def mended(s, z, kind):
        if (s, kind) not in joined:
            ends = [(side.e(s, 0) + side.h(s, 0))[kind][:rows] for side in (after, before)]
            joined[s, kind] = jnp.where(left[:rows], ends[0], ends[1])
        value = (walk.e(s, z) + walk.h(s, z))[kind][:rows]
        return jnp.where(inner, value, rolled(joined[s, kind], -(z * SEAM + EDGE), 1))

    middle = layers // 2
    slab_records = [[None] * 2 for _ in range(STEPS)]
    records = [[None] * RECORDS for _ in range(STEPS)]
    for z in range(layers):
        for kind in range(6):
            value = mended(STEPS, z, kind)
            if kind < 3:
                e_out[kind, z] = value
            else:
                h_out[kind - 3, z] = value
        for s in range(STEPS):
            if z == middle:
                slab_records[s] = [mended(s + 1, z, kind) for kind in (0, 1)]
            if z == layers - 1:
                records[s] = [mended(s + 1, z, kind) for kind in (0, 1, 3, 4)]
    sent = [
        pltpu.make_async_copy(e_out, e_any, done.at[0]),
        pltpu.make_async_copy(h_out, h_any, done.at[1]),
    ]
    for copy in sent:
        copy.start()
    frequencies = slab_ref.shape[1] // 2

    def one_frequency(f, carry):
        coef = waves_of(coef_ref, f)
        for c in range(2):
            for part in range(2):
                value = slab_ref[c, part * frequencies + f]
                for s in range(STEPS):
                    value = value + coef(s, 0, part) * slab_records[s][c]
                slab_out[c, part * frequencies + f] = value
        return carry

    lax.fori_loop(0, frequencies, one_frequency, 0, unroll=4)
    sent.append(pltpu.make_async_copy(slab_out, slab_out_any, done.at[2]))
    sent[-1].start()
    for w in range(monitor_ref.shape[0]):
        coef = waves_of(coef_ref, wave_ref[w])
        for part in range(2):
            for c in range(RECORDS):
                value = monitor_ref[w, part, c]
                for s in range(STEPS):
                    value = value + coef(s, c // 2, part) * records[s][c]
                monitor_out[w, part, c] = value
    sent.append(pltpu.make_async_copy(monitor_out, monitor_out_any, done.at[3]))
    sent[-1].start()
    for copy in sent:
        copy.wait()


def wave_coefficients(freq_count):
    omegas = OMEGA_LOW + (OMEGA_HIGH - OMEGA_LOW) * np.arange(freq_count) / (freq_count - 1)
    times = TIME_STEP * (np.arange(1, STEPS + 1)[:, None] - np.array([0.0, 0.5])[None, :])
    angles = omegas[:, None, None] * times[None]
    table = np.stack([TIME_STEP * np.cos(angles), -TIME_STEP * np.sin(angles)], axis=-1)
    return table.reshape(-1).astype(np.float32)


def angles_of(length, kept):
    wanted = (np.arange(kept) - kept // 2) % length
    return 2.0 * math.pi / length * (np.arange(length)[:, None] * wanted[None, :] % length)


def y_table(length):
    angles = angles_of(length, OY)
    return split_table(np.concatenate([np.cos(angles), np.sin(angles)], axis=1))


def split_table(table):
    table = table.astype(np.float32)
    coarse = table.astype(ml_dtypes.bfloat16)
    fine = (table - coarse.astype(np.float32)).astype(ml_dtypes.bfloat16)
    return jnp.asarray(np.stack([coarse, fine]))


def record_table(length, blocks):
    angles = angles_of(length, OY)
    table = np.concatenate([np.cos(angles), -np.sin(angles)], axis=1)
    columns = length // blocks
    seams = np.zeros((blocks, DEEP, SEAM, 2 * OY))
    for block in range(blocks):
        for column in range(-STEPS, STEPS):
            row = ((block + 1) * columns + column) % length
            seams[block, DEEP - 1, EDGE + column] = table[row]
    inner = table.copy()
    place = np.arange(length) % columns
    inner[(place < STEPS) | (place >= columns - STEPS)] = 0.0
    return split_table(np.concatenate([seams.reshape(-1, 2 * OY), inner]))


def order_of(blocks):
    return list(reversed(range(blocks)))


def x_table(length, blocks, scaling):
    angles = angles_of(length, OX).reshape(blocks, length // blocks, OX)[order_of(blocks)]
    real = np.concatenate([np.cos(angles), -np.sin(angles)], axis=2)
    imag = np.concatenate([np.sin(angles), np.cos(angles)], axis=2)
    table = np.stack([real, imag], axis=1) * scaling
    return split_table(table.reshape(2 * length, 2 * OX))


def call(kernel, in_specs, shapes, *operands, name, flops=0, moved=0, **more):
    kind = jax.ShapeDtypeStruct
    out = [kind(shape, jnp.float32) for shape in shapes]
    return pl.pallas_call(
        kernel,
        out_shape=out,
        in_specs=in_specs,
        out_specs=more.pop("out_specs", [VMEM] * len(out)),
        compiler_params=PARAMS,
        cost_estimate=pl.CostEstimate(flops=flops, bytes_accessed=moved, transcendentals=0),
        name=name,
        **more,
    )(*operands)


def per_device(
    electric, magnetic, material, permittivity, slab_spectra, monitor_spectra, wave_index
):
    layers, rows, columns = material.shape
    x_blocks, y_blocks = lax.axis_size("gx"), lax.axis_size("gy")
    waves = monitor_spectra.shape[0]
    group_waves = waves // y_blocks
    fields = (electric, magnetic, material)
    groups = layers * STEPS // rows

    faces = (KINDS, groups, rows, columns)
    block = (group_waves,) + monitor_spectra.shape[1:]
    early = [y_blocks // 2]
    late = [distance for distance in range(1, y_blocks) if distance not in early]
    packed, cross, *blocks = call(
        functools.partial(pack_faces, early),
        [HBM] * 5,
        [faces, faces] + [block] * len(early),
        *[in_hbm(array) for array in (permittivity, *fields, monitor_spectra)],
        name="pack_faces",
        flops=10**5,
        moved=10**6,
        scratch_shapes=[
            pltpu.SMEM(permittivity.shape, jnp.float32),
            pltpu.VMEM(electric.shape, jnp.float32),
            pltpu.VMEM(magnetic.shape, jnp.float32),
            pltpu.VMEM(material.shape, jnp.int32),
            pltpu.SemaphoreType.DMA((4,)),
            pltpu.SemaphoreType.DMA((len(early),)),
        ],
    )
    line = range(x_blocks)
    same = lax.ppermute(packed, "gx", [(i, i ^ 1) for i in line])
    cross = lax.ppermute(cross, "gx", [(i, (i + (1 if i % 2 else -1)) % x_blocks) for i in line])
    spectra = {
        distance: passed_along(block, "gy", -distance) for distance, block in zip(early, blocks)
    }
    blocks = call(
        functools.partial(other_blocks, late),
        [ANY, HBM],
        [block] * len(late),
        packed,
        in_hbm(monitor_spectra),
        name="other_blocks",
        flops=1,
        moved=1,
        scratch_shapes=[pltpu.SemaphoreType.DMA((len(late),))],
    )
    for distance, block in zip(late, blocks):
        spectra[distance] = passed_along(block, "gy", -distance)

    far_height = (STEPS * RECORDS + 3) * rows
    near_height = far_height + 3 * rows
    forth, back, far, edges = call(
        monitor_message,
        [SMEM] + [VMEM] * 5,
        [
            (near_height, columns),
            (near_height, columns),
            (far_height, columns),
            (KINDS, 2 * rows, layers * SEAM),
        ],
        permittivity,
        *fields,
        same,
        cross,
        name="monitor_message",
        flops=1,
        moved=1,
    )
    message_before = passed_along(forth, "gy", 1)
    message_after = passed_along(back, "gy", -1)
    messages = [far, message_after]
    for distance in range(2, y_blocks - 1):
        messages.append(passed_along(far, "gy", -distance))
    messages = (messages + [message_before])[:y_blocks]

    coefs = jnp.asarray(wave_coefficients(slab_spectra.shape[1] // 2))
    length_x, length_y = rows * x_blocks, columns * y_blocks
    kept = OY // x_blocks
    out_tiles = -(-group_waves * RECORDS * kept // OY)
    sums_y = y_table(length_y)
    slab_here, monitor_here = call(
        fetch,
        [ANY] + [HBM] * 2,
        [slab_spectra.shape, monitor_spectra.shape],
        far,
        in_hbm(slab_spectra),
        in_hbm(monitor_spectra),
        name="fetch",
        flops=1,
        moved=3 * 10**6,
        scratch_shapes=[pltpu.SemaphoreType.DMA((2,))],
    )
    monitor_y, weights = call(
        y_monitor,
        [SMEM] * 2 + [VMEM] * (1 + y_blocks),
        [(x_blocks, out_tiles * 2 * rows, OY), (out_tiles * STEPS * 2, rows, OY)],
        wave_index,
        coefs,
        sums_y,
        monitor_here,
        *[spectra[distance] for distance in [y_blocks // 2] + list(range(y_blocks // 2 + 1, y_blocks)) + list(range(1, y_blocks // 2))],
        name="y_monitor",
        flops=10**8,
        moved=2 * 10**6,
    )
    (spectrum_y,) = call(
        functools.partial(y_records, group_waves),
        [VMEM] * (3 + y_blocks),
        [monitor_y.shape],
        record_table(length_y, y_blocks),
        monitor_y,
        weights,
        *messages[::-1],
        out_specs=[HBM],
        scratch_shapes=[
            pltpu.VMEM(monitor_y.shape, jnp.float32),
            pltpu.SemaphoreType.DMA((x_blocks,)),
        ],
        name="y_records",
        flops=10**8,
        moved=2 * 10**6,
    )
    members = [
        [x * y_blocks + y for x in order_of(x_blocks)] for y in range(y_blocks)
    ]
    swapped = lax.all_to_all(
        spectrum_y, ("gx", "gy"), split_axis=0, concat_axis=0, axis_index_groups=members, tiled=True
    )

    electric_next, magnetic_next, slab_next, monitor_next = call(
        local_updates,
        [SMEM] * 3 + [VMEM] * 10,
        [electric.shape, magnetic.shape, slab_spectra.shape, monitor_spectra.shape],
        permittivity,
        wave_index,
        coefs,
        *fields,
        same,
        cross,
        edges,
        message_after,
        message_before,
        slab_here,
        monitor_here,
        name="local_updates",
        scratch_shapes=[
            pltpu.VMEM(electric.shape, jnp.float32),
            pltpu.VMEM(magnetic.shape, jnp.float32),
            pltpu.VMEM(slab_spectra.shape, jnp.float32),
            pltpu.VMEM(monitor_spectra.shape, jnp.float32),
            pltpu.SemaphoreType.DMA((4,)),
        ],
        out_specs=[HBM] * 4,
        flops=10**7,
        moved=6 * 10**6,
    )

    scaling = 1.0 / math.sqrt(length_x * length_y)
    (orders,) = call(
        functools.partial(x_orders, kept),
        [VMEM] * 2,
        [(group_waves, 2, RECORDS, kept, OX)],
        swapped,
        x_table(length_x, x_blocks, scaling),
        name="x_orders",
        flops=10**7,
        moved=5 * 10**5,
    )
    return (electric_next, magnetic_next, slab_next, monitor_next, orders)


def solution(mesh):
    in_specs = (
        P(None, None, "gx", "gy"),
        P(None, None, "gx", "gy"),
        P(None, "gx", "gy"),
        P(),
        P(None, None, "gx", "gy"),
        P(None, None, None, "gx", "gy"),
        P(),
    )
    out_specs = (
        P(None, None, "gx", "gy"),
        P(None, None, "gx", "gy"),
        P(None, None, "gx", "gy"),
        P(None, None, None, "gx", "gy"),
        P("gy", None, None, "gx", None),
    )
    return jax.shard_map(
        per_device, mesh=mesh, in_specs=in_specs, out_specs=out_specs, check_vma=False
    )
```

```python
import functools
import math

import jax
import jax.numpy as jnp
import ml_dtypes
import numpy as np
from jax import lax
from jax.experimental import pallas as pl
from jax.experimental.pallas import tpu as pltpu
from jax.sharding import PartitionSpec as P

OY = 128
OX = 64

TIME_STEP = 0.5
OMEGA_LOW = 0.15
OMEGA_HIGH = 0.8

STEPS = 2
EDGE = 2 * STEPS
SEAM = 2 * EDGE
DEEP = 4
OUTER = SEAM // STEPS
KINDS = 7
RECORDS = 4

VMEM = pl.BlockSpec(memory_space=pltpu.VMEM)
HBM = pl.BlockSpec(memory_space=pltpu.HBM)
ANY = pl.BlockSpec(memory_space=pl.ANY)
SMEM = pl.BlockSpec(memory_space=pltpu.SMEM)
PARAMS = pltpu.CompilerParams(vmem_limit_bytes=48 * 1024 * 1024)


def in_hbm(array):
    return pltpu.with_memory_space_constraint(array, pltpu.HBM)


def passed_along(block, axis, distance):
    devices = range(lax.axis_size(axis))
    route = [((i - distance) % len(devices), i) for i in devices]
    return lax.ppermute(block, axis, route)


def rolled(values, shift, axis):
    shift %= values.shape[axis]
    return pltpu.roll(values, shift, axis) if shift else values


def iota(shape, axis):
    return lax.broadcasted_iota(jnp.int32, shape, axis)


def rates_of(permittivity, classes, shape):
    return [TIME_STEP / jnp.full(shape, permittivity[k], jnp.float32) for k in range(classes)]


def rate_at(material, rates):
    rate = rates[-1]
    for k in range(len(rates) - 2, -1, -1):
        rate = jnp.where(material == k, rates[k], rate)
    return rate


class Leapfrog:
    def __init__(self, start, layers=None, above=None, below=None):
        self.start = start
        self.layers = layers
        self.above = above
        self.below = below
        self.known = {}

    def first(self, z):
        if ("0", z) not in self.known:
            self.known["0", z] = self.start(z)
        return self.known["0", z]

    def e(self, s, z):
        if s == 0:
            return self.first(z)[0:3]
        if ("e", s, z) not in self.known:
            ex, ey, ez = self.e(s - 1, z)
            hx, hy, hz = self.h(s, z)
            if self.layers is None:
                down_x, down_y = self.below(hx), self.below(hy)
            else:
                down_x, down_y = self.h(s, z - 1)[:2] if z else (0.0, 0.0)
            rate = self.first(z)[6]
            self.known["e", s, z] = (
                ex + rate * ((hz - rolled(hz, 1, 1)) - (hy - down_y)),
                ey + rate * ((hx - down_x) - (hz - rolled(hz, 1, 0))),
                ez + rate * ((hy - rolled(hy, 1, 0)) - (hx - rolled(hx, 1, 1))),
            )
        return self.known["e", s, z]

    def h(self, s, z):
        if s == 0:
            return self.first(z)[3:6]
        if ("h", s, z) not in self.known:
            ex, ey, ez = self.e(s - 1, z)
            hx, hy, hz = self.h(s - 1, z)
            if self.layers is None:
                up_x, up_y = self.above(ex), self.above(ey)
            else:
                up_x, up_y = self.e(s - 1, z + 1)[:2] if z + 1 < self.layers else (0.0, 0.0)
            self.known["h", s, z] = (
                hx - TIME_STEP * ((rolled(ez, -1, 1) - ez) - (up_y - ey)),
                hy - TIME_STEP * ((up_x - ex) - (rolled(ez, -1, 0) - ez)),
                hz - TIME_STEP * ((rolled(ey, -1, 0) - ey) - (rolled(ex, -1, 1) - ex)),
            )
        return self.known["h", s, z]

    def records(self, s, z):
        return self.e(s, z)[:2] + self.h(s, z)[:2]


def seam_leapfrog(tiles, layers):
    layer = iota(tiles[0].shape, 1) // SEAM % layers
    return Leapfrog(
        lambda z: tiles,
        above=lambda f: jnp.where(layer < layers - 1, rolled(f, -SEAM, 1), 0.0),
        below=lambda f: jnp.where(layer > 0, rolled(f, SEAM, 1), 0.0),
    )


def own_planes(e_ref, h_ref, m_ref, rates):
    def at(z):
        rate = rate_at(m_ref[z], rates)
        return [e_ref[c, z] for c in range(3)] + [h_ref[c, z] for c in range(3)] + [rate]

    return at


def widened_planes(own, same_ref, cross_ref):
    even = lax.rem(lax.axis_index("gx"), 2) == 0

    def at(z):
        planes = own(z)
        rows = planes[0].shape[0]
        group, place = divmod(z, rows // STEPS)
        row = iota(planes[0].shape, 0)
        wide = []
        for kind in range(KINDS):
            same, cross = same_ref[kind, group], cross_ref[kind, group]
            after = rolled(jnp.where(even, same, cross), -STEPS * place, 0)
            before = rolled(jnp.where(even, cross, same), rows - STEPS - STEPS * place, 0)
            halo = jnp.where(row < STEPS, after, before)
            wide.append(jnp.concatenate([planes[kind], halo], axis=0))
        return wide

    return at


def block_copy(distance, spectra_any, block_ref, semaphore):
    waves = block_ref.shape[0]
    blocks = spectra_any.shape[0] // waves
    owner = lax.rem(lax.axis_index("gy") + blocks - distance, blocks)
    source = spectra_any.at[pl.ds(owner * waves, waves)]
    return pltpu.make_async_copy(source, block_ref, semaphore)


def other_blocks(distances, after_this, spectra_any, *refs):
    *block_refs, sent = refs
    copies = [
        block_copy(distance, spectra_any, block_ref, sent.at[i])
        for i, (distance, block_ref) in enumerate(zip(distances, block_refs))
    ]
    for copy in copies:
        copy.start()
    for copy in copies:
        copy.wait()


def pack_faces(
    distances,
    perm_any,
    e_any,
    h_any,
    m_any,
    spectra_any,
    same_ref,
    cross_ref,
    *refs,
):
    even = lax.rem(lax.axis_index("gx"), 2) == 0
    *block_refs, perm_ref, e_ref, h_ref, m_ref, ready, sent = refs
    sources, targets = (e_any, h_any, m_any, perm_any), (e_ref, h_ref, m_ref, perm_ref)
    copies = [
        pltpu.make_async_copy(source, target, ready.at[i])
        for i, (source, target) in enumerate(zip(sources, targets))
    ]
    for i, (distance, block_ref) in enumerate(zip(distances, block_refs)):
        copies.append(block_copy(distance, spectra_any, block_ref, sent.at[i]))
    for copy in copies:
        copy.start()
    for copy in copies[:4]:
        copy.wait()
    layers, rows, columns = m_ref.shape
    rates = rates_of(perm_ref, perm_ref.shape[0], (rows, columns))
    own = own_planes(e_ref, h_ref, m_ref, rates)
    row = iota((rows, columns), 0)
    per_group = rows // STEPS
    for group in range(layers // per_group):
        planes = [own(group * per_group + place) for place in range(per_group)]
        for kind in range(KINDS):
            forth = rolled(planes[0][kind], STEPS - rows, 0)
            back = planes[0][kind]
            for place in range(1, per_group):
                spot = STEPS * place
                here = planes[place][kind]
                forth = jnp.where(row >= spot, rolled(here, spot + STEPS - rows, 0), forth)
                back = jnp.where(row >= spot, rolled(here, spot, 0), back)
            same_ref[kind, group] = jnp.where(even, forth, back)
            cross_ref[kind, group] = jnp.where(even, back, forth)
    for copy in copies[4:]:
        copy.wait()


def blocks_transposed(tiles):
    tiles = list(tiles)
    count = len(tiles)
    width = tiles[0].shape[1] // count
    block = iota(tiles[0].shape, 1) // width
    bit = 1
    while bit < count:
        low = (block & bit) == 0
        for i in range(count):
            if not i & bit:
                first, second = tiles[i], tiles[i + bit]
                tiles[i] = jnp.where(low, first, rolled(second, bit * width, 1))
                tiles[i + bit] = jnp.where(low, rolled(first, -bit * width, 1), second)
        bit *= 2
    return tiles


def packed_edges(planes, layers, spot):
    tile = None
    for z in range(layers):
        here = rolled(planes[z], spot + z * SEAM + EDGE, 1)
        if tile is None:
            tile = here
        else:
            tile = jnp.where(iota(tile.shape, 1) >= spot + z * SEAM, here, tile)
    return tile


def squeezed(first, second):
    rows = first.shape[0] // 2
    row = iota((rows, first.shape[1]), 0)
    ends = (row < STEPS) | (row >= rows - STEPS)
    second_halo = second[rows:]
    moved = jnp.where(
        row < 2 * STEPS, rolled(second_halo, STEPS, 0), rolled(second_halo, -STEPS, 0)
    )
    return first[:rows], second[:rows], jnp.where(ends, first[rows:], moved)


def stretched(first, second, halo):
    rows = first.shape[0]
    row = iota(halo.shape, 0)
    moved = jnp.where(row < 2 * STEPS, rolled(halo, -STEPS, 0), rolled(halo, STEPS, 0))
    return jnp.concatenate([first, halo], axis=0), jnp.concatenate([second, moved], axis=0)


def pair_of_tiles(ref, pair, rows):
    base = (STEPS * RECORDS + 3 * pair) * rows
    return stretched(*[ref[pl.ds(base + i * rows, rows), :] for i in range(3)])


def monitor_message(
    perm_ref,
    e_ref,
    h_ref,
    m_ref,
    same_ref,
    cross_ref,
    forth_ref,
    back_ref,
    far_ref,
    edges_ref,
):
    layers, rows, columns = m_ref.shape
    rates = rates_of(perm_ref, perm_ref.shape[0], (rows, columns))
    wide = widened_planes(own_planes(e_ref, h_ref, m_ref, rates), same_ref, cross_ref)
    low = layers - DEEP
    walk = Leapfrog(lambda z: wide(low + z), layers=DEEP)
    for s in range(STEPS):
        for c, record in enumerate(walk.records(s + 1, DEEP - 1)):
            place = pl.ds((s * RECORDS + c) * rows, rows)
            for ref in (forth_ref, back_ref, far_ref):
                ref[place, :] = record[:rows]
    planes = [wide(z) for z in range(low)] + [walk.first(z) for z in range(DEEP)]
    span = DEEP * SEAM
    per_tile = columns // span
    tops, lasts, firsts = ([None, None] for _ in range(3))
    for kind in range(KINDS):
        edges = packed_edges([planes[z][kind] for z in range(layers)], layers, 0)
        edges_ref[kind] = edges
        lane = iota(edges.shape, 1)
        tile, spot = divmod(kind, per_tile)
        here = rolled(edges, spot * span - low * SEAM, 1)
        tops[tile] = jnp.where(lane >= spot * span, here, tops[tile]) if spot else here
        tile, spot = divmod(kind, OUTER)
        for tiles, shift in ((lasts, STEPS), (firsts, EDGE)):
            here = rolled(edges, spot * STEPS - shift, 1)
            tiles[tile] = jnp.where(lane % SEAM >= spot * STEPS, here, tiles[tile]) if spot else here
    base = STEPS * RECORDS * rows
    for i, part in enumerate(squeezed(*tops)):
        for ref in (forth_ref, back_ref, far_ref):
            ref[pl.ds(base + i * rows, rows), :] = part
    for ref, tiles in ((forth_ref, lasts), (back_ref, firsts)):
        for i, part in enumerate(squeezed(*tiles)):
            ref[pl.ds(base + (3 + i) * rows, rows), :] = part


def waves_of(coef_ref, wave):
    base = wave * (STEPS * 4)
    return lambda s, half, part: coef_ref[base + (s * 2 + half) * 2 + part]


def exact_dot(left, right, contracted):
    return lax.dot_general(
        left,
        right,
        (contracted, ((), ())),
        precision=lax.Precision.HIGHEST,
        preferred_element_type=jnp.float32,
    )


def split_dot(values, tables, total, contracted=((1,), (0,))):
    coarse = values.astype(jnp.bfloat16)
    fine = (values - coarse.astype(jnp.float32)).astype(jnp.bfloat16)
    for left, right in ((coarse, tables[0]), (fine, tables[0]), (coarse, tables[1])):
        product = lax.dot_general(
            left, right, (contracted, ((), ())), preferred_element_type=jnp.float32
        )
        total = product if total is None else total + product
    return total


def packed_orders(values, planes, kept):
    rows = values.shape[0] // planes
    parts = [values[plane * rows : (plane + 1) * rows] for plane in range(planes)]
    targets = per_tile = OY // kept
    if planes % per_tile == 0 and not targets & (targets - 1):
        groups = [parts[i : i + per_tile] for i in range(0, planes, per_tile)]
        return list(zip(*[blocks_transposed(group) for group in groups]))
    lane = iota((rows, OY), 1)
    packed = []
    for target in range(targets):
        tiles = []
        for first in range(0, planes, per_tile):
            tile = None
            for plane in range(first, min(planes, first + per_tile)):
                spot = (plane - first) * kept
                here = rolled(parts[plane], spot - target * kept, 1)
                tile = here if tile is None else jnp.where(lane >= spot, here, tile)
            tiles.append(tile)
        packed.append(tiles)
    return packed


def fetch(after_this, slab_any, monitor_any, slab_ref, monitor_ref, ready):
    copies = [
        pltpu.make_async_copy(slab_any, slab_ref, ready.at[0]),
        pltpu.make_async_copy(monitor_any, monitor_ref, ready.at[1]),
    ]
    for copy in copies:
        copy.start()
    for copy in copies:
        copy.wait()


def y_monitor(wave_ref, coef_ref, table_ref, own_ref, *refs):
    *spectra, out_ref, weights_ref = refs
    half = len(spectra) // 2
    spectra = spectra[half + 1 :] + spectra[:1] + spectra[1 : half + 1]
    blocks = len(spectra) + 1
    waves, _, records, rows, columns = spectra[0].shape
    me = lax.axis_index("gy")
    spectra = [own_ref.at[pl.ds(me * waves, waves)]] + spectra
    total = None
    for block in range(blocks):
        owner = lax.rem(me + block, blocks)
        place = pl.ds(pl.multiple_of(owner * columns, columns), columns)
        parts = []
        for part in range(2):
            for w in range(waves):
                parts += [spectra[block][w, part, c] for c in range(records)]
        tables = [table_ref[i, place, :] for i in range(2)]
        total = split_dot(jnp.concatenate(parts, axis=0), tables, total)
    half = waves * records * rows
    real = total[:half, :OY] + total[half:, OY:]
    imag = total[half:, :OY] - total[:half, OY:]
    targets = out_ref.shape[0]
    for part, values in enumerate((real, imag)):
        packed = packed_orders(values, waves * records, OY // targets)
        for target in range(targets):
            for i, tile in enumerate(packed[target]):
                out_ref[target, pl.ds((i * 2 + part) * rows, rows), :] = tile
    kept = OY // targets
    lane = iota((rows, OY), 1)
    per_wave = RECORDS * kept
    per_tile = OY // per_wave
    for tile in range(weights_ref.shape[0] // (2 * STEPS)):
        some = range(tile * per_tile, min(waves, (tile + 1) * per_tile))
        coefs = [waves_of(coef_ref, wave_ref[me * waves + w]) for w in some]
        for s in range(STEPS):
            for part in range(2):
                weight = None
                for i, coef in enumerate(coefs):
                    for half in range(2):
                        value = jnp.full((rows, OY), coef(s, half, part), jnp.float32)
                        spot = i * per_wave + half * (per_wave // 2)
                        weight = value if weight is None else jnp.where(lane >= spot, value, weight)
                weights_ref[(tile * STEPS + s) * 2 + part] = weight


def y_records(waves, table_ref, monitor_ref, weights_ref, *refs):
    *messages, out_any, out_ref, done = refs
    messages = messages[::-1]
    blocks = len(messages)
    columns = messages[0].shape[1]
    targets, height, _ = out_ref.shape
    kept = OY // targets
    out_tiles = -(-waves * RECORDS * kept // OY)
    rows = height // (2 * out_tiles)
    me = lax.axis_index("gy")
    span = DEEP * SEAM
    per_tile = columns // span
    base = STEPS * RECORDS * rows
    column = iota((2 * rows, columns), 1) % SEAM
    edges = [pair_of_tiles(message, 0, rows) for message in messages]

    total = None
    for block in range(blocks):
        owner = lax.rem(me + block, blocks)
        place = pl.ds(pl.multiple_of(blocks * span + owner * columns, span), columns)
        values = messages[block][pl.ds(0, base), :]
        total = split_dot(values, [table_ref[part, place, :] for part in range(2)], total)
    for tile in range(-(-blocks // per_tile)):
        seams = range(tile * per_tile, min(blocks, (tile + 1) * per_tile))
        kinds = []
        for part in range(2):
            mixed = []
            for seam in list(seams) + [seams[0]] * (per_tile - len(seams)):
                here, after = edges[seam][part], edges[(seam + 1) % blocks][part]
                mixed.append(jnp.where(column < EDGE, here, after))
            kinds += blocks_transposed(mixed)
        walk = seam_leapfrog(kinds[:KINDS], DEEP)
        record = []
        for s in range(STEPS):
            record += [value[:rows] for value in walk.records(s + 1, 0)]
        values = jnp.concatenate(record, axis=0)[:, : len(seams) * span]
        owners = [lax.rem(me + seam, blocks) for seam in seams]
        places = [pl.ds(pl.multiple_of(owner * span, span), span) for owner in owners]
        tables = [
            jnp.concatenate([table_ref[part, place, :] for place in places], axis=0)
            for part in range(2)
        ]
        total = split_dot(values, tables, total)
    lane = iota((rows, OY), 1)
    per_wave = RECORDS * kept
    per_tile = OY // per_wave
    packed_parts = [
        packed_orders(total[:, part * OY : (part + 1) * OY], STEPS * RECORDS, kept)
        for part in range(2)
    ]
    copies = []
    for target in range(targets):
        spot = order_of(targets).index(target)
        sides = []
        for part in range(2):
            (packed,) = packed_parts[part][target]
            steps = []
            for s in range(STEPS):
                spread = None
                for i in range(min(per_tile, waves)):
                    here = rolled(packed, i * per_wave - s * per_wave, 1)
                    spread = here if i == 0 else jnp.where(lane >= i * per_wave, here, spread)
                steps.append(spread)
            sides.append(steps)
        for tile in range(out_tiles):
            for part in range(2):
                place = pl.ds((tile * 2 + part) * rows, rows)
                value = monitor_ref[target, place, :]
                for s in range(STEPS):
                    first = (tile * STEPS + s) * 2
                    real, imag = weights_ref[first], weights_ref[first + 1]
                    if part == 0:
                        value = value + (real * sides[0][s] - imag * sides[1][s])
                    else:
                        value = value + (imag * sides[0][s] + real * sides[1][s])
                out_ref[spot, place, :] = value
        copies.append(
            pltpu.make_async_copy(out_ref.at[spot], out_any.at[spot], done.at[spot])
        )
        copies[-1].start()
    for copy in copies:
        copy.wait()


def x_orders(kept, values_ref, table_ref, out_any, out_ref, done):
    sources, height, lanes = values_ref.shape
    waves, _, records, _, _ = out_ref.shape
    depth = table_ref.shape[1]
    rows = depth // sources
    per_tile = lanes // kept
    copies = []
    for tile in range(height // rows):
        values = jnp.concatenate(
            [values_ref[source, pl.ds(tile * rows, rows), :] for source in range(sources)], axis=0
        )
        result = split_dot(values, [table_ref[0], table_ref[1]], None, ((0,), (0,)))
        for place in range(per_tile):
            wave, record = divmod(tile * per_tile + place, records)
            if wave < waves:
                here = result[place * kept : (place + 1) * kept]
                out_ref[wave, 0, record] = here[:, :OX]
                out_ref[wave, 1, record] = here[:, OX:]
                if record == records - 1:
                    copies.append(
                        pltpu.make_async_copy(out_ref.at[wave], out_any.at[wave], done.at[wave])
                    )
                    copies[-1].start()
    for copy in copies:
        copy.wait()


def local_updates(
    perm_ref,
    wave_ref,
    coef_ref,
    e_ref,
    h_ref,
    m_ref,
    same_ref,
    cross_ref,
    edges_ref,
    message_after_ref,
    message_before_ref,
    slab_ref,
    monitor_ref,
    e_any,
    h_any,
    slab_out_any,
    monitor_out_any,
    e_out,
    h_out,
    slab_out,
    monitor_out,
    done,
):
    layers, rows, columns = m_ref.shape
    rates = rates_of(perm_ref, perm_ref.shape[0], (rows, columns))
    wide = widened_planes(own_planes(e_ref, h_ref, m_ref, rates), same_ref, cross_ref)
    walk = Leapfrog(wide, layers=layers)
    left = iota((2 * rows, layers * SEAM), 1) % SEAM < EDGE
    last = pair_of_tiles(message_before_ref, 1, rows)
    first = pair_of_tiles(message_after_ref, 1, rows)
    before, after = [], []
    for kind in range(KINDS):
        mine = edges_ref[kind]
        tile, spot = divmod(kind, OUTER)
        from_before = rolled(last[tile], STEPS - spot * STEPS, 1)
        from_after = rolled(first[tile], EDGE - spot * STEPS, 1)
        before.append(jnp.where(left, from_before, mine))
        after.append(jnp.where(left, mine, from_after))
    before = seam_leapfrog(before, layers)
    after = seam_leapfrog(after, layers)
    column = iota((rows, columns), 1)
    inner = (column >= STEPS) & (column < columns - STEPS)
    joined = {}

    def mended(s, z, kind):
        if (s, kind) not in joined:
            ends = [(side.e(s, 0) + side.h(s, 0))[kind][:rows] for side in (after, before)]
            joined[s, kind] = jnp.where(left[:rows], ends[0], ends[1])
        value = (walk.e(s, z) + walk.h(s, z))[kind][:rows]
        return jnp.where(inner, value, rolled(joined[s, kind], -(z * SEAM + EDGE), 1))

    middle = layers // 2
    slab_records = [[None] * 2 for _ in range(STEPS)]
    records = [[None] * RECORDS for _ in range(STEPS)]
    for z in range(layers):
        for kind in range(6):
            value = mended(STEPS, z, kind)
            if kind < 3:
                e_out[kind, z] = value
            else:
                h_out[kind - 3, z] = value
        for s in range(STEPS):
            if z == middle:
                slab_records[s] = [mended(s + 1, z, kind) for kind in (0, 1)]
            if z == layers - 1:
                records[s] = [mended(s + 1, z, kind) for kind in (0, 1, 3, 4)]
    sent = [
        pltpu.make_async_copy(e_out, e_any, done.at[0]),
        pltpu.make_async_copy(h_out, h_any, done.at[1]),
    ]
    for copy in sent:
        copy.start()
    frequencies = slab_ref.shape[1] // 2

    def one_frequency(f, carry):
        coef = waves_of(coef_ref, f)
        for c in range(2):
            for part in range(2):
                value = slab_ref[c, part * frequencies + f]
                for s in range(STEPS):
                    value = value + coef(s, 0, part) * slab_records[s][c]
                slab_out[c, part * frequencies + f] = value
        return carry

    lax.fori_loop(0, frequencies, one_frequency, 0, unroll=4)
    sent.append(pltpu.make_async_copy(slab_out, slab_out_any, done.at[2]))
    sent[-1].start()
    for w in range(monitor_ref.shape[0]):
        coef = waves_of(coef_ref, wave_ref[w])
        for part in range(2):
            for c in range(RECORDS):
                value = monitor_ref[w, part, c]
                for s in range(STEPS):
                    value = value + coef(s, c // 2, part) * records[s][c]
                monitor_out[w, part, c] = value
    sent.append(pltpu.make_async_copy(monitor_out, monitor_out_any, done.at[3]))
    sent[-1].start()
    for copy in sent:
        copy.wait()


def wave_coefficients(freq_count):
    omegas = OMEGA_LOW + (OMEGA_HIGH - OMEGA_LOW) * np.arange(freq_count) / (freq_count - 1)
    times = TIME_STEP * (np.arange(1, STEPS + 1)[:, None] - np.array([0.0, 0.5])[None, :])
    angles = omegas[:, None, None] * times[None]
    table = np.stack([TIME_STEP * np.cos(angles), -TIME_STEP * np.sin(angles)], axis=-1)
    return table.reshape(-1).astype(np.float32)


def angles_of(length, kept):
    wanted = (np.arange(kept) - kept // 2) % length
    return 2.0 * math.pi / length * (np.arange(length)[:, None] * wanted[None, :] % length)


def y_table(length):
    angles = angles_of(length, OY)
    return split_table(np.concatenate([np.cos(angles), np.sin(angles)], axis=1))


def split_table(table):
    table = table.astype(np.float32)
    coarse = table.astype(ml_dtypes.bfloat16)
    fine = (table - coarse.astype(np.float32)).astype(ml_dtypes.bfloat16)
    return jnp.asarray(np.stack([coarse, fine]))


def record_table(length, blocks):
    angles = angles_of(length, OY)
    table = np.concatenate([np.cos(angles), -np.sin(angles)], axis=1)
    columns = length // blocks
    seams = np.zeros((blocks, DEEP, SEAM, 2 * OY))
    for block in range(blocks):
        for column in range(-STEPS, STEPS):
            row = ((block + 1) * columns + column) % length
            seams[block, DEEP - 1, EDGE + column] = table[row]
    inner = table.copy()
    place = np.arange(length) % columns
    inner[(place < STEPS) | (place >= columns - STEPS)] = 0.0
    return split_table(np.concatenate([seams.reshape(-1, 2 * OY), inner]))


def order_of(blocks):
    return list(reversed(range(blocks)))


def x_table(length, blocks, scaling):
    angles = angles_of(length, OX).reshape(blocks, length // blocks, OX)[order_of(blocks)]
    real = np.concatenate([np.cos(angles), -np.sin(angles)], axis=2)
    imag = np.concatenate([np.sin(angles), np.cos(angles)], axis=2)
    table = np.stack([real, imag], axis=1) * scaling
    return split_table(table.reshape(2 * length, 2 * OX))


def call(kernel, in_specs, shapes, *operands, name, flops=0, moved=0, **more):
    kind = jax.ShapeDtypeStruct
    out = [kind(shape, jnp.float32) for shape in shapes]
    return pl.pallas_call(
        kernel,
        out_shape=out,
        in_specs=in_specs,
        out_specs=more.pop("out_specs", [VMEM] * len(out)),
        compiler_params=PARAMS,
        cost_estimate=pl.CostEstimate(flops=flops, bytes_accessed=moved, transcendentals=0),
        name=name,
        **more,
    )(*operands)


def per_device(
    electric, magnetic, material, permittivity, slab_spectra, monitor_spectra, wave_index
):
    layers, rows, columns = material.shape
    x_blocks, y_blocks = lax.axis_size("gx"), lax.axis_size("gy")
    waves = monitor_spectra.shape[0]
    group_waves = waves // y_blocks
    fields = (electric, magnetic, material)
    groups = layers * STEPS // rows

    faces = (KINDS, groups, rows, columns)
    block = (group_waves,) + monitor_spectra.shape[1:]
    early = [y_blocks // 2]
    late = [distance for distance in range(1, y_blocks) if distance not in early]
    packed, cross, *blocks = call(
        functools.partial(pack_faces, early),
        [HBM] * 5,
        [faces, faces] + [block] * len(early),
        *[in_hbm(array) for array in (permittivity, *fields, monitor_spectra)],
        name="pack_faces",
        flops=10**5,
        moved=10**6,
        scratch_shapes=[
            pltpu.SMEM(permittivity.shape, jnp.float32),
            pltpu.VMEM(electric.shape, jnp.float32),
            pltpu.VMEM(magnetic.shape, jnp.float32),
            pltpu.VMEM(material.shape, jnp.int32),
            pltpu.SemaphoreType.DMA((4,)),
            pltpu.SemaphoreType.DMA((len(early),)),
        ],
    )
    line = range(x_blocks)
    same = lax.ppermute(packed, "gx", [(i, i ^ 1) for i in line])
    cross = lax.ppermute(cross, "gx", [(i, (i + (1 if i % 2 else -1)) % x_blocks) for i in line])
    spectra = {
        distance: passed_along(block, "gy", -distance) for distance, block in zip(early, blocks)
    }
    blocks = call(
        functools.partial(other_blocks, late),
        [ANY, HBM],
        [block] * len(late),
        packed,
        in_hbm(monitor_spectra),
        name="other_blocks",
        flops=1,
        moved=1,
        scratch_shapes=[pltpu.SemaphoreType.DMA((len(late),))],
    )
    for distance, block in zip(late, blocks):
        spectra[distance] = passed_along(block, "gy", -distance)

    far_height = (STEPS * RECORDS + 3) * rows
    near_height = far_height + 3 * rows
    forth, back, far, edges = call(
        monitor_message,
        [SMEM] + [VMEM] * 5,
        [
            (near_height, columns),
            (near_height, columns),
            (far_height, columns),
            (KINDS, 2 * rows, layers * SEAM),
        ],
        permittivity,
        *fields,
        same,
        cross,
        name="monitor_message",
        flops=1,
        moved=1,
    )
    message_before = passed_along(forth, "gy", 1)
    message_after = passed_along(back, "gy", -1)
    messages = [far, message_after]
    for distance in range(2, y_blocks - 1):
        messages.append(passed_along(far, "gy", -distance))
    messages = (messages + [message_before])[:y_blocks]

    coefs = jnp.asarray(wave_coefficients(slab_spectra.shape[1] // 2))
    length_x, length_y = rows * x_blocks, columns * y_blocks
    kept = OY // x_blocks
    out_tiles = -(-group_waves * RECORDS * kept // OY)
    sums_y = y_table(length_y)
    slab_here, monitor_here = call(
        fetch,
        [ANY] + [HBM] * 2,
        [slab_spectra.shape, monitor_spectra.shape],
        far,
        in_hbm(slab_spectra),
        in_hbm(monitor_spectra),
        name="fetch",
        flops=1,
        moved=3 * 10**6,
        scratch_shapes=[pltpu.SemaphoreType.DMA((2,))],
    )
    monitor_y, weights = call(
        y_monitor,
        [SMEM] * 2 + [VMEM] * (1 + y_blocks),
        [(x_blocks, out_tiles * 2 * rows, OY), (out_tiles * STEPS * 2, rows, OY)],
        wave_index,
        coefs,
        sums_y,
        monitor_here,
        *[spectra[distance] for distance in [y_blocks // 2] + list(range(y_blocks // 2 + 1, y_blocks)) + list(range(1, y_blocks // 2))],
        name="y_monitor",
        flops=10**8,
        moved=2 * 10**6,
    )
    (spectrum_y,) = call(
        functools.partial(y_records, group_waves),
        [VMEM] * (3 + y_blocks),
        [monitor_y.shape],
        record_table(length_y, y_blocks),
        monitor_y,
        weights,
        *messages[::-1],
        out_specs=[HBM],
        scratch_shapes=[
            pltpu.VMEM(monitor_y.shape, jnp.float32),
            pltpu.SemaphoreType.DMA((x_blocks,)),
        ],
        name="y_records",
        flops=10**8,
        moved=2 * 10**6,
    )
    members = [
        [x * y_blocks + y for x in order_of(x_blocks)] for y in range(y_blocks)
    ]
    swapped = lax.all_to_all(
        spectrum_y, ("gx", "gy"), split_axis=0, concat_axis=0, axis_index_groups=members, tiled=True
    )

    electric_next, magnetic_next, slab_next, monitor_next = call(
        local_updates,
        [SMEM] * 3 + [VMEM] * 10,
        [electric.shape, magnetic.shape, slab_spectra.shape, monitor_spectra.shape],
        permittivity,
        wave_index,
        coefs,
        *fields,
        same,
        cross,
        edges,
        message_after,
        message_before,
        slab_here,
        monitor_here,
        name="local_updates",
        scratch_shapes=[
            pltpu.VMEM(electric.shape, jnp.float32),
            pltpu.VMEM(magnetic.shape, jnp.float32),
            pltpu.VMEM(slab_spectra.shape, jnp.float32),
            pltpu.VMEM(monitor_spectra.shape, jnp.float32),
            pltpu.SemaphoreType.DMA((4,)),
        ],
        out_specs=[HBM] * 4,
        flops=10**7,
        moved=6 * 10**6,
    )

    scaling = 1.0 / math.sqrt(length_x * length_y)
    (orders,) = call(
        functools.partial(x_orders, kept),
        [VMEM] * 2,
        [(group_waves, 2, RECORDS, kept, OX)],
        swapped,
        x_table(length_x, x_blocks, scaling),
        out_specs=[HBM],
        scratch_shapes=[
            pltpu.VMEM((group_waves, 2, RECORDS, kept, OX), jnp.float32),
            pltpu.SemaphoreType.DMA((group_waves,)),
        ],
        name="x_orders",
        flops=10**7,
        moved=5 * 10**5,
    )
    return (electric_next, magnetic_next, slab_next, monitor_next, orders)


def solution(mesh):
    in_specs = (
        P(None, None, "gx", "gy"),
        P(None, None, "gx", "gy"),
        P(None, "gx", "gy"),
        P(),
        P(None, None, "gx", "gy"),
        P(None, None, None, "gx", "gy"),
        P(),
    )
    out_specs = (
        P(None, None, "gx", "gy"),
        P(None, None, "gx", "gy"),
        P(None, None, "gx", "gy"),
        P(None, None, None, "gx", "gy"),
        P("gy", None, None, "gx", None),
    )
    return jax.shard_map(
        per_device, mesh=mesh, in_specs=in_specs, out_specs=out_specs, check_vma=False
    )
```

```python
import functools
import math

import jax
import jax.numpy as jnp
import ml_dtypes
import numpy as np
from jax import lax
from jax.experimental import pallas as pl
from jax.experimental.pallas import tpu as pltpu
from jax.sharding import PartitionSpec as P

OY = 128
OX = 64

TIME_STEP = 0.5
OMEGA_LOW = 0.15
OMEGA_HIGH = 0.8

STEPS = 2
EDGE = 2 * STEPS
SEAM = 2 * EDGE
DEEP = 4
OUTER = SEAM // STEPS
KINDS = 7
RECORDS = 4

VMEM = pl.BlockSpec(memory_space=pltpu.VMEM)
HBM = pl.BlockSpec(memory_space=pltpu.HBM)
ANY = pl.BlockSpec(memory_space=pl.ANY)
SMEM = pl.BlockSpec(memory_space=pltpu.SMEM)
PARAMS = pltpu.CompilerParams(vmem_limit_bytes=48 * 1024 * 1024)


def in_hbm(array):
    return pltpu.with_memory_space_constraint(array, pltpu.HBM)


def passed_along(block, axis, distance):
    devices = range(lax.axis_size(axis))
    route = [((i - distance) % len(devices), i) for i in devices]
    return lax.ppermute(block, axis, route)


def rolled(values, shift, axis):
    shift %= values.shape[axis]
    return pltpu.roll(values, shift, axis) if shift else values


def iota(shape, axis):
    return lax.broadcasted_iota(jnp.int32, shape, axis)


def rates_of(permittivity, classes, shape):
    return [TIME_STEP / jnp.full(shape, permittivity[k], jnp.float32) for k in range(classes)]


def rate_at(material, rates):
    rate = rates[-1]
    for k in range(len(rates) - 2, -1, -1):
        rate = jnp.where(material == k, rates[k], rate)
    return rate


class Leapfrog:
    def __init__(self, start, layers=None, above=None, below=None):
        self.start = start
        self.layers = layers
        self.above = above
        self.below = below
        self.known = {}

    def first(self, z):
        if ("0", z) not in self.known:
            self.known["0", z] = self.start(z)
        return self.known["0", z]

    def e(self, s, z):
        if s == 0:
            return self.first(z)[0:3]
        if ("e", s, z) not in self.known:
            ex, ey, ez = self.e(s - 1, z)
            hx, hy, hz = self.h(s, z)
            if self.layers is None:
                down_x, down_y = self.below(hx), self.below(hy)
            else:
                down_x, down_y = self.h(s, z - 1)[:2] if z else (0.0, 0.0)
            rate = self.first(z)[6]
            self.known["e", s, z] = (
                ex + rate * ((hz - rolled(hz, 1, 1)) - (hy - down_y)),
                ey + rate * ((hx - down_x) - (hz - rolled(hz, 1, 0))),
                ez + rate * ((hy - rolled(hy, 1, 0)) - (hx - rolled(hx, 1, 1))),
            )
        return self.known["e", s, z]

    def h(self, s, z):
        if s == 0:
            return self.first(z)[3:6]
        if ("h", s, z) not in self.known:
            ex, ey, ez = self.e(s - 1, z)
            hx, hy, hz = self.h(s - 1, z)
            if self.layers is None:
                up_x, up_y = self.above(ex), self.above(ey)
            else:
                up_x, up_y = self.e(s - 1, z + 1)[:2] if z + 1 < self.layers else (0.0, 0.0)
            self.known["h", s, z] = (
                hx - TIME_STEP * ((rolled(ez, -1, 1) - ez) - (up_y - ey)),
                hy - TIME_STEP * ((up_x - ex) - (rolled(ez, -1, 0) - ez)),
                hz - TIME_STEP * ((rolled(ey, -1, 0) - ey) - (rolled(ex, -1, 1) - ex)),
            )
        return self.known["h", s, z]

    def records(self, s, z):
        return self.e(s, z)[:2] + self.h(s, z)[:2]


def seam_leapfrog(tiles, layers):
    layer = iota(tiles[0].shape, 1) // SEAM % layers
    return Leapfrog(
        lambda z: tiles,
        above=lambda f: jnp.where(layer < layers - 1, rolled(f, -SEAM, 1), 0.0),
        below=lambda f: jnp.where(layer > 0, rolled(f, SEAM, 1), 0.0),
    )


def own_planes(e_ref, h_ref, m_ref, rates):
    def at(z):
        rate = rate_at(m_ref[z], rates)
        return [e_ref[c, z] for c in range(3)] + [h_ref[c, z] for c in range(3)] + [rate]

    return at


def widened_planes(own, same_ref, cross_ref):
    even = lax.rem(lax.axis_index("gx"), 2) == 0

    def at(z):
        planes = own(z)
        rows = planes[0].shape[0]
        group, place = divmod(z, rows // STEPS)
        row = iota(planes[0].shape, 0)
        wide = []
        for kind in range(KINDS):
            same, cross = same_ref[kind, group], cross_ref[kind, group]
            after = rolled(jnp.where(even, same, cross), -STEPS * place, 0)
            before = rolled(jnp.where(even, cross, same), rows - STEPS - STEPS * place, 0)
            halo = jnp.where(row < STEPS, after, before)
            wide.append(jnp.concatenate([planes[kind], halo], axis=0))
        return wide

    return at


def block_copy(distance, spectra_any, block_ref, semaphore):
    waves = block_ref.shape[0]
    blocks = spectra_any.shape[0] // waves
    owner = lax.rem(lax.axis_index("gy") + blocks - distance, blocks)
    source = spectra_any.at[pl.ds(owner * waves, waves)]
    return pltpu.make_async_copy(source, block_ref, semaphore)


def other_blocks(distances, after_this, spectra_any, *refs):
    *block_refs, sent = refs
    copies = [
        block_copy(distance, spectra_any, block_ref, sent.at[i])
        for i, (distance, block_ref) in enumerate(zip(distances, block_refs))
    ]
    for copy in copies:
        copy.start()
    for copy in copies:
        copy.wait()


def pack_faces(
    distances,
    perm_any,
    e_any,
    h_any,
    m_any,
    spectra_any,
    same_ref,
    cross_ref,
    *refs,
):
    even = lax.rem(lax.axis_index("gx"), 2) == 0
    *block_refs, perm_ref, e_ref, h_ref, m_ref, ready, sent = refs
    sources, targets = (e_any, h_any, m_any, perm_any), (e_ref, h_ref, m_ref, perm_ref)
    copies = [
        pltpu.make_async_copy(source, target, ready.at[i])
        for i, (source, target) in enumerate(zip(sources, targets))
    ]
    for i, (distance, block_ref) in enumerate(zip(distances, block_refs)):
        copies.append(block_copy(distance, spectra_any, block_ref, sent.at[i]))
    for copy in copies:
        copy.start()
    for copy in copies[:4]:
        copy.wait()
    layers, rows, columns = m_ref.shape
    rates = rates_of(perm_ref, perm_ref.shape[0], (rows, columns))
    own = own_planes(e_ref, h_ref, m_ref, rates)
    row = iota((rows, columns), 0)
    per_group = rows // STEPS
    for group in range(layers // per_group):
        planes = [own(group * per_group + place) for place in range(per_group)]
        for kind in range(KINDS):
            forth = rolled(planes[0][kind], STEPS - rows, 0)
            back = planes[0][kind]
            for place in range(1, per_group):
                spot = STEPS * place
                here = planes[place][kind]
                forth = jnp.where(row >= spot, rolled(here, spot + STEPS - rows, 0), forth)
                back = jnp.where(row >= spot, rolled(here, spot, 0), back)
            same_ref[kind, group] = jnp.where(even, forth, back)
            cross_ref[kind, group] = jnp.where(even, back, forth)
    for copy in copies[4:]:
        copy.wait()


def blocks_transposed(tiles):
    tiles = list(tiles)
    count = len(tiles)
    width = tiles[0].shape[1] // count
    block = iota(tiles[0].shape, 1) // width
    bit = 1
    while bit < count:
        low = (block & bit) == 0
        for i in range(count):
            if not i & bit:
                first, second = tiles[i], tiles[i + bit]
                tiles[i] = jnp.where(low, first, rolled(second, bit * width, 1))
                tiles[i + bit] = jnp.where(low, rolled(first, -bit * width, 1), second)
        bit *= 2
    return tiles


def packed_edges(planes, layers, spot):
    tile = None
    for z in range(layers):
        here = rolled(planes[z], spot + z * SEAM + EDGE, 1)
        if tile is None:
            tile = here
        else:
            tile = jnp.where(iota(tile.shape, 1) >= spot + z * SEAM, here, tile)
    return tile


def squeezed(first, second):
    rows = first.shape[0] // 2
    row = iota((rows, first.shape[1]), 0)
    ends = (row < STEPS) | (row >= rows - STEPS)
    second_halo = second[rows:]
    moved = jnp.where(
        row < 2 * STEPS, rolled(second_halo, STEPS, 0), rolled(second_halo, -STEPS, 0)
    )
    return first[:rows], second[:rows], jnp.where(ends, first[rows:], moved)


def stretched(first, second, halo):
    rows = first.shape[0]
    row = iota(halo.shape, 0)
    moved = jnp.where(row < 2 * STEPS, rolled(halo, -STEPS, 0), rolled(halo, STEPS, 0))
    return jnp.concatenate([first, halo], axis=0), jnp.concatenate([second, moved], axis=0)


def pair_of_tiles(ref, pair, rows):
    base = (STEPS * RECORDS + 3 * pair) * rows
    return stretched(*[ref[pl.ds(base + i * rows, rows), :] for i in range(3)])


def monitor_message(
    perm_ref,
    e_ref,
    h_ref,
    m_ref,
    same_ref,
    cross_ref,
    forth_ref,
    back_ref,
    far_ref,
    edges_ref,
):
    layers, rows, columns = m_ref.shape
    rates = rates_of(perm_ref, perm_ref.shape[0], (rows, columns))
    wide = widened_planes(own_planes(e_ref, h_ref, m_ref, rates), same_ref, cross_ref)
    low = layers - DEEP
    walk = Leapfrog(lambda z: wide(low + z), layers=DEEP)
    for s in range(STEPS):
        for c, record in enumerate(walk.records(s + 1, DEEP - 1)):
            place = pl.ds((s * RECORDS + c) * rows, rows)
            for ref in (forth_ref, back_ref, far_ref):
                ref[place, :] = record[:rows]
    planes = [wide(z) for z in range(low)] + [walk.first(z) for z in range(DEEP)]
    span = DEEP * SEAM
    per_tile = columns // span
    tops, lasts, firsts = ([None, None] for _ in range(3))
    for kind in range(KINDS):
        edges = packed_edges([planes[z][kind] for z in range(layers)], layers, 0)
        edges_ref[kind] = edges
        lane = iota(edges.shape, 1)
        tile, spot = divmod(kind, per_tile)
        here = rolled(edges, spot * span - low * SEAM, 1)
        tops[tile] = jnp.where(lane >= spot * span, here, tops[tile]) if spot else here
        tile, spot = divmod(kind, OUTER)
        for tiles, shift in ((lasts, STEPS), (firsts, EDGE)):
            here = rolled(edges, spot * STEPS - shift, 1)
            tiles[tile] = jnp.where(lane % SEAM >= spot * STEPS, here, tiles[tile]) if spot else here
    base = STEPS * RECORDS * rows
    for i, part in enumerate(squeezed(*tops)):
        for ref in (forth_ref, back_ref, far_ref):
            ref[pl.ds(base + i * rows, rows), :] = part
    for ref, tiles in ((forth_ref, lasts), (back_ref, firsts)):
        for i, part in enumerate(squeezed(*tiles)):
            ref[pl.ds(base + (3 + i) * rows, rows), :] = part


def waves_of(coef_ref, wave):
    base = wave * (STEPS * 4)
    return lambda s, half, part: coef_ref[base + (s * 2 + half) * 2 + part]


def exact_dot(left, right, contracted):
    return lax.dot_general(
        left,
        right,
        (contracted, ((), ())),
        precision=lax.Precision.HIGHEST,
        preferred_element_type=jnp.float32,
    )


def split_dot(values, tables, total, contracted=((1,), (0,))):
    coarse = values.astype(jnp.bfloat16)
    fine = (values - coarse.astype(jnp.float32)).astype(jnp.bfloat16)
    for left, right in ((coarse, tables[0]), (fine, tables[0]), (coarse, tables[1])):
        product = lax.dot_general(
            left, right, (contracted, ((), ())), preferred_element_type=jnp.float32
        )
        total = product if total is None else total + product
    return total


def packed_orders(values, planes, kept):
    rows = values.shape[0] // planes
    parts = [values[plane * rows : (plane + 1) * rows] for plane in range(planes)]
    targets = per_tile = OY // kept
    if planes % per_tile == 0 and not targets & (targets - 1):
        groups = [parts[i : i + per_tile] for i in range(0, planes, per_tile)]
        return list(zip(*[blocks_transposed(group) for group in groups]))
    lane = iota((rows, OY), 1)
    packed = []
    for target in range(targets):
        tiles = []
        for first in range(0, planes, per_tile):
            tile = None
            for plane in range(first, min(planes, first + per_tile)):
                spot = (plane - first) * kept
                here = rolled(parts[plane], spot - target * kept, 1)
                tile = here if tile is None else jnp.where(lane >= spot, here, tile)
            tiles.append(tile)
        packed.append(tiles)
    return packed


def fetch(after_this, slab_any, monitor_any, slab_ref, monitor_ref, ready):
    copies = [
        pltpu.make_async_copy(slab_any, slab_ref, ready.at[0]),
        pltpu.make_async_copy(monitor_any, monitor_ref, ready.at[1]),
    ]
    for copy in copies:
        copy.start()
    for copy in copies:
        copy.wait()


def y_monitor(wave_ref, coef_ref, table_ref, own_ref, *refs):
    *spectra, out_ref, weights_ref = refs
    half = len(spectra) // 2
    spectra = spectra[1 : half + 1] + spectra[:1] + spectra[half + 1 :]
    blocks = len(spectra) + 1
    waves, _, records, rows, columns = spectra[0].shape
    me = lax.axis_index("gy")
    spectra = [own_ref.at[pl.ds(me * waves, waves)]] + spectra
    total = None
    for block in range(blocks):
        owner = lax.rem(me + block, blocks)
        place = pl.ds(pl.multiple_of(owner * columns, columns), columns)
        parts = []
        for part in range(2):
            for w in range(waves):
                parts += [spectra[block][w, part, c] for c in range(records)]
        tables = [table_ref[i, place, :] for i in range(2)]
        total = split_dot(jnp.concatenate(parts, axis=0), tables, total)
    half = waves * records * rows
    real = total[:half, :OY] + total[half:, OY:]
    imag = total[half:, :OY] - total[:half, OY:]
    targets = out_ref.shape[0]
    for part, values in enumerate((real, imag)):
        packed = packed_orders(values, waves * records, OY // targets)
        for target in range(targets):
            for i, tile in enumerate(packed[target]):
                out_ref[target, pl.ds((i * 2 + part) * rows, rows), :] = tile
    kept = OY // targets
    lane = iota((rows, OY), 1)
    per_wave = RECORDS * kept
    per_tile = OY // per_wave
    for tile in range(weights_ref.shape[0] // (2 * STEPS)):
        some = range(tile * per_tile, min(waves, (tile + 1) * per_tile))
        coefs = [waves_of(coef_ref, wave_ref[me * waves + w]) for w in some]
        for s in range(STEPS):
            for part in range(2):
                weight = None
                for i, coef in enumerate(coefs):
                    for half in range(2):
                        value = jnp.full((rows, OY), coef(s, half, part), jnp.float32)
                        spot = i * per_wave + half * (per_wave // 2)
                        weight = value if weight is None else jnp.where(lane >= spot, value, weight)
                weights_ref[(tile * STEPS + s) * 2 + part] = weight


def y_records(waves, table_ref, monitor_ref, weights_ref, *refs):
    *messages, out_any, out_ref, done = refs
    messages = messages[::-1]
    blocks = len(messages)
    columns = messages[0].shape[1]
    targets, height, _ = out_ref.shape
    kept = OY // targets
    out_tiles = -(-waves * RECORDS * kept // OY)
    rows = height // (2 * out_tiles)
    me = lax.axis_index("gy")
    span = DEEP * SEAM
    per_tile = columns // span
    base = STEPS * RECORDS * rows
    column = iota((2 * rows, columns), 1) % SEAM
    edges = [pair_of_tiles(message, 0, rows) for message in messages]

    total = None
    for block in range(blocks):
        owner = lax.rem(me + block, blocks)
        place = pl.ds(pl.multiple_of(blocks * span + owner * columns, span), columns)
        values = messages[block][pl.ds(0, base), :]
        total = split_dot(values, [table_ref[part, place, :] for part in range(2)], total)
    for tile in range(-(-blocks // per_tile)):
        seams = range(tile * per_tile, min(blocks, (tile + 1) * per_tile))
        kinds = []
        for part in range(2):
            mixed = []
            for seam in list(seams) + [seams[0]] * (per_tile - len(seams)):
                here, after = edges[seam][part], edges[(seam + 1) % blocks][part]
                mixed.append(jnp.where(column < EDGE, here, after))
            kinds += blocks_transposed(mixed)
        walk = seam_leapfrog(kinds[:KINDS], DEEP)
        record = []
        for s in range(STEPS):
            record += [value[:rows] for value in walk.records(s + 1, 0)]
        values = jnp.concatenate(record, axis=0)[:, : len(seams) * span]
        owners = [lax.rem(me + seam, blocks) for seam in seams]
        places = [pl.ds(pl.multiple_of(owner * span, span), span) for owner in owners]
        tables = [
            jnp.concatenate([table_ref[part, place, :] for place in places], axis=0)
            for part in range(2)
        ]
        total = split_dot(values, tables, total)
    lane = iota((rows, OY), 1)
    per_wave = RECORDS * kept
    per_tile = OY // per_wave
    packed_parts = [
        packed_orders(total[:, part * OY : (part + 1) * OY], STEPS * RECORDS, kept)
        for part in range(2)
    ]
    copies = []
    for target in range(targets):
        spot = order_of(targets).index(target)
        sides = []
        for part in range(2):
            (packed,) = packed_parts[part][target]
            steps = []
            for s in range(STEPS):
                spread = None
                for i in range(min(per_tile, waves)):
                    here = rolled(packed, i * per_wave - s * per_wave, 1)
                    spread = here if i == 0 else jnp.where(lane >= i * per_wave, here, spread)
                steps.append(spread)
            sides.append(steps)
        for tile in range(out_tiles):
            for part in range(2):
                place = pl.ds((tile * 2 + part) * rows, rows)
                value = monitor_ref[target, place, :]
                for s in range(STEPS):
                    first = (tile * STEPS + s) * 2
                    real, imag = weights_ref[first], weights_ref[first + 1]
                    if part == 0:
                        value = value + (real * sides[0][s] - imag * sides[1][s])
                    else:
                        value = value + (imag * sides[0][s] + real * sides[1][s])
                out_ref[spot, place, :] = value
        copies.append(
            pltpu.make_async_copy(out_ref.at[spot], out_any.at[spot], done.at[spot])
        )
        copies[-1].start()
    for copy in copies:
        copy.wait()


def x_orders(kept, values_ref, table_ref, out_any, out_ref, done):
    sources, height, lanes = values_ref.shape
    waves, _, records, _, _ = out_ref.shape
    depth = table_ref.shape[1]
    rows = depth // sources
    per_tile = lanes // kept
    copies = []
    for tile in range(height // rows):
        values = jnp.concatenate(
            [values_ref[source, pl.ds(tile * rows, rows), :] for source in range(sources)], axis=0
        )
        result = split_dot(values, [table_ref[0], table_ref[1]], None, ((0,), (0,)))
        for place in range(per_tile):
            wave, record = divmod(tile * per_tile + place, records)
            if wave < waves:
                here = result[place * kept : (place + 1) * kept]
                out_ref[wave, 0, record] = here[:, :OX]
                out_ref[wave, 1, record] = here[:, OX:]
                if record == records - 1:
                    copies.append(
                        pltpu.make_async_copy(out_ref.at[wave], out_any.at[wave], done.at[wave])
                    )
                    copies[-1].start()
    for copy in copies:
        copy.wait()


def local_updates(
    perm_ref,
    wave_ref,
    coef_ref,
    e_ref,
    h_ref,
    m_ref,
    same_ref,
    cross_ref,
    edges_ref,
    message_after_ref,
    message_before_ref,
    slab_ref,
    monitor_ref,
    e_any,
    h_any,
    slab_out_any,
    monitor_out_any,
    e_out,
    h_out,
    slab_out,
    monitor_out,
    done,
):
    layers, rows, columns = m_ref.shape
    rates = rates_of(perm_ref, perm_ref.shape[0], (rows, columns))
    wide = widened_planes(own_planes(e_ref, h_ref, m_ref, rates), same_ref, cross_ref)
    walk = Leapfrog(wide, layers=layers)
    left = iota((2 * rows, layers * SEAM), 1) % SEAM < EDGE
    last = pair_of_tiles(message_before_ref, 1, rows)
    first = pair_of_tiles(message_after_ref, 1, rows)
    before, after = [], []
    for kind in range(KINDS):
        mine = edges_ref[kind]
        tile, spot = divmod(kind, OUTER)
        from_before = rolled(last[tile], STEPS - spot * STEPS, 1)
        from_after = rolled(first[tile], EDGE - spot * STEPS, 1)
        before.append(jnp.where(left, from_before, mine))
        after.append(jnp.where(left, mine, from_after))
    before = seam_leapfrog(before, layers)
    after = seam_leapfrog(after, layers)
    column = iota((rows, columns), 1)
    inner = (column >= STEPS) & (column < columns - STEPS)
    joined = {}

    def mended(s, z, kind):
        if (s, kind) not in joined:
            ends = [(side.e(s, 0) + side.h(s, 0))[kind][:rows] for side in (after, before)]
            joined[s, kind] = jnp.where(left[:rows], ends[0], ends[1])
        value = (walk.e(s, z) + walk.h(s, z))[kind][:rows]
        return jnp.where(inner, value, rolled(joined[s, kind], -(z * SEAM + EDGE), 1))

    middle = layers // 2
    slab_records = [[None] * 2 for _ in range(STEPS)]
    records = [[None] * RECORDS for _ in range(STEPS)]
    for z in range(layers):
        for kind in range(6):
            value = mended(STEPS, z, kind)
            if kind < 3:
                e_out[kind, z] = value
            else:
                h_out[kind - 3, z] = value
        for s in range(STEPS):
            if z == middle:
                slab_records[s] = [mended(s + 1, z, kind) for kind in (0, 1)]
            if z == layers - 1:
                records[s] = [mended(s + 1, z, kind) for kind in (0, 1, 3, 4)]
    sent = [
        pltpu.make_async_copy(e_out, e_any, done.at[0]),
        pltpu.make_async_copy(h_out, h_any, done.at[1]),
    ]
    for copy in sent:
        copy.start()
    frequencies = slab_ref.shape[1] // 2

    def one_frequency(f, carry):
        coef = waves_of(coef_ref, f)
        for c in range(2):
            for part in range(2):
                value = slab_ref[c, part * frequencies + f]
                for s in range(STEPS):
                    value = value + coef(s, 0, part) * slab_records[s][c]
                slab_out[c, part * frequencies + f] = value
        return carry

    lax.fori_loop(0, frequencies, one_frequency, 0, unroll=4)
    sent.append(pltpu.make_async_copy(slab_out, slab_out_any, done.at[2]))
    sent[-1].start()
    for w in range(monitor_ref.shape[0]):
        coef = waves_of(coef_ref, wave_ref[w])
        for part in range(2):
            for c in range(RECORDS):
                value = monitor_ref[w, part, c]
                for s in range(STEPS):
                    value = value + coef(s, c // 2, part) * records[s][c]
                monitor_out[w, part, c] = value
    sent.append(pltpu.make_async_copy(monitor_out, monitor_out_any, done.at[3]))
    sent[-1].start()
    for copy in sent:
        copy.wait()


def wave_coefficients(freq_count):
    omegas = OMEGA_LOW + (OMEGA_HIGH - OMEGA_LOW) * np.arange(freq_count) / (freq_count - 1)
    times = TIME_STEP * (np.arange(1, STEPS + 1)[:, None] - np.array([0.0, 0.5])[None, :])
    angles = omegas[:, None, None] * times[None]
    table = np.stack([TIME_STEP * np.cos(angles), -TIME_STEP * np.sin(angles)], axis=-1)
    return table.reshape(-1).astype(np.float32)


def angles_of(length, kept):
    wanted = (np.arange(kept) - kept // 2) % length
    return 2.0 * math.pi / length * (np.arange(length)[:, None] * wanted[None, :] % length)


def y_table(length):
    angles = angles_of(length, OY)
    return split_table(np.concatenate([np.cos(angles), np.sin(angles)], axis=1))


def split_table(table):
    table = table.astype(np.float32)
    coarse = table.astype(ml_dtypes.bfloat16)
    fine = (table - coarse.astype(np.float32)).astype(ml_dtypes.bfloat16)
    return jnp.asarray(np.stack([coarse, fine]))


def record_table(length, blocks):
    angles = angles_of(length, OY)
    table = np.concatenate([np.cos(angles), -np.sin(angles)], axis=1)
    columns = length // blocks
    seams = np.zeros((blocks, DEEP, SEAM, 2 * OY))
    for block in range(blocks):
        for column in range(-STEPS, STEPS):
            row = ((block + 1) * columns + column) % length
            seams[block, DEEP - 1, EDGE + column] = table[row]
    inner = table.copy()
    place = np.arange(length) % columns
    inner[(place < STEPS) | (place >= columns - STEPS)] = 0.0
    return split_table(np.concatenate([seams.reshape(-1, 2 * OY), inner]))


def order_of(blocks):
    return list(reversed(range(blocks)))


def x_table(length, blocks, scaling):
    angles = angles_of(length, OX).reshape(blocks, length // blocks, OX)[order_of(blocks)]
    real = np.concatenate([np.cos(angles), -np.sin(angles)], axis=2)
    imag = np.concatenate([np.sin(angles), np.cos(angles)], axis=2)
    table = np.stack([real, imag], axis=1) * scaling
    return split_table(table.reshape(2 * length, 2 * OX))


def call(kernel, in_specs, shapes, *operands, name, flops=0, moved=0, **more):
    kind = jax.ShapeDtypeStruct
    out = [kind(shape, jnp.float32) for shape in shapes]
    return pl.pallas_call(
        kernel,
        out_shape=out,
        in_specs=in_specs,
        out_specs=more.pop("out_specs", [VMEM] * len(out)),
        compiler_params=PARAMS,
        cost_estimate=pl.CostEstimate(flops=flops, bytes_accessed=moved, transcendentals=0),
        name=name,
        **more,
    )(*operands)


def per_device(
    electric, magnetic, material, permittivity, slab_spectra, monitor_spectra, wave_index
):
    layers, rows, columns = material.shape
    x_blocks, y_blocks = lax.axis_size("gx"), lax.axis_size("gy")
    waves = monitor_spectra.shape[0]
    group_waves = waves // y_blocks
    fields = (electric, magnetic, material)
    groups = layers * STEPS // rows

    faces = (KINDS, groups, rows, columns)
    block = (group_waves,) + monitor_spectra.shape[1:]
    early = [y_blocks // 2]
    late = [distance for distance in range(1, y_blocks) if distance not in early]
    packed, cross, *blocks = call(
        functools.partial(pack_faces, early),
        [HBM] * 5,
        [faces, faces] + [block] * len(early),
        *[in_hbm(array) for array in (permittivity, *fields, monitor_spectra)],
        name="pack_faces",
        flops=10**5,
        moved=10**6,
        scratch_shapes=[
            pltpu.SMEM(permittivity.shape, jnp.float32),
            pltpu.VMEM(electric.shape, jnp.float32),
            pltpu.VMEM(magnetic.shape, jnp.float32),
            pltpu.VMEM(material.shape, jnp.int32),
            pltpu.SemaphoreType.DMA((4,)),
            pltpu.SemaphoreType.DMA((len(early),)),
        ],
    )
    line = range(x_blocks)
    same = lax.ppermute(packed, "gx", [(i, i ^ 1) for i in line])
    cross = lax.ppermute(cross, "gx", [(i, (i + (1 if i % 2 else -1)) % x_blocks) for i in line])
    spectra = {
        distance: passed_along(block, "gy", -distance) for distance, block in zip(early, blocks)
    }
    blocks = call(
        functools.partial(other_blocks, late),
        [ANY, HBM],
        [block] * len(late),
        packed,
        in_hbm(monitor_spectra),
        name="other_blocks",
        flops=1,
        moved=1,
        scratch_shapes=[pltpu.SemaphoreType.DMA((len(late),))],
    )
    for distance, block in zip(late, blocks):
        spectra[distance] = passed_along(block, "gy", -distance)

    far_height = (STEPS * RECORDS + 3) * rows
    near_height = far_height + 3 * rows
    forth, back, far, edges = call(
        monitor_message,
        [SMEM] + [VMEM] * 5,
        [
            (near_height, columns),
            (near_height, columns),
            (far_height, columns),
            (KINDS, 2 * rows, layers * SEAM),
        ],
        permittivity,
        *fields,
        same,
        cross,
        name="monitor_message",
        flops=1,
        moved=1,
    )
    message_before = passed_along(forth, "gy", 1)
    message_after = passed_along(back, "gy", -1)
    messages = [far, message_after]
    for distance in range(2, y_blocks - 1):
        messages.append(passed_along(far, "gy", -distance))
    messages = (messages + [message_before])[:y_blocks]

    coefs = jnp.asarray(wave_coefficients(slab_spectra.shape[1] // 2))
    length_x, length_y = rows * x_blocks, columns * y_blocks
    kept = OY // x_blocks
    out_tiles = -(-group_waves * RECORDS * kept // OY)
    sums_y = y_table(length_y)
    slab_here, monitor_here = call(
        fetch,
        [ANY] + [HBM] * 2,
        [slab_spectra.shape, monitor_spectra.shape],
        far,
        in_hbm(slab_spectra),
        in_hbm(monitor_spectra),
        name="fetch",
        flops=1,
        moved=3 * 10**6,
        scratch_shapes=[pltpu.SemaphoreType.DMA((2,))],
    )
    monitor_y, weights = call(
        y_monitor,
        [SMEM] * 2 + [VMEM] * (1 + y_blocks),
        [(x_blocks, out_tiles * 2 * rows, OY), (out_tiles * STEPS * 2, rows, OY)],
        wave_index,
        coefs,
        sums_y,
        monitor_here,
        *[spectra[distance] for distance in [y_blocks // 2] + list(range(1, y_blocks // 2)) + list(range(y_blocks // 2 + 1, y_blocks))],
        name="y_monitor",
        flops=10**8,
        moved=2 * 10**6,
    )
    (spectrum_y,) = call(
        functools.partial(y_records, group_waves),
        [VMEM] * (3 + y_blocks),
        [monitor_y.shape],
        record_table(length_y, y_blocks),
        monitor_y,
        weights,
        *messages[::-1],
        out_specs=[HBM],
        scratch_shapes=[
            pltpu.VMEM(monitor_y.shape, jnp.float32),
            pltpu.SemaphoreType.DMA((x_blocks,)),
        ],
        name="y_records",
        flops=10**8,
        moved=2 * 10**6,
    )
    members = [
        [x * y_blocks + y for x in order_of(x_blocks)] for y in range(y_blocks)
    ]
    swapped = lax.all_to_all(
        spectrum_y, ("gx", "gy"), split_axis=0, concat_axis=0, axis_index_groups=members, tiled=True
    )

    electric_next, magnetic_next, slab_next, monitor_next = call(
        local_updates,
        [SMEM] * 3 + [VMEM] * 10,
        [electric.shape, magnetic.shape, slab_spectra.shape, monitor_spectra.shape],
        permittivity,
        wave_index,
        coefs,
        *fields,
        same,
        cross,
        edges,
        message_after,
        message_before,
        slab_here,
        monitor_here,
        name="local_updates",
        scratch_shapes=[
            pltpu.VMEM(electric.shape, jnp.float32),
            pltpu.VMEM(magnetic.shape, jnp.float32),
            pltpu.VMEM(slab_spectra.shape, jnp.float32),
            pltpu.VMEM(monitor_spectra.shape, jnp.float32),
            pltpu.SemaphoreType.DMA((4,)),
        ],
        out_specs=[HBM] * 4,
        flops=10**7,
        moved=6 * 10**6,
    )

    scaling = 1.0 / math.sqrt(length_x * length_y)
    (orders,) = call(
        functools.partial(x_orders, kept),
        [VMEM] * 2,
        [(group_waves, 2, RECORDS, kept, OX)],
        swapped,
        x_table(length_x, x_blocks, scaling),
        out_specs=[HBM],
        scratch_shapes=[
            pltpu.VMEM((group_waves, 2, RECORDS, kept, OX), jnp.float32),
            pltpu.SemaphoreType.DMA((group_waves,)),
        ],
        name="x_orders",
        flops=10**7,
        moved=5 * 10**5,
    )
    return (electric_next, magnetic_next, slab_next, monitor_next, orders)


def solution(mesh):
    in_specs = (
        P(None, None, "gx", "gy"),
        P(None, None, "gx", "gy"),
        P(None, "gx", "gy"),
        P(),
        P(None, None, "gx", "gy"),
        P(None, None, None, "gx", "gy"),
        P(),
    )
    out_specs = (
        P(None, None, "gx", "gy"),
        P(None, None, "gx", "gy"),
        P(None, None, "gx", "gy"),
        P(None, None, None, "gx", "gy"),
        P("gy", None, None, "gx", None),
    )
    return jax.shard_map(
        per_device, mesh=mesh, in_specs=in_specs, out_specs=out_specs, check_vma=False
    )
```
